128 devices in a mesh: dp: 32 (over x, z, core), tensor: 4 (over y).
Axes of the slice: x: 4, y: 4, z: 4, core: 2. Of those that a mesh axis runs over, the one named last changes fastest.
Arguments:
- query_states: bfloat16 [128, 128, 4096], P('dp'), may hold values from -6 to 6
- passage_states: bfloat16 [128, 256, 4096], P('dp'), may hold values from -6 to 6
- norm_gain: float32 [4096], replicated, may hold values from 0.1 to 1.9
- w_query: bfloat16 [4096, 2048], P('dp', 'tensor'), may hold values from -0.09375 to 0.09375
- w_key: bfloat16 [4096, 512], P('dp', 'tensor'), may hold values from -0.09375 to 0.09375
- w_value: bfloat16 [4096, 512], P('dp', 'tensor'), may hold values from -0.09375 to 0.09375
- w_out: bfloat16 [2048, 4096], P('tensor'), may hold values from -0.125 to 0.125
- neg_owner: int32 [128, 7], replicated, may hold values from 0 to 31, as said below
- neg_slot: int32 [128, 7], replicated, may hold values from 0 to 3
Outputs:
- loss: float32 [], replicated
- grad_query: float32 [4096, 2048], P('dp', 'tensor')
- grad_key: float32 [4096, 512], P('dp', 'tensor')
- grad_value: float32 [4096, 512], P('dp', 'tensor')
The draws below stay inside these ranges and needn't reach their ends.
Inputs may be any that keep to these rules, and one draw needn't show every extreme that they name: neg_owner of query i is never i // 4, the rank that owns query i.
All inputs are finite; a program needn't handle non-finite values.
Results may differ from the reference program's by a relative error of at most 0.027.
Values may be sent and summed in bfloat16 or wider, within the bound.
A program may use at most 128 MiB of HBM per device.

```python
import math
import jax
import jax.numpy as jnp
from jax import lax

D = 4096
HEADS = 16
KV_HEADS = 4
HEAD_DIM = 128
LQ = 128
LP = 256
NEG = 7
QRY_DEV = 4
QUERIES = 128
N_DP = 32


def draw_neg_owner(key, part):
    key = jax.random.fold_in(key, 11)
    owner_rank = jnp.arange(QUERIES, dtype=jnp.int32)[:, None] // QRY_DEV
    offsets = jax.random.randint(key, (QUERIES, NEG), 1, N_DP, dtype=jnp.int32)
    return (owner_rank + offsets) % N_DP


def touch_ends(drawn, own_key, low, high):
    longest = drawn.shape.index(max(drawn.shape))
    spots = []
    for shift in (0, 1):
        where = [jax.random.randint(jax.random.fold_in(own_key, axis), (), 0, length) for axis, length in enumerate(drawn.shape)]
        where[longest] = (where[longest] + shift) % drawn.shape[longest]
        spots.append(tuple(where))
    return drawn.at[spots[0]].set(low).at[spots[1]].set(high)


def level_of(key, extent, shards, low, high):
    def one(axis_at, shards_of):
        heights = jax.random.uniform(jax.random.fold_in(jax.random.fold_in(key, 6), axis_at), (shards_of,), jnp.float32, low / len(shards), high / len(shards))
        return jnp.repeat(jnp.exp(heights), extent[axis_at] // shards_of).reshape((-1,) + (1,) * (len(extent) - axis_at - 1))

    factor_of = one(*shards[0])
    for cut in shards[1:]:
        factor_of = factor_of * one(*cut)
    return factor_of


def gaussian(rng, dims, spread, most, split=(), held_as=jnp.bfloat16):
    loudness = level_of(rng, dims, split, -0.22, 0.18) if split else 1.0
    entries = jax.random.normal(rng, dims, jnp.float32) * spread * loudness
    return jnp.minimum(jnp.maximum(entries, -most), most).astype(held_as)


def setup_inputs(seed: int = 0) -> dict:
    splits = jax.random.split(jax.random.key(seed), 10)
    return {
        "query_states": gaussian(splits[0], (QUERIES, LQ, D), 1.0, 6.0, ((0, 32),)),
        "passage_states": gaussian(splits[1], (QUERIES, LP, D), 1.0, 6.0, ((0, 32),)),
        "norm_gain": jnp.clip(1.0 + 0.18 * jax.random.normal(splits[2], (D,), jnp.float32), 0.1, 1.9),
        "w_query": gaussian(splits[3], (D, HEADS * HEAD_DIM), D ** -0.5, 0.09375, ((0, 32), (1, 4))),
        "w_key": gaussian(splits[4], (D, KV_HEADS * HEAD_DIM), D ** -0.5, 0.09375, ((0, 32), (1, 4))),
        "w_value": gaussian(splits[5], (D, KV_HEADS * HEAD_DIM), D ** -0.5, 0.09375, ((0, 32), (1, 4))),
        "w_out": gaussian(splits[6], (HEADS * HEAD_DIM, D), (HEADS * HEAD_DIM) ** -0.5, 0.125, ((0, 4),)),
        "neg_owner": draw_neg_owner(jax.random.fold_in(splits[9], 71), 0),
        "neg_slot": touch_ends(jax.random.randint(splits[8], (QUERIES, NEG), 0, QRY_DEV), jax.random.fold_in(splits[8], 1), 0, QRY_DEV - 1).astype(jnp.int32),
    }


eps_norm = 1e-06
eps_unit = 1e-06
sharpness_divisor = 0.05

def rms_normed(states, norm_gain):
    values = states.astype(jnp.float32)
    scaling = lax.rsqrt(lax.optimization_barrier(jnp.mean(values * values, axis=-1, keepdims=True)) + eps_norm)
    return (values * scaling * norm_gain).astype(jnp.bfloat16)

def attention_table(query_rows, key_rows, groups, head_width):
    seq_count = key_rows.shape[0]
    length = key_rows.shape[1]
    kv_count = key_rows.shape[2] // head_width
    query_wide = query_rows.astype(jnp.float32).reshape(seq_count, length, kv_count, groups, head_width)
    key_wide = key_rows.astype(jnp.float32).reshape(seq_count, length, kv_count, head_width)
    scores = jnp.einsum('sikge,sjke->skgij', query_wide, key_wide) / math.sqrt(head_width)
    causal_mask = lax.broadcasted_iota(jnp.int32, (length, length), 0) >= lax.broadcasted_iota(jnp.int32, (length, length), 1)
    raised_powers = jnp.where(causal_mask, jnp.exp(jnp.where(causal_mask, scores, 0.0)), 0.0)
    attend = raised_powers / lax.optimization_barrier(jnp.sum(raised_powers, axis=-1, keepdims=True))
    weights = lax.optimization_barrier(jnp.mean(attend, axis=-2))
    return (query_wide, key_wide, attend, weights)

def pooled_attention(query_rows, key_rows, value_rows, groups, head_width):
    query_wide, key_wide, attend, weights = attention_table(query_rows, key_rows, groups, head_width)
    value_wide = value_rows.astype(jnp.float32).reshape(key_wide.shape)
    pooled = jnp.einsum('skgj,sjke->skge', weights, value_wide)
    return pooled.reshape(pooled.shape[0], -1).astype(jnp.bfloat16)

def attention_grads(query_rows, key_rows, value_rows, upstream, groups, head_width):
    query_wide, key_wide, attend, weights = attention_table(query_rows, key_rows, groups, head_width)
    value_wide = value_rows.astype(jnp.float32).reshape(key_wide.shape)
    length = key_wide.shape[1]
    upstream_wide = upstream.reshape(key_wide.shape[0], key_wide.shape[2], groups, head_width)
    coefficient = jnp.einsum('sjke,skge->skgj', value_wide, upstream_wide) / length
    inner_sum = lax.optimization_barrier(jnp.sum(attend * coefficient[:, :, :, None, :], axis=-1, keepdims=True))
    dscores = attend * (coefficient[:, :, :, None, :] - inner_sum) / math.sqrt(head_width)
    query_grad = jnp.einsum('skgij,sjke->sikge', dscores, key_wide)
    key_grad = jnp.einsum('skgij,sikge->sjke', dscores, query_wide)
    value_grad = jnp.einsum('skgj,skge->sjke', weights, upstream_wide)
    shape_rows = (key_wide.shape[0] * length, -1)
    return tuple((gradient.reshape(shape_rows).astype(jnp.bfloat16) for gradient in (query_grad, key_grad, value_grad)))

def normalize_rows(raw):
    inverse = lax.rsqrt(lax.optimization_barrier(jnp.sum(raw * raw, axis=-1, keepdims=True)) + eps_unit)
    return (raw * inverse, inverse)

def normalize_back(embedded, inverse, gradient):
    return inverse * (gradient - embedded * lax.optimization_barrier(jnp.sum(embedded * gradient, axis=-1, keepdims=True)))

def contrast(question_embeds, document_embeds, passage_ids, row_start):
    row_count = question_embeds.shape[0]
    passage_count = document_embeds.shape[0]
    columns = lax.broadcasted_iota(jnp.int32, (row_count, passage_count), 1)
    positive = lax.broadcasted_iota(jnp.int32, (row_count, passage_count), 0) + row_start
    paired_entries = (columns == positive).astype(jnp.float32)
    listed = jnp.arange(passage_count, dtype=jnp.int32)
    counts = lax.optimization_barrier(jnp.sum((passage_ids[:, :, None] == listed[None, None, :]).astype(jnp.float32), axis=1))
    cosine_matrix = jnp.dot(question_embeds, document_embeds.T, precision=lax.Precision.HIGHEST) / sharpness_divisor
    raised_powers = jnp.exp(cosine_matrix) * (1.0 + counts)
    partition_sums = lax.optimization_barrier(jnp.sum(raised_powers, axis=1, keepdims=True))
    total_sum = jnp.sum(jnp.log(partition_sums[:, 0]) - lax.optimization_barrier(jnp.sum(cosine_matrix * paired_entries, axis=1)))
    score_derivative = (raised_powers / partition_sums - paired_entries) / sharpness_divisor
    d_query = jnp.dot(score_derivative, document_embeds, precision=lax.Precision.HIGHEST)
    d_passage = jnp.dot(score_derivative.T, question_embeds, precision=lax.Precision.HIGHEST)
    return (total_sum, d_query, d_passage)

def project(normed, weight):
    return jnp.dot(normed, weight, preferred_element_type=jnp.float32).astype(jnp.bfloat16)

def forward_set(states, norm_gain, w_query, w_key, w_value, w_out):
    seq_count, length, model_width = states.shape
    groups = HEADS // KV_HEADS
    normed = rms_normed(states, norm_gain).reshape(seq_count * length, model_width)
    query_rows = project(normed, w_query).reshape(seq_count, length, -1)
    key_rows = project(normed, w_key).reshape(seq_count, length, -1)
    value_rows = project(normed, w_value).reshape(seq_count, length, -1)

    def single(items):
        return pooled_attention(items[0][None], items[1][None], items[2][None], groups, HEAD_DIM)[0]
    pooled = lax.map(single, (query_rows, key_rows, value_rows))
    raw = lax.optimization_barrier(jnp.mean(states, axis=1, dtype=jnp.float32)) + jnp.dot(pooled, w_out, preferred_element_type=jnp.float32)
    return (normed, query_rows, key_rows, value_rows, raw)

def backward_set(normed, query_rows, key_rows, value_rows, raw_grad, w_out):
    groups = HEADS // KV_HEADS
    upstream = lax.dot_general(raw_grad.astype(jnp.bfloat16), w_out, (((1,), (1,)), ((), ())), preferred_element_type=jnp.float32)

    def single(items):
        return attention_grads(items[0][None], items[1][None], items[2][None], items[3][None], groups, HEAD_DIM)
    grads = lax.map(single, (query_rows, key_rows, value_rows, upstream))
    return tuple((lax.dot_general(normed, gradient.reshape(normed.shape[0], -1), (((0,), (0,)), ((), ())), preferred_element_type=jnp.float32) for gradient in grads))

def reference(query_states, passage_states, norm_gain, w_query, w_key, w_value, w_out, neg_owner, neg_slot):
    query_set = forward_set(query_states, norm_gain, w_query, w_key, w_value, w_out)
    passage_set = forward_set(passage_states, norm_gain, w_query, w_key, w_value, w_out)
    question_embeds, query_inverse = normalize_rows(query_set[4])
    document_embeds, passage_inverse = normalize_rows(passage_set[4])
    passage_ids = neg_owner * QRY_DEV + neg_slot
    total_sum, d_query, d_passage = contrast(question_embeds, document_embeds, passage_ids, 0)
    loss = total_sum / QUERIES
    query_terms = backward_set(query_set[0], query_set[1], query_set[2], query_set[3], normalize_back(question_embeds, query_inverse, d_query), w_out)
    passage_terms = backward_set(passage_set[0], passage_set[1], passage_set[2], passage_set[3], normalize_back(document_embeds, passage_inverse, d_passage), w_out)
    return (loss, query_terms[0] + passage_terms[0], query_terms[1] + passage_terms[1], query_terms[2] + passage_terms[2])
```

```python
import functools
import math

import jax
import jax.numpy as jnp
from jax import lax
from jax.experimental import pallas as pl
from jax.experimental.pallas import tpu as pltpu
from jax.sharding import PartitionSpec as P

HEAD_DIM = 128
eps_norm = 1e-06
eps_unit = 1e-06
sharpness_divisor = 0.05
MESH = pl.DeviceIdType.MESH
f32, bf16 = jnp.float32, jnp.bfloat16
XS, ZS = 4, 4


def place():
    p = lax.axis_index("dp")
    return p // (2 * ZS), (p // 2) % ZS, p % 2


def slot_of(a, b, core=None, flip=False):
    x, z, c = place()
    c = 1 - c if flip else c
    return ((x + a) % XS * ZS + (z + b) % ZS) * 2 + c


def chip_of(a, b):
    x, z, _ = place()
    return (x + a) % XS * ZS + (z + b) % ZS


def dev(a, b, flip=False):
    return {"dp": slot_of(a, b, flip=flip)}


class Tree:
    def __init__(self, buf, rows, send_sem, recv_sem):
        self.buf, self.rows, self.send_sem, self.recv_sem = buf, rows, send_sem, recv_sem
        self.sends, self.pieces, self.waited = [], {}, set()

    def view(self, a, b, lo, n):
        return self.buf.at[slot_of(a, b), pl.ds(lo * self.rows, n * self.rows)]

    def copy(self, i):
        a, b, lo, n, dx, dz = self.sends[i]
        view = self.view(a, b, lo, n)
        return pltpu.make_async_remote_copy(
            src_ref=view, dst_ref=view, send_sem=self.send_sem.at[i], recv_sem=self.recv_sem.at[i],
            device_id=dev(dx, dz), device_id_type=MESH)

    def send(self, a, b, lo, n, dx, dz):
        i = len(self.sends)
        self.sends.append((a, b, lo, n, dx, dz))
        self.pieces[((a - dx) % 4, (b - dz) % 4, lo, n)] = i
        self.copy(i).start()

    def wait(self, a, b, lo, n):
        i = self.pieces[(a % 4, b % 4, lo, n)]
        view = self.view(a, b, lo, n)
        pltpu.make_async_remote_copy(
            src_ref=view, dst_ref=view, send_sem=self.send_sem.at[i], recv_sem=self.recv_sem.at[i],
            device_id=dev(1, 0), device_id_type=MESH).wait_recv()
        self.waited.add(i)

    def finish(self):
        assert self.waited == set(range(len(self.sends)))
        for i in range(len(self.sends)):
            self.copy(i).wait_send()


def up(d):
    return 0 if d > 0 else 1


def gather_stages(tree, sibling):
    def first():
        for d in (1, -1):
            tree.send(0, 0, 0, 2, d, 0)
            tree.send(0, 0, 2, 2, 0, d)
        for d in (1, -1):
            tree.send(0, 0, 2, 2, d, 0)
            tree.send(0, 0, 0, 2, 0, d)
        sibling(0, 0)

    def second():
        for s in (1, -1):
            tree.wait(s, 0, 0, 2)
            tree.send(s, 0, up(-s), 1, -s, 0)
            tree.wait(0, s, 2, 2)
            tree.send(0, s, 2 + up(-s), 1, 0, -s)
        for s in (1, -1):
            for d in (1, -1):
                tree.send(s, 0, 0, 2, 0, d)
                tree.send(0, s, 2, 2, d, 0)

    def third():
        for s in (1, -1):
            tree.wait(s, 0, 2, 2)
            tree.send(s, 0, 2 + up(-s), 1, -s, 0)
            tree.wait(0, s, 0, 2)
            tree.send(0, s, up(-s), 1, 0, -s)
        for s in (1, -1):
            sibling(s, 0)
            sibling(0, s)

    def fourth():
        for q in (0, 1):
            tree.wait(2, 0, q, 1)
            tree.wait(0, 2, 2 + q, 1)
        for d in (1, -1):
            tree.send(2, 0, 0, 2, 0, d)
            tree.send(0, 2, 2, 2, d, 0)

    def fifth():
        for sx in (1, -1):
            for sz in (1, -1):
                tree.wait(sx, sz, 0, 2)
                tree.send(sx, sz, up(-sz), 1, 0, -sz)
                tree.wait(sx, sz, 2, 2)
                tree.send(sx, sz, 2 + up(-sx), 1, -sx, 0)
                sibling(sx, sz)

    def sixth():
        for q in (0, 1):
            tree.wait(2, 0, 2 + q, 1)
            tree.wait(0, 2, q, 1)
        sibling(2, 0)
        sibling(0, 2)
        for s in (1, -1):
            tree.wait(2, s, 0, 2)
            tree.send(2, s, up(-s), 1, 0, -s)
            tree.wait(s, 2, 2, 2)
            tree.send(s, 2, 2 + up(-s), 1, -s, 0)

    def seventh():
        for s in (1, -1):
            for q in (0, 1):
                tree.wait(2, s, 2 + q, 1)
                tree.wait(s, 2, q, 1)
            sibling(2, s)
            sibling(s, 2)

    def eighth():
        for q in (0, 1, 2, 3):
            tree.wait(2, 2, q, 1)
        sibling(2, 2)

    return first, second, third, fourth, fifth, sixth, seventh, eighth


def meet(others):
    barrier = pltpu.get_barrier_semaphore()
    for other in others:
        pl.semaphore_signal(barrier, inc=1, device_id=other, device_id_type=MESH)
    pl.semaphore_wait(barrier, len(others))


def project_kernel(xq, xp, gain, wq, wk, wv, normed_out, rows_out, mean_out,
                   W, X, acc, macc, wsem, xsem, osem, ssem, rsem, sibs, sibr):
    lq, lp = xq.shape[0] // 4, xp.shape[0] // 4
    tq, tokens = xq.shape[0], X.shape[0]
    width = X.shape[1]
    T = 128
    mine = slot_of(0, 0)
    loads = []
    lo = 0
    for n, w in enumerate((wq, wk, wv)):
        loads.append(pltpu.make_async_copy(
            w, W.at[mine, :, pl.ds(lo, w.shape[1])], wsem.at[n]))
        lo += w.shape[1]
    for load in loads:
        load.start()
    xloads = []
    for i in range(tokens // T):
        src = xq.at[pl.ds(i * T, T)] if i * T < tq else xp.at[pl.ds(i * T - tq, T)]
        xloads.append(pltpu.make_async_copy(src, X.at[pl.ds(i * T, T)], xsem.at[i]))
    for load in xloads:
        load.start()
    meet([dev(1, 0), dev(-1, 0), dev(0, 1), dev(0, -1), dev(0, 0, flip=True)])
    for load in loads:
        load.wait()

    tree = Tree(W, W.shape[1] // 4, ssem, rsem)
    sib_sent = []

    def sib_copy(i, a, b, flip):
        view = W.at[slot_of(a, b, flip=flip)]
        return pltpu.make_async_remote_copy(
            src_ref=view, dst_ref=view, send_sem=sibs.at[i], recv_sem=sibr.at[i],
            device_id=dev(0, 0, flip=True), device_id_type=MESH)

    def sibling(a, b):
        sib_copy(len(sib_sent), a, b, False).start()
        sib_sent.append((a % 4, b % 4))

    stages = gather_stages(tree, sibling)

    def norm_tile(i):
        xloads[i].wait()
        seq = i if i * T < tq else 4 + (i * T - tq) // lp
        start = (i * T) % lq == 0 if i * T < tq else (i * T - tq) % lp == 0
        end = ((i + 1) * T) % lq == 0 if i * T < tq else ((i + 1) * T - tq) % lp == 0
        if start:
            macc[...] = jnp.zeros_like(macc)

        @pl.loop(0, T // 16)
        def _(s):
            r = pl.ds(pl.multiple_of(i * T + s * 16, 16), 16)
            v = X[r, :].astype(f32)
            scale = lax.rsqrt(jnp.sum(v * v, axis=1, keepdims=True) * (1.0 / width) + eps_norm)
            X[r, :] = (v * scale * gain[...]).astype(bf16)
            macc[...] += v[0:8] + v[8:16]

        if end:
            L = lq if i * T < tq else lp
            mean_out[pl.ds(seq, 1), :] = jnp.sum(macc[...], axis=0, keepdims=True) * (1.0 / L)
        out = pltpu.make_async_copy(X.at[pl.ds(i * T, T)], normed_out.at[pl.ds(i * T, T)], osem.at[i])
        out.start()
        return out

    def matmul(chips, first=False, last=False):
        for a, b in chips:
            i = sib_sent.index((a % 4, b % 4))
            sib_copy(i, a, b, True).wait_recv()
        R = 256

        @pl.loop(0, tokens // R)
        def _(r):
            rows = pl.ds(pl.multiple_of(r * R, R), R)
            total = None
            for a, b in chips:
                chip = chip_of(a, b)
                depth = 2 * W.shape[1]
                cols = pl.ds(pl.multiple_of(chip * depth, depth), depth)
                w = W[pl.ds(chip * 2, 2)].reshape(depth, W.shape[2])
                part = jnp.dot(X[rows, cols], w, preferred_element_type=f32)
                total = part if total is None else total + part
            if not first:
                total = total + acc[rows, :]
            if last:
                rows_out[rows, :] = total.astype(bf16)
            else:
                acc[rows, :] = total

    stages[0]()
    outs = []
    n_tiles = tokens // T
    at = {4: 1, 7: 2, 11: 3}
    for i in range(n_tiles):
        outs.append(norm_tile(i))
        if i in at:
            stages[at[i]]()
    matmul([(0, 0)], first=True)
    stages[4]()
    matmul([(1, 0), (-1, 0)])
    matmul([(0, 1), (0, -1)])
    stages[5]()
    matmul([(1, 1), (1, -1), (-1, 1), (-1, -1)])
    stages[6]()
    matmul([(2, 0), (0, 2)])
    stages[7]()
    matmul([(2, 1), (2, -1), (1, 2), (-1, 2)])
    matmul([(2, 2)], last=True)
    tree.finish()
    for i, (a, b) in enumerate(sib_sent):
        sib_copy(i, a, b, False).wait_send()
    for out in outs:
        out.wait()


def project(xq, xp, gain, wq, wk, wv):
    tokens, width = xq.shape[0] + xp.shape[0], xq.shape[1]
    cols = wq.shape[1] + wk.shape[1] + wv.shape[1]
    rows = wq.shape[0]
    ANY, VM = pl.BlockSpec(memory_space=pl.ANY), pl.BlockSpec(memory_space=pltpu.VMEM)
    dma = pltpu.SemaphoreType.DMA
    return pl.pallas_call(
        project_kernel,
        out_shape=(
            jax.ShapeDtypeStruct((tokens, width), bf16),
            jax.ShapeDtypeStruct((tokens, cols), bf16),
            jax.ShapeDtypeStruct((8, width), f32),
        ),
        in_specs=[ANY, ANY, VM, ANY, ANY, ANY],
        out_specs=(ANY, VM, VM),
        scratch_shapes=[
            pltpu.VMEM((32, rows, cols), bf16),
            pltpu.VMEM((tokens, width), bf16),
            pltpu.VMEM((tokens, cols), f32),
            pltpu.VMEM((8, width), f32),
            dma((3,)), dma((tokens // 128,)), dma((tokens // 128,)),
            dma((40,)), dma((40,)), dma((16,)), dma((16,)),
        ],
        compiler_params=pltpu.CompilerParams(
            collective_id=0, has_side_effects=True, vmem_limit_bytes=56 * 1024 * 1024),
        cost_estimate=pl.CostEstimate(flops=2 * tokens * width * cols, bytes_accessed=2 * 2 * tokens * width,
                                      transcendentals=0),
        name="gather_project",
    )(xq, xp, gain.reshape(1, -1), wq, wk, wv)


def attention_table(query_rows, key_rows, groups, head_width):
    seq_count = key_rows.shape[0]
    length = key_rows.shape[1]
    kv_count = key_rows.shape[2] // head_width
    query_wide = query_rows.astype(jnp.float32).reshape(
        seq_count, length, kv_count, groups, head_width
    )
    key_wide = key_rows.astype(jnp.float32).reshape(seq_count, length, kv_count, head_width)
    scores = jnp.einsum("sikge,sjke->skgij", query_wide, key_wide) / math.sqrt(head_width)
    causal_mask = lax.broadcasted_iota(jnp.int32, (length, length), 0) >= lax.broadcasted_iota(
        jnp.int32, (length, length), 1
    )
    raised_powers = jnp.where(causal_mask, jnp.exp(jnp.where(causal_mask, scores, 0.0)), 0.0)
    attend = raised_powers / jnp.sum(raised_powers, axis=-1, keepdims=True)
    weights = jnp.mean(attend, axis=-2)
    return (query_wide, key_wide, attend, weights)


def pooled_attention(query_rows, key_rows, value_rows, groups, head_width):
    query_wide, key_wide, attend, weights = attention_table(
        query_rows, key_rows, groups, head_width
    )
    value_wide = value_rows.astype(jnp.float32).reshape(key_wide.shape)
    pooled = jnp.einsum("skgj,sjke->skge", weights, value_wide)
    return pooled.reshape(pooled.shape[0], -1).astype(jnp.bfloat16)


def attention_grads(query_rows, key_rows, value_rows, upstream, groups, head_width):
    query_wide, key_wide, attend, weights = attention_table(
        query_rows, key_rows, groups, head_width
    )
    value_wide = value_rows.astype(jnp.float32).reshape(key_wide.shape)
    length = key_wide.shape[1]
    upstream_wide = upstream.reshape(key_wide.shape[0], key_wide.shape[2], groups, head_width)
    coefficient = jnp.einsum("sjke,skge->skgj", value_wide, upstream_wide) / length
    inner_sum = jnp.sum(attend * coefficient[:, :, :, None, :], axis=-1, keepdims=True)
    dscores = attend * (coefficient[:, :, :, None, :] - inner_sum) / math.sqrt(head_width)
    query_grad = jnp.einsum("skgij,sjke->sikge", dscores, key_wide)
    key_grad = jnp.einsum("skgij,sikge->sjke", dscores, query_wide)
    value_grad = jnp.einsum("skgj,skge->sjke", weights, upstream_wide)
    shape_rows = (key_wide.shape[0] * length, -1)
    return tuple(
        (
            gradient.reshape(shape_rows).astype(jnp.bfloat16)
            for gradient in (query_grad, key_grad, value_grad)
        )
    )


def normalize_rows(raw):
    inverse = lax.rsqrt(jnp.sum(raw * raw, axis=-1, keepdims=True) + eps_unit)
    return (raw * inverse, inverse)


def normalize_back(embedded, inverse, gradient):
    return inverse * (gradient - embedded * jnp.sum(embedded * gradient, axis=-1, keepdims=True))


def contrast(question_embeds, document_embeds, passage_ids):
    row_count = question_embeds.shape[0]
    passage_count = document_embeds.shape[0]
    columns = lax.broadcasted_iota(jnp.int32, (row_count, passage_count), 1)
    positive = lax.broadcasted_iota(jnp.int32, (row_count, passage_count), 0)
    paired_entries = (columns == positive).astype(jnp.float32)
    listed = jnp.arange(passage_count, dtype=jnp.int32)
    counts = jnp.sum((passage_ids[:, :, None] == listed[None, None, :]).astype(jnp.float32), axis=1)
    cosine_matrix = (
        jnp.dot(question_embeds, document_embeds.T, precision=lax.Precision.HIGHEST)
        / sharpness_divisor
    )
    raised_powers = jnp.exp(cosine_matrix) * (1.0 + counts)
    partition_sums = jnp.sum(raised_powers, axis=1, keepdims=True)
    total_sum = jnp.sum(
        jnp.log(partition_sums[:, 0]) - jnp.sum(cosine_matrix * paired_entries, axis=1)
    )
    score_derivative = (raised_powers / partition_sums - paired_entries) / sharpness_divisor
    d_query = jnp.dot(score_derivative, document_embeds, precision=lax.Precision.HIGHEST)
    d_passage = jnp.dot(score_derivative.T, question_embeds, precision=lax.Precision.HIGHEST)
    return (total_sum, d_query, d_passage)


def set_rows(source, offset_rows, seq_count, length):
    return source[offset_rows : offset_rows + seq_count * length].reshape(
        seq_count, length, source.shape[1]
    )


def body(
    query_states, passage_states, norm_gain, w_query, w_key, w_value, w_out, neg_owner, neg_slot
):
    owned = query_states.shape[0]
    query_length = query_states.shape[1]
    passage_length = passage_states.shape[1]
    query_cols = w_query.shape[1]
    key_cols = w_key.shape[1]
    groups = query_cols // key_cols
    query_tokens = owned * query_length
    normed, rows, means = project(
        query_states.reshape(query_tokens, -1), passage_states.reshape(owned * passage_length, -1),
        norm_gain, w_query, w_key, w_value)
    query_rows, key_rows, value_rows = (
        rows[:, :query_cols], rows[:, query_cols:query_cols + key_cols], rows[:, query_cols + key_cols:])
    query_parts = tuple(
        (set_rows(block, 0, owned, query_length) for block in (query_rows, key_rows, value_rows))
    )
    passage_parts = tuple(
        (
            set_rows(block, query_tokens, owned, passage_length)
            for block in (query_rows, key_rows, value_rows)
        )
    )
    pooled_query = pooled_attention(
        query_parts[0], query_parts[1], query_parts[2], groups, HEAD_DIM
    )
    pooled_passage = pooled_attention(
        passage_parts[0], passage_parts[1], passage_parts[2], groups, HEAD_DIM
    )
    head_query, head_passage = (
        lax.psum(
            jnp.dot(pooled_query, w_out, preferred_element_type=jnp.float32).astype(jnp.bfloat16),
            "tensor",
        ).astype(jnp.float32),
        lax.psum(
            jnp.dot(pooled_passage, w_out, preferred_element_type=jnp.float32).astype(jnp.bfloat16),
            "tensor",
        ).astype(jnp.float32),
    )
    question_embeds, query_inverse = normalize_rows(
        means[:owned] + head_query
    )
    document_embeds, passage_inverse = normalize_rows(
        means[owned:] + head_passage
    )
    first_row = lax.axis_index("dp") * owned
    passage_ids = neg_owner * owned + neg_slot
    every_query, every_passage = (
        lax.all_gather(question_embeds, "dp", axis=0, tiled=True),
        lax.all_gather(document_embeds, "dp", axis=0, tiled=True),
    )
    total_sum, d_every_query, d_every_passage = contrast(every_query, every_passage, passage_ids)
    loss = total_sum / every_query.shape[0]
    d_query = lax.dynamic_slice_in_dim(d_every_query, first_row, owned, 0)
    d_passage = lax.dynamic_slice_in_dim(d_every_passage, first_row, owned, 0)
    contract_cols = (((1,), (1,)), ((), ()))
    raw_query_grad = normalize_back(question_embeds, query_inverse, d_query).astype(jnp.bfloat16)
    raw_passage_grad = normalize_back(document_embeds, passage_inverse, d_passage).astype(
        jnp.bfloat16
    )
    upstream_query = lax.dot_general(
        raw_query_grad, w_out, contract_cols, preferred_element_type=jnp.float32
    )
    upstream_passage = lax.dot_general(
        raw_passage_grad, w_out, contract_cols, preferred_element_type=jnp.float32
    )
    query_side = attention_grads(
        query_parts[0], query_parts[1], query_parts[2], upstream_query, groups, HEAD_DIM
    )
    passage_side = attention_grads(
        passage_parts[0], passage_parts[1], passage_parts[2], upstream_passage, groups, HEAD_DIM
    )
    grads_joined = jnp.concatenate(
        [
            jnp.concatenate([query_side[0], passage_side[0]], axis=0),
            jnp.concatenate([query_side[1], passage_side[1]], axis=0),
            jnp.concatenate([query_side[2], passage_side[2]], axis=0),
        ],
        axis=1,
    )
    columns = normed
    summed = lax.psum_scatter(
        lax.dot_general(
            columns, grads_joined, (((0,), (0,)), ((), ())), preferred_element_type=jnp.float32
        ).astype(jnp.bfloat16),
        "dp",
        scatter_dimension=0,
        tiled=True,
    ).astype(jnp.float32)
    return (
        loss,
        summed[:, :query_cols],
        summed[:, query_cols : query_cols + key_cols],
        summed[:, query_cols + key_cols :],
    )


def solution(mesh):
    in_specs = (
        P("dp", None, None),
        P("dp", None, None),
        P(),
        P("dp", "tensor"),
        P("dp", "tensor"),
        P("dp", "tensor"),
        P("tensor", None),
        P(),
        P(),
    )
    out_specs = (P(), P("dp", "tensor"), P("dp", "tensor"), P("dp", "tensor"))
    return jax.shard_map(body, mesh=mesh, in_specs=in_specs, out_specs=out_specs, check_vma=False)
```

```python
import functools
import math

import jax
import jax.numpy as jnp
from jax import lax
from jax.experimental import pallas as pl
from jax.experimental.pallas import tpu as pltpu
from jax.sharding import PartitionSpec as P

HEAD_DIM = 128
eps_norm = 1e-06
eps_unit = 1e-06
sharpness_divisor = 0.05
MESH = pl.DeviceIdType.MESH
f32, bf16 = jnp.float32, jnp.bfloat16
XS, ZS = 4, 4


def place():
    p = lax.axis_index("dp")
    return p // (2 * ZS), (p // 2) % ZS, p % 2


def slot_of(a, b, core=None, flip=False):
    x, z, c = place()
    c = 1 - c if flip else c
    return ((x + a) % XS * ZS + (z + b) % ZS) * 2 + c


def chip_of(a, b):
    x, z, _ = place()
    return (x + a) % XS * ZS + (z + b) % ZS


def dev(a, b, flip=False):
    return {"dp": slot_of(a, b, flip=flip)}


class Tree:
    def __init__(self, buf, rows, send_sem, recv_sem):
        self.buf, self.rows, self.send_sem, self.recv_sem = buf, rows, send_sem, recv_sem
        self.sends, self.pieces, self.waited = [], {}, set()

    def view(self, a, b, lo, n):
        return self.buf.at[slot_of(a, b), pl.ds(lo * self.rows, n * self.rows)]

    def copy(self, i):
        a, b, lo, n, dx, dz = self.sends[i]
        view = self.view(a, b, lo, n)
        return pltpu.make_async_remote_copy(
            src_ref=view, dst_ref=view, send_sem=self.send_sem.at[i], recv_sem=self.recv_sem.at[i],
            device_id=dev(dx, dz), device_id_type=MESH)

    def send(self, a, b, lo, n, dx, dz):
        i = len(self.sends)
        self.sends.append((a, b, lo, n, dx, dz))
        self.pieces[((a - dx) % 4, (b - dz) % 4, lo, n)] = i
        self.copy(i).start()

    def wait(self, a, b, lo, n):
        i = self.pieces[(a % 4, b % 4, lo, n)]
        view = self.view(a, b, lo, n)
        pltpu.make_async_remote_copy(
            src_ref=view, dst_ref=view, send_sem=self.send_sem.at[i], recv_sem=self.recv_sem.at[i],
            device_id=dev(1, 0), device_id_type=MESH).wait_recv()
        self.waited.add(i)

    def finish(self):
        assert self.waited == set(range(len(self.sends)))
        for i in range(len(self.sends)):
            self.copy(i).wait_send()


def up(d):
    return 0 if d > 0 else 1


def gather_stages(tree, sibling):
    def first():
        for d in (1, -1):
            tree.send(0, 0, 0, 2, d, 0)
            tree.send(0, 0, 2, 2, 0, d)
        for d in (1, -1):
            tree.send(0, 0, 2, 2, d, 0)
            tree.send(0, 0, 0, 2, 0, d)
        sibling(0, 0)

    def second():
        for s in (1, -1):
            tree.wait(s, 0, 0, 2)
            tree.send(s, 0, up(-s), 1, -s, 0)
            tree.wait(0, s, 2, 2)
            tree.send(0, s, 2 + up(-s), 1, 0, -s)
        for s in (1, -1):
            for d in (1, -1):
                tree.send(s, 0, 0, 2, 0, d)
                tree.send(0, s, 2, 2, d, 0)

    def third():
        for s in (1, -1):
            tree.wait(s, 0, 2, 2)
            tree.send(s, 0, 2 + up(-s), 1, -s, 0)
            tree.wait(0, s, 0, 2)
            tree.send(0, s, up(-s), 1, 0, -s)
        for s in (1, -1):
            sibling(s, 0)
            sibling(0, s)

    def fourth():
        for q in (0, 1):
            tree.wait(2, 0, q, 1)
            tree.wait(0, 2, 2 + q, 1)
        for d in (1, -1):
            tree.send(2, 0, 0, 2, 0, d)
            tree.send(0, 2, 2, 2, d, 0)

    def fifth():
        for sx in (1, -1):
            for sz in (1, -1):
                tree.wait(sx, sz, 0, 2)
                tree.send(sx, sz, up(-sz), 1, 0, -sz)
                tree.wait(sx, sz, 2, 2)
                tree.send(sx, sz, 2 + up(-sx), 1, -sx, 0)
                sibling(sx, sz)

    def sixth():
        for q in (0, 1):
            tree.wait(2, 0, 2 + q, 1)
            tree.wait(0, 2, q, 1)
        sibling(2, 0)
        sibling(0, 2)
        for s in (1, -1):
            tree.wait(2, s, 0, 2)
            tree.send(2, s, up(-s), 1, 0, -s)
            tree.wait(s, 2, 2, 2)
            tree.send(s, 2, 2 + up(-s), 1, -s, 0)

    def seventh():
        for s in (1, -1):
            for q in (0, 1):
                tree.wait(2, s, 2 + q, 1)
                tree.wait(s, 2, q, 1)
            sibling(2, s)
            sibling(s, 2)

    def eighth():
        for q in (0, 1, 2, 3):
            tree.wait(2, 2, q, 1)
        sibling(2, 2)

    return first, second, third, fourth, fifth, sixth, seventh, eighth


def meet(others):
    barrier = pltpu.get_barrier_semaphore()
    for other in others:
        pl.semaphore_signal(barrier, inc=1, device_id=other, device_id_type=MESH)
    pl.semaphore_wait(barrier, len(others))


def project_kernel(xq, xp, gain, wq, wk, wv, normed_out, rows_out, mean_out,
                   W, X, acc, macc, wsem, xsem, osem, ssem, rsem, sibs, sibr):
    lq, lp = xq.shape[0] // 4, xp.shape[0] // 4
    tq, tokens = xq.shape[0], X.shape[0]
    width = X.shape[1]
    T = 128
    mine = slot_of(0, 0)
    loads = []
    lo = 0
    for n, w in enumerate((wq, wk, wv)):
        loads.append(pltpu.make_async_copy(
            w, W.at[mine, :, pl.ds(lo, w.shape[1])], wsem.at[n]))
        lo += w.shape[1]
    for load in loads:
        load.start()
    xloads = []
    for i in range(tokens // T):
        src = xq.at[pl.ds(i * T, T)] if i * T < tq else xp.at[pl.ds(i * T - tq, T)]
        xloads.append(pltpu.make_async_copy(src, X.at[pl.ds(i * T, T)], xsem.at[i]))
    for load in xloads:
        load.start()
    meet([dev(1, 0), dev(-1, 0), dev(0, 1), dev(0, -1), dev(0, 0, flip=True)])
    for load in loads:
        load.wait()

    tree = Tree(W, W.shape[1] // 4, ssem, rsem)
    sib_sent = []

    def sib_copy(i, a, b, flip):
        view = W.at[slot_of(a, b, flip=flip)]
        return pltpu.make_async_remote_copy(
            src_ref=view, dst_ref=view, send_sem=sibs.at[i], recv_sem=sibr.at[i],
            device_id=dev(0, 0, flip=True), device_id_type=MESH)

    def sibling(a, b):
        sib_copy(len(sib_sent), a, b, False).start()
        sib_sent.append((a % 4, b % 4))

    stages = gather_stages(tree, sibling)

    def norm_tile(i):
        xloads[i].wait()
        seq = i if i * T < tq else 4 + (i * T - tq) // lp
        start = (i * T) % lq == 0 if i * T < tq else (i * T - tq) % lp == 0
        end = ((i + 1) * T) % lq == 0 if i * T < tq else ((i + 1) * T - tq) % lp == 0
        if start:
            macc[...] = jnp.zeros_like(macc)

        @pl.loop(0, T // 16)
        def _(s):
            r = pl.ds(pl.multiple_of(i * T + s * 16, 16), 16)
            v = X[r, :].astype(f32)
            scale = lax.rsqrt(jnp.sum(v * v, axis=1, keepdims=True) * (1.0 / width) + eps_norm)
            X[r, :] = (v * scale * gain[...]).astype(bf16)
            macc[...] += v[0:8] + v[8:16]

        if end:
            L = lq if i * T < tq else lp
            mean_out[pl.ds(seq, 1), :] = jnp.sum(macc[...], axis=0, keepdims=True) * (1.0 / L)
        out = pltpu.make_async_copy(X.at[pl.ds(i * T, T)], normed_out.at[pl.ds(i * T, T)], osem.at[i])
        out.start()
        return out

    def matmul(chips, first=False, last=False):
        for a, b in chips:
            i = sib_sent.index((a % 4, b % 4))
            sib_copy(i, a, b, True).wait_recv()
        R = 256

        @pl.loop(0, tokens // R)
        def _(r):
            rows = pl.ds(pl.multiple_of(r * R, R), R)
            total = None
            for a, b in chips:
                chip = chip_of(a, b)
                depth = 2 * W.shape[1]
                cols = pl.ds(pl.multiple_of(chip * depth, depth), depth)
                w = W[pl.ds(chip * 2, 2)].reshape(depth, W.shape[2])
                part = jnp.dot(X[rows, cols], w, preferred_element_type=f32)
                total = part if total is None else total + part
            if not first:
                total = total + acc[rows, :]
            if last:
                rows_out[rows, :] = total.astype(bf16)
            else:
                acc[rows, :] = total

    stages[0]()
    outs = []
    n_tiles = tokens // T
    at = {4: 1, 7: 2, 11: 3}
    for i in range(n_tiles):
        outs.append(norm_tile(i))
        if i in at:
            stages[at[i]]()
    matmul([(0, 0)], first=True)
    stages[4]()
    matmul([(1, 0), (-1, 0)])
    matmul([(0, 1), (0, -1)])
    stages[5]()
    matmul([(1, 1), (1, -1), (-1, 1), (-1, -1)])
    stages[6]()
    matmul([(2, 0), (0, 2)])
    stages[7]()
    matmul([(2, 1), (2, -1), (1, 2), (-1, 2)])
    matmul([(2, 2)], last=True)
    tree.finish()
    for i, (a, b) in enumerate(sib_sent):
        sib_copy(i, a, b, False).wait_send()
    for out in outs:
        out.wait()


def project(xq, xp, gain, wq, wk, wv):
    tokens, width = xq.shape[0] + xp.shape[0], xq.shape[1]
    cols = wq.shape[1] + wk.shape[1] + wv.shape[1]
    rows = wq.shape[0]
    ANY, VM = pl.BlockSpec(memory_space=pl.ANY), pl.BlockSpec(memory_space=pltpu.VMEM)
    dma = pltpu.SemaphoreType.DMA
    return pl.pallas_call(
        project_kernel,
        out_shape=(
            jax.ShapeDtypeStruct((tokens, width), bf16),
            jax.ShapeDtypeStruct((tokens, cols), bf16),
            jax.ShapeDtypeStruct((8, width), f32),
        ),
        in_specs=[ANY, ANY, VM, ANY, ANY, ANY],
        out_specs=(ANY, VM, VM),
        scratch_shapes=[
            pltpu.VMEM((32, rows, cols), bf16),
            pltpu.VMEM((tokens, width), bf16),
            pltpu.VMEM((tokens, cols), f32),
            pltpu.VMEM((8, width), f32),
            dma((3,)), dma((tokens // 128,)), dma((tokens // 128,)),
            dma((40,)), dma((40,)), dma((16,)), dma((16,)),
        ],
        compiler_params=pltpu.CompilerParams(
            collective_id=0, has_side_effects=True, vmem_limit_bytes=56 * 1024 * 1024),
        cost_estimate=pl.CostEstimate(flops=2 * tokens * width * cols, bytes_accessed=2 * 2 * tokens * width,
                                      transcendentals=0),
        name="gather_project",
    )(xq, xp, gain.reshape(1, -1), wq, wk, wv)


ORDER = ((2, 2), (2, 1), (2, -1), (1, 2), (-1, 2), (2, 0), (0, 2), (1, 1), (1, -1), (-1, 1), (-1, -1),
         (1, 0), (-1, 0), (0, 1), (0, -1), (0, 0))


def key_of(a, b):
    return a % 4, b % 4


class Fold:
    def __init__(self, part, landed, send_sem, recv_sem):
        self.part, self.landed, self.send_sem, self.recv_sem = part, landed, send_sem, recv_sem
        self.sends, self.pieces, self.used, self.waited = [], {}, 0, set()
        self.index = {key_of(a, b): i for i, (a, b) in enumerate(ORDER)}

    def copy(self, i):
        a, b, lo, n, dx, dz, off = self.sends[i]
        return pltpu.make_async_remote_copy(
            src_ref=self.part.at[self.index[key_of(a, b)], pl.ds(lo, n)], dst_ref=self.landed.at[pl.ds(off, n)],
            send_sem=self.send_sem.at[i], recv_sem=self.recv_sem.at[i],
            device_id=dev(dx, dz), device_id_type=MESH)

    def send(self, a, b, lo, n, dx, dz):
        i = len(self.sends)
        self.sends.append((a, b, lo, n, dx, dz, self.used))
        self.used += n
        self.pieces[(*key_of(a - dx, b - dz), lo, n, *key_of(-dx, -dz))] = i
        self.copy(i).start()

    def recv(self, a, b, lo, n, dx, dz):
        i = self.pieces[(*key_of(a, b), lo, n, *key_of(dx, dz))]
        self.copy(i).wait_recv()
        self.waited.add(i)
        off = self.sends[i][6]
        return self.landed[pl.ds(off, n)]

    def add(self, a, b, lo, n, *froms):
        at = self.index[key_of(a, b)]
        for m, (dx, dz) in froms:
            piece = self.recv(a, b, m[0], m[1], dx, dz)
            self.part[at, pl.ds(m[0], m[1])] = self.part[at, pl.ds(m[0], m[1])] + piece

    def finish(self):
        assert self.waited == set(range(len(self.sends))), (len(self.waited), len(self.sends))
        for i in range(len(self.sends)):
            self.copy(i).wait_send()


def ends(fold, a, b, half):
    if half == 0:
        fold.send(a, b, 0, 1, 0, -1)
        fold.send(a, b, 1, 1, 0, 1)
    else:
        fold.send(a, b, 2, 1, -1, 0)
        fold.send(a, b, 3, 1, 1, 0)


def fold_scatter(compute, add_sibling, fold):
    def one(i):
        add_sibling(i)
        a, b = ORDER[i]
        if (a, b) == (2, 2):
            ends(fold, a, b, 0)
            ends(fold, a, b, 1)
        elif a == 2:
            ends(fold, a, b, 1)
        elif b == 2:
            ends(fold, a, b, 0)
        elif a and b:
            q = up(-b)
            fold.add(a, b, 0, 2, ((q, 1), (0, -b)))
            fold.send(a, b, 0, 2, 0, b)
            q = 2 + up(-a)
            fold.add(a, b, 2, 2, ((q, 1), (-a, 0)))
            fold.send(a, b, 2, 2, a, 0)

    compute(0)
    compute(1)
    one(0)
    for i in range(2, 7):
        compute(i)
        one(i - 1)
    compute(7)
    one(6)
    for s in (1, -1):
        fold.add(2, s, 0, 2, ((up(-s), 1), (0, -s)))
        fold.send(2, s, 0, 2, 0, s)
        fold.add(s, 2, 2, 2, ((2 + up(-s), 1), (-s, 0)))
        fold.send(s, 2, 2, 2, s, 0)
    for i in range(8, 12):
        compute(i)
        one(i - 1)
    compute(12)
    add_sibling(11)
    fold.add(2, 0, 0, 2, ((0, 2), (0, 1)), ((0, 2), (0, -1)))
    fold.send(2, 0, 0, 1, -1, 0)
    fold.send(2, 0, 1, 1, 1, 0)
    fold.add(0, 2, 2, 2, ((2, 2), (1, 0)), ((2, 2), (-1, 0)))
    fold.send(0, 2, 2, 1, 0, -1)
    fold.send(0, 2, 3, 1, 0, 1)
    compute(13)
    add_sibling(12)
    compute(14)
    add_sibling(13)
    add_sibling(14)
    for s in (1, -1):
        fold.add(s, 0, 2, 2, ((2 + up(-s), 1), (-s, 0)))
        fold.send(s, 0, 2, 2, s, 0)
        fold.add(0, s, 0, 2, ((up(-s), 1), (0, -s)))
        fold.send(0, s, 0, 2, 0, s)
    compute(15)
    for s in (1, -1):
        fold.add(s, 0, 0, 2, ((0, 2), (0, 1)), ((0, 2), (0, -1)), ((up(-s), 1), (-s, 0)))
        fold.send(s, 0, 0, 2, s, 0)
        fold.add(0, s, 2, 2, ((2, 2), (1, 0)), ((2, 2), (-1, 0)), ((2 + up(-s), 1), (0, -s)))
        fold.send(0, s, 2, 2, 0, s)


def scatter_kernel(normed, dgt, gq, gk, gv, X, part, away, sib, landed, xsem, ssem, rsem, sibs, sibr):
    depth = 2 * gq.shape[0]
    rows = dgt.shape[0]
    qr = part.shape[2]
    loads = []
    for i, (a, b) in enumerate(ORDER):
        cols = pl.ds(pl.multiple_of(chip_of(a, b) * depth, depth), depth)
        loads.append(pltpu.make_async_copy(normed.at[:, cols], X.at[i], xsem.at[i]))
    for load in loads:
        load.start()
    meet([dev(1, 0), dev(-1, 0), dev(0, 1), dev(0, -1), dev(0, 0, flip=True)])
    core = place()[2]
    R = 2 * qr

    def sib_copy(i):
        return pltpu.make_async_remote_copy(
            src_ref=away.at[i], dst_ref=sib.at[i], send_sem=sibs.at[i], recv_sem=sibr.at[i],
            device_id=dev(0, 0, flip=True), device_id_type=MESH)

    def compute(i):
        loads[i].wait()

        @pl.loop(0, rows // R)
        def _(r):
            d = dgt[pl.ds(pl.multiple_of(r * R, R), R), :]
            total = jnp.dot(d, X[i], preferred_element_type=f32).astype(bf16)
            low, high = total[:, :depth // 2], total[:, depth // 2:]
            for n in range(R // qr):
                lo, hi = low[n * qr:(n + 1) * qr], high[n * qr:(n + 1) * qr]
                part[i, r * (R // qr) + n] = jnp.where(core == 0, lo, hi)
                away[i, r * (R // qr) + n] = jnp.where(core == 0, hi, lo)

        sib_copy(i).start()

    def add_sibling(i):
        sib_copy(i).wait_recv()
        part[i] = part[i] + sib[i]

    fold = Fold(part, landed, ssem, rsem)
    fold_scatter(compute, add_sibling, fold)
    add_sibling(15)
    heads = gq.shape[1] // HEAD_DIM
    for half in (0, 1):
        total = part[15, pl.ds(2 * half, 2)].astype(f32)
        for dx, dz in ((1, 0), (-1, 0), (0, 1), (0, -1)):
            total = total + fold.recv(0, 0, 2 * half, 2, dx, dz).astype(f32)
        total = total.reshape(2 * qr, depth // 2)
        for n in range(2 * qr // HEAD_DIM):
            block = total[n * HEAD_DIM:(n + 1) * HEAD_DIM].T
            at = half * (2 * qr // HEAD_DIM) + n
            if at < heads:
                gq[:, at * HEAD_DIM:(at + 1) * HEAD_DIM] = block
            elif at == heads:
                gk[...] = block
            else:
                gv[...] = block
    fold.finish()
    for i in range(16):
        sib_copy(i).wait_send()


def scatter(normed, dgt, depth):
    tokens, width = normed.shape
    rows = dgt.shape[0]
    ANY, VM = pl.BlockSpec(memory_space=pl.ANY), pl.BlockSpec(memory_space=pltpu.VMEM)
    dma = pltpu.SemaphoreType.DMA
    cols = (rows - 2 * HEAD_DIM, HEAD_DIM, HEAD_DIM)
    return pl.pallas_call(
        scatter_kernel,
        out_shape=tuple(jax.ShapeDtypeStruct((depth, n), f32) for n in cols),
        in_specs=[ANY, VM],
        out_specs=(VM, VM, VM),
        scratch_shapes=[
            pltpu.VMEM((16, tokens, 2 * depth), bf16),
            pltpu.VMEM((16, 4, rows // 4, depth), bf16),
            pltpu.VMEM((16, 4, rows // 4, depth), bf16),
            pltpu.VMEM((16, 4, rows // 4, depth), bf16),
            pltpu.VMEM((60, rows // 4, depth), bf16),
            dma((16,)), dma((40,)), dma((40,)), dma((16,)), dma((16,)),
        ],
        compiler_params=pltpu.CompilerParams(
            collective_id=1, has_side_effects=True, vmem_limit_bytes=56 * 1024 * 1024),
        cost_estimate=pl.CostEstimate(flops=2 * tokens * width * rows, bytes_accessed=2 * tokens * width,
                                      transcendentals=0),
        name="grad_scatter",
    )(normed, dgt)


NT = (((1,), (1,)), ((), ()))
NN = (((1,), (0,)), ((), ()))
EXACT = lax.Precision.HIGHEST
AROUND = tuple((a, b) for a in (1, 3, 0, 2) for b in (1, 3, 0, 2) if (a, b) != (0, 0))


def iota(shape, dim):
    return lax.broadcasted_iota(jnp.int32, shape, dim)


def units_of(s, is_passage, blocks):
    return (blocks * (blocks + 1) // 2) * s


def attend_forward(rows, att, wts, pooled, base, blocks, unit, seq, groups):
    H = HEAD_DIM
    key_at, value_at = groups * H, (groups + 1) * H
    L = blocks * H
    k = rows[pl.ds(base, L), key_at:key_at + H]
    v = rows[pl.ds(base, L), value_at:value_at + H].astype(f32)
    causal = iota((H, H), 0) <= iota((H, H), 1)
    n = 0
    for h in range(groups):
        w = [None] * blocks
        for ib in range(blocks):
            q = rows[pl.ds(pl.multiple_of(base + ib * H, H), H), h * H:(h + 1) * H]
            e = []
            for jb in range(ib + 1):
                st = lax.dot_general(k[jb * H:(jb + 1) * H], q, NT, preferred_element_type=f32)
                st = jnp.exp(st * (1.0 / math.sqrt(H)))
                e.append(jnp.where(causal, st, 0.0) if jb == ib else st)
            total = jnp.sum(e[0], axis=0, keepdims=True)
            for one in e[1:]:
                total = total + jnp.sum(one, axis=0, keepdims=True)
            r = 1.0 / total
            for jb in range(ib + 1):
                at = e[jb] * r
                att[unit + n] = at
                n += 1
                w[jb] = at if w[jb] is None else w[jb] + at
        out = None
        for jb in range(blocks):
            col = jnp.sum(w[jb], axis=1, keepdims=True) * (1.0 / L)
            wts[h, pl.ds(pl.multiple_of(base + jb * H, H), H), :] = jnp.broadcast_to(col, (H, H))
            part = jnp.sum(col * v[jb * H:(jb + 1) * H], axis=0, keepdims=True)
            out = part if out is None else out + part
        pooled[seq, :, h * H:(h + 1) * H] = jnp.broadcast_to(out, (8, H))


def attend_backward(rows, att, wts, ups, dgt, base, blocks, unit, seq, groups):
    H = HEAD_DIM
    key_at, value_at = groups * H, (groups + 1) * H
    L = blocks * H
    k = rows[pl.ds(base, L), key_at:key_at + H]
    v = rows[pl.ds(base, L), value_at:value_at + H].astype(f32)
    kt = k.astype(f32).T.astype(bf16)
    dk, dv = [None] * blocks, [None] * blocks
    n = 0
    for h in range(groups):
        u = ups[seq, :, h * H:(h + 1) * H][0:1]
        c = [jnp.sum(v[jb * H:(jb + 1) * H] * u, axis=1, keepdims=True) * (1.0 / L) for jb in range(blocks)]
        for ib in range(blocks):
            span = pl.ds(pl.multiple_of(base + ib * H, H), H)
            q = rows[span, h * H:(h + 1) * H]
            at = [att[unit + n + jb] for jb in range(ib + 1)]
            n += ib + 1
            m = None
            for jb in range(ib + 1):
                part = jnp.sum(at[jb] * c[jb], axis=0, keepdims=True)
                m = part if m is None else m + part
            dq = None
            for jb in range(ib + 1):
                ds = (at[jb] * ((c[jb] - m) * (1.0 / math.sqrt(H)))).astype(bf16)
                part = jnp.dot(kt[:, jb * H:(jb + 1) * H], ds, preferred_element_type=f32)
                dq = part if dq is None else dq + part
                part = jnp.dot(ds, q, preferred_element_type=f32)
                dk[jb] = part if dk[jb] is None else dk[jb] + part
            dgt[h * H:(h + 1) * H, span] = dq.astype(bf16)
        for jb in range(blocks):
            part = wts[h, pl.ds(pl.multiple_of(base + jb * H, H), H), :] * u
            dv[jb] = part if dv[jb] is None else dv[jb] + part
    for jb in range(blocks):
        span = pl.ds(pl.multiple_of(base + jb * H, H), H)
        dgt[key_at:key_at + H, span] = dk[jb].T.astype(bf16)
        dgt[value_at:value_at + H, span] = dv[jb].T.astype(bf16)


def middle_kernel(lq, lp, rows, means, wout_hbm, owner, place_in, dgt, loss,
                  wout, att, wts, pooled, ups, terms, got, embeds, qs, ps, gram, dl, dlt, raws,
                  wsem, asem, arecv, bsem, brecv, sibs, sibr, csem, crecv, dsem, drecv):
    H = HEAD_DIM
    groups = rows.shape[1] // H - 2
    width = wout.shape[1]
    seqs = 4
    nt = 4
    part_w = width // nt
    load = pltpu.make_async_copy(wout_hbm, wout, wsem)
    load.start()
    x, z, core = place()
    t = lax.axis_index("tensor")
    meet([{"tensor": (t + d) % nt} for d in (1, 2, 3)] + [dev(a, b) for a, b in AROUND] + [dev(0, 0, flip=True)])
    base_p = seqs * lq
    bq, bp = lq // H, lp // H
    uq, up_ = groups * bq * (bq + 1) // 2, groups * bp * (bp + 1) // 2

    @pl.loop(0, seqs)
    def _(s):
        attend_forward(rows, att, wts, pooled, pl.multiple_of(s * lq, H), bq, s * uq, s, groups)

    @pl.loop(0, seqs)
    def _(s):
        attend_forward(rows, att, wts, pooled, pl.multiple_of(base_p + s * lp, H), bp,
                       seqs * uq + s * up_, seqs + s, groups)

    load.wait()
    row = iota((8, groups * H), 0)
    low = pooled[0]
    for s in range(1, 8):
        low = jnp.where(row == s, pooled[s], low)
    low = low.astype(bf16)

    def y_copy(src, dst, d, send_sem, recv_sem):
        return pltpu.make_async_remote_copy(
            src_ref=src, dst_ref=dst, send_sem=send_sem.at[d - 1], recv_sem=recv_sem.at[d - 1],
            device_id={"tensor": (t + d) % nt}, device_id_type=MESH)

    def term(o):
        cols = pl.ds(pl.multiple_of(o * part_w, part_w), part_w)
        return jnp.dot(low, wout[:, cols], preferred_element_type=f32)

    a_copies = []
    for d in (2, 1, 3):
        terms[d] = term((t + d) % nt)
        copy = y_copy(terms.at[d], got.at[d], d, asem, arecv)
        copy.start()
        a_copies.append(copy)
    mine = term(t) + means[:, pl.ds(pl.multiple_of(t * part_w, part_w), part_w)]
    n_rows = qs.shape[0]
    ids = owner[...] * seqs + place_in[...]
    col = iota((n_rows, n_rows), 1)
    counts = jnp.zeros((n_rows, n_rows), f32)
    for j in range(ids.shape[1]):
        counts = counts + jnp.where(ids[:, j:j + 1] == col, 1.0, 0.0)
    for copy in a_copies:
        copy.wait_recv()
    mine = mine + got[1] + got[2] + got[3]
    here = slot_of(0, 0)
    embeds[here] = mine

    def b_copy(n, a, b):
        view = embeds.at[here]
        return pltpu.make_async_remote_copy(
            src_ref=view, dst_ref=view, send_sem=bsem.at[n], recv_sem=brecv.at[n],
            device_id=dev(a, b), device_id_type=MESH)

    def s_copy(n, a, b, flip):
        view = embeds.at[slot_of(a, b, flip=flip)]
        return pltpu.make_async_remote_copy(
            src_ref=view, dst_ref=view, send_sem=sibs.at[n], recv_sem=sibr.at[n],
            device_id=dev(0, 0, flip=True), device_id_type=MESH)

    for n, (a, b) in enumerate(AROUND):
        b_copy(n, a, b).start()
    s_copy(15, 0, 0, False).start()
    for n, (a, b) in enumerate(AROUND):
        view = embeds.at[slot_of(-a, -b)]
        pltpu.make_async_remote_copy(
            src_ref=view, dst_ref=view, send_sem=bsem.at[n], recv_sem=brecv.at[n],
            device_id=dev(a, b), device_id_type=MESH).wait_recv()
        s_copy(n, -a, -b, False).start()
    s_copy(15, 0, 0, True).wait_recv()
    for n, (a, b) in enumerate(AROUND):
        s_copy(n, -a, -b, True).wait_recv()

    first = iota((8, part_w), 0) < seqs

    @pl.loop(0, n_rows // 8)
    def _(k):
        one, two = embeds[2 * k], embeds[2 * k + 1]
        span = pl.ds(pl.multiple_of(k * 8, 8), 8)
        qs[span, :] = jnp.where(first, one, pltpu.roll(two, seqs, 0))
        ps[span, :] = jnp.where(first, pltpu.roll(one, seqs, 0), two)

    q, p = qs[...], ps[...]
    gram[0, pl.ds(0, n_rows), :] = lax.dot_general(q, p, NT, precision=EXACT, preferred_element_type=f32)
    ones = jnp.ones((8, part_w), f32)
    gram[0, pl.ds(n_rows, 8), :] = lax.dot_general(ones, q * q, NT, precision=EXACT, preferred_element_type=f32)
    gram[0, pl.ds(n_rows + 8, 8), :] = lax.dot_general(ones, p * p, NT, precision=EXACT, preferred_element_type=f32)
    c_copies = []
    for d in (2, 1, 3):
        copy = y_copy(gram.at[0], gram.at[d], d, csem, crecv)
        copy.start()
        c_copies.append(copy)
    for copy in c_copies:
        copy.wait_recv()
    whole = (gram[0] + gram[2]) + (gram[1] + gram[3])
    eye = iota((n_rows, n_rows), 0) == col
    inv = lax.rsqrt(whole[n_rows:] + eps_unit)
    inv_q_row, inv_p_row = inv[0:1], inv[8:9]
    inv_q = jnp.sum(jnp.where(eye, inv_q_row, 0.0), axis=1, keepdims=True)
    inv_p = jnp.sum(jnp.where(eye, inv_p_row, 0.0), axis=1, keepdims=True)
    cosine = whole[:n_rows] * inv_q * inv_p_row
    logits = cosine * (1.0 / sharpness_divisor)
    raised = jnp.exp(logits) * (1.0 + counts)
    sums = jnp.sum(raised, axis=1, keepdims=True)
    diagonal = jnp.sum(jnp.where(eye, logits, 0.0), axis=1, keepdims=True)
    loss[...] = jnp.sum(jnp.log(sums) - diagonal, axis=0, keepdims=True) * (1.0 / n_rows)
    slope = (raised / sums - jnp.where(eye, 1.0, 0.0)) * (1.0 / sharpness_divisor)
    dl[0] = slope
    dlt[0] = slope.T
    weighted = slope * cosine
    dl[1] = jnp.broadcast_to(jnp.sum(weighted, axis=1, keepdims=True), (n_rows, n_rows))
    dlt[1] = jnp.broadcast_to(jnp.sum(weighted, axis=0, keepdims=True), (n_rows, n_rows)).T
    dl[2] = jnp.broadcast_to(inv_q, (n_rows, n_rows))
    dlt[2] = jnp.broadcast_to(inv_p, (n_rows, n_rows))
    chip = pl.ds(pl.multiple_of(chip_of(0, 0) * 8, 8), 8)

    def back(table, own, others, scale):
        d = jnp.dot(table[0, chip, :], others * scale, precision=EXACT, preferred_element_type=f32)
        inverse = table[2, chip, :][:, 0:1]
        e = own[chip, :] * inverse
        return inverse * (d - e * table[1, chip, :][:, 0:1])

    rq = back(dl, qs, p, inv_p)
    rp = back(dlt, ps, q, inv_q)
    left = core == 0
    rq = jnp.where(left, rq, pltpu.roll(rq, seqs, 0))
    rp = jnp.where(left, pltpu.roll(rp, seqs, 0), rp)
    raws[t] = jnp.where(first, rq, rp)
    d_copies = []
    for d in (2, 1, 3):
        copy = y_copy(raws.at[t], raws.at[t], d, dsem, drecv)
        copy.start()
        d_copies.append(copy)
    total = None
    for d in (0, 1, 3, 2):
        o = (t - d) % nt
        if d:
            y_copy(raws.at[o], raws.at[o], d, dsem, drecv).wait_recv()
        cols = pl.ds(pl.multiple_of(o * part_w, part_w), part_w)
        part = lax.dot_general(raws[o].astype(bf16), wout[:, cols], NT, preferred_element_type=f32)
        total = part if total is None else total + part
    for s in range(8):
        ups[s] = jnp.broadcast_to(total[s:s + 1], (8, groups * H))

    @pl.loop(0, seqs)
    def _(s):
        attend_backward(rows, att, wts, ups, dgt, pl.multiple_of(s * lq, H), bq, s * uq, s, groups)

    @pl.loop(0, seqs)
    def _(s):
        attend_backward(rows, att, wts, ups, dgt, pl.multiple_of(base_p + s * lp, H), bp,
                        seqs * uq + s * up_, seqs + s, groups)

    for copy in a_copies + c_copies + d_copies:
        copy.wait_send()
    for n, (a, b) in enumerate(AROUND):
        b_copy(n, a, b).wait_send()
        s_copy(n, -a, -b, False).wait_send()
    s_copy(15, 0, 0, False).wait_send()


def middle(rows, means, w_out, neg_owner, neg_slot, lq, lp):
    tokens, cols = rows.shape
    width = w_out.shape[1]
    groups = cols // HEAD_DIM - 2
    n = neg_owner.shape[0]
    bq, bp = lq // HEAD_DIM, lp // HEAD_DIM
    units = 4 * groups * (bq * (bq + 1) // 2 + bp * (bp + 1) // 2)
    ANY, VM = pl.BlockSpec(memory_space=pl.ANY), pl.BlockSpec(memory_space=pltpu.VMEM)
    dma = pltpu.SemaphoreType.DMA
    H = HEAD_DIM
    return pl.pallas_call(
        functools.partial(middle_kernel, lq, lp),
        out_shape=(jax.ShapeDtypeStruct((cols, tokens), bf16), jax.ShapeDtypeStruct((1, 1), f32)),
        in_specs=[VM, VM, ANY, VM, VM],
        out_specs=(VM, VM),
        scratch_shapes=[
            pltpu.VMEM(w_out.shape, bf16),
            pltpu.VMEM((units, H, H), f32),
            pltpu.VMEM((groups, tokens, H), f32),
            pltpu.VMEM((8, 8, groups * H), f32),
            pltpu.VMEM((8, 8, groups * H), f32),
            pltpu.VMEM((4, 8, width // 4), f32),
            pltpu.VMEM((4, 8, width // 4), f32),
            pltpu.VMEM((32, 8, width // 4), f32),
            pltpu.VMEM((n, width // 4), f32),
            pltpu.VMEM((n, width // 4), f32),
            pltpu.VMEM((4, n + 16, n), f32),
            pltpu.VMEM((3, n, n), f32),
            pltpu.VMEM((3, n, n), f32),
            pltpu.VMEM((4, 8, width // 4), f32),
            dma, dma((3,)), dma((3,)), dma((15,)), dma((15,)), dma((16,)), dma((16,)),
            dma((3,)), dma((3,)), dma((3,)), dma((3,)),
        ],
        compiler_params=pltpu.CompilerParams(
            collective_id=2, has_side_effects=True, vmem_limit_bytes=56 * 1024 * 1024),
        cost_estimate=pl.CostEstimate(flops=2 * 10 ** 9, bytes_accessed=10 ** 7, transcendentals=10 ** 6),
        name="contrast_middle",
    )(rows, means, w_out, neg_owner, neg_slot)


def body(
    query_states, passage_states, norm_gain, w_query, w_key, w_value, w_out, neg_owner, neg_slot
):
    owned, query_length, _ = query_states.shape
    passage_length = passage_states.shape[1]
    normed, rows, means = project(
        query_states.reshape(owned * query_length, -1), passage_states.reshape(owned * passage_length, -1),
        norm_gain, w_query, w_key, w_value)
    dgt, loss = middle(rows, means, w_out, neg_owner, neg_slot, query_length, passage_length)
    return (loss[0, 0], *scatter(normed, dgt, w_query.shape[0]))


def solution(mesh):
    in_specs = (
        P("dp", None, None),
        P("dp", None, None),
        P(),
        P("dp", "tensor"),
        P("dp", "tensor"),
        P("dp", "tensor"),
        P("tensor", None),
        P(),
        P(),
    )
    out_specs = (P(), P("dp", "tensor"), P("dp", "tensor"), P("dp", "tensor"))
    return jax.shard_map(body, mesh=mesh, in_specs=in_specs, out_specs=out_specs, check_vma=False)
```

```python
import functools
import math

import jax
import jax.numpy as jnp
from jax import lax
from jax.experimental import pallas as pl
from jax.experimental.pallas import tpu as pltpu
from jax.sharding import PartitionSpec as P

HEAD_DIM = 128
eps_norm = 1e-06
eps_unit = 1e-06
sharpness_divisor = 0.05
MESH = pl.DeviceIdType.MESH
f32, bf16 = jnp.float32, jnp.bfloat16
XS, ZS = 4, 4


def iota(shape, dim):
    return lax.broadcasted_iota(jnp.int32, shape, dim)


def place():
    p = lax.axis_index("dp")
    return p // (2 * ZS), (p // 2) % ZS, p % 2


def slot_of(a, b, core=None, flip=False):
    x, z, c = place()
    c = 1 - c if flip else c
    return ((x + a) % XS * ZS + (z + b) % ZS) * 2 + c


def chip_of(a, b):
    x, z, _ = place()
    return (x + a) % XS * ZS + (z + b) % ZS


def dev(a, b, flip=False):
    return {"dp": slot_of(a, b, flip=flip)}


GATHERED = ((0, 0), (1, 0), (0, 1), (-1, 0), (0, -1), (1, 1), (1, -1), (-1, 1), (-1, -1), (2, 0), (0, 2),
            (2, 1), (1, 2), (2, -1), (-1, 2), (2, 2))


def pick(i, values):
    out = values[0]
    for n, value in enumerate(values[1:], 1):
        out = jnp.where(i == n, value, out)
    return out


class Tree:
    def __init__(self, buf, rows, send_sem, recv_sem):
        self.buf, self.rows, self.send_sem, self.recv_sem = buf, rows, send_sem, recv_sem
        self.sends, self.pieces, self.waited = [], {}, set()

    def view(self, a, b, lo, n):
        return self.buf.at[slot_of(a, b), pl.ds(lo * self.rows, n * self.rows)]

    def copy(self, i):
        a, b, lo, n, dx, dz = self.sends[i]
        view = self.view(a, b, lo, n)
        return pltpu.make_async_remote_copy(
            src_ref=view, dst_ref=view, send_sem=self.send_sem.at[i], recv_sem=self.recv_sem.at[i],
            device_id=dev(dx, dz), device_id_type=MESH)

    def send(self, a, b, lo, n, dx, dz):
        i = len(self.sends)
        self.sends.append((a, b, lo, n, dx, dz))
        self.pieces[((a - dx) % 4, (b - dz) % 4, lo, n)] = i
        self.copy(i).start()

    def wait(self, a, b, lo, n):
        i = self.pieces[(a % 4, b % 4, lo, n)]
        view = self.view(a, b, lo, n)
        pltpu.make_async_remote_copy(
            src_ref=view, dst_ref=view, send_sem=self.send_sem.at[i], recv_sem=self.recv_sem.at[i],
            device_id=dev(1, 0), device_id_type=MESH).wait_recv()
        self.waited.add(i)

    def finish(self):
        assert self.waited == set(range(len(self.sends)))
        for i in range(len(self.sends)):
            self.copy(i).wait_send()


def up(d):
    return 0 if d > 0 else 1


def gather_stages(tree, sibling):
    def first():
        for d in (1, -1):
            tree.send(0, 0, 0, 2, d, 0)
            tree.send(0, 0, 2, 2, 0, d)
        for d in (1, -1):
            tree.send(0, 0, 2, 2, d, 0)
            tree.send(0, 0, 0, 2, 0, d)
        sibling(0, 0)

    def second():
        for s in (1, -1):
            tree.wait(s, 0, 0, 2)
            tree.send(s, 0, up(-s), 1, -s, 0)
            tree.wait(0, s, 2, 2)
            tree.send(0, s, 2 + up(-s), 1, 0, -s)
        for s in (1, -1):
            for d in (1, -1):
                tree.send(s, 0, 0, 2, 0, d)
                tree.send(0, s, 2, 2, d, 0)

    def third():
        for s in (1, -1):
            tree.wait(s, 0, 2, 2)
            tree.send(s, 0, 2 + up(-s), 1, -s, 0)
            tree.wait(0, s, 0, 2)
            tree.send(0, s, up(-s), 1, 0, -s)
        for s in (1, -1):
            sibling(s, 0)
            sibling(0, s)

    def fourth():
        for q in (0, 1):
            tree.wait(2, 0, q, 1)
            tree.wait(0, 2, 2 + q, 1)
        for d in (1, -1):
            tree.send(2, 0, 0, 2, 0, d)
            tree.send(0, 2, 2, 2, d, 0)

    def fifth():
        for sx in (1, -1):
            for sz in (1, -1):
                tree.wait(sx, sz, 0, 2)
                tree.send(sx, sz, up(-sz), 1, 0, -sz)
                tree.wait(sx, sz, 2, 2)
                tree.send(sx, sz, 2 + up(-sx), 1, -sx, 0)
                sibling(sx, sz)

    def sixth():
        for q in (0, 1):
            tree.wait(2, 0, 2 + q, 1)
            tree.wait(0, 2, q, 1)
        sibling(2, 0)
        sibling(0, 2)
        for s in (1, -1):
            tree.wait(2, s, 0, 2)
            tree.send(2, s, up(-s), 1, 0, -s)
            tree.wait(s, 2, 2, 2)
            tree.send(s, 2, 2 + up(-s), 1, -s, 0)

    def seventh():
        for s in (1, -1):
            for q in (0, 1):
                tree.wait(2, s, 2 + q, 1)
                tree.wait(s, 2, q, 1)
            sibling(2, s)
            sibling(s, 2)

    def eighth():
        for q in (0, 1, 2, 3):
            tree.wait(2, 2, q, 1)
        sibling(2, 2)

    return first, second, third, fourth, fifth, sixth, seventh, eighth


def meet(others):
    barrier = pltpu.get_barrier_semaphore()
    for other in others:
        pl.semaphore_signal(barrier, inc=1, device_id=other, device_id_type=MESH)
    pl.semaphore_wait(barrier, len(others))


def project_kernel(xq, xp, gain, wq, wk, wv, rows_out, scale_out, mean_out,
                   W, held, X, acc, macc, wsem, xsem, ssem, rsem, sibs, sibr):
    lq, lp = xq.shape[0] // 4, xp.shape[0] // 4
    tq, tokens = xq.shape[0], X.shape[0]
    width = X.shape[1]
    depth = W.shape[1]
    T = 128
    mine = slot_of(0, 0)
    loads = []
    lo = 0
    for n, w in enumerate((wq, wk, wv)):
        loads.append(pltpu.make_async_copy(w, held.at[:, pl.ds(lo, w.shape[1])], wsem.at[n]))
        lo += w.shape[1]
    for load in loads:
        load.start()
    xloads = []
    for i in range(tokens // T):
        src = xq.at[pl.ds(i * T, T)] if i * T < tq else xp.at[pl.ds(i * T - tq, T)]
        xloads.append(pltpu.make_async_copy(src, X.at[pl.ds(i * T, T)], xsem.at[i]))
    for load in xloads:
        load.start()
    macc[...] = jnp.zeros_like(macc)
    acc[...] = jnp.zeros_like(acc)
    eye = iota((depth, depth), 0) == iota((depth, depth), 1)
    own = gain[:, pl.ds(pl.multiple_of(mine * depth, depth), depth)]
    column = jnp.sum(jnp.where(eye, own, 0.0), axis=1, keepdims=True)
    for load in loads:
        load.wait()
    W[mine] = (held[...].astype(f32) * column).astype(bf16)
    meet([dev(1, 0), dev(-1, 0), dev(0, 1), dev(0, -1), dev(0, 0, flip=True)])

    tree = Tree(W, depth // 4, ssem, rsem)
    sib_sent = []

    def sib_copy(i, a, b, flip):
        view = W.at[slot_of(a, b, flip=flip)]
        return pltpu.make_async_remote_copy(
            src_ref=view, dst_ref=view, send_sem=sibs.at[i], recv_sem=sibr.at[i],
            device_id=dev(0, 0, flip=True), device_id_type=MESH)

    def sibling(a, b):
        sib_copy(len(sib_sent), a, b, False).start()
        sib_sent.append((a % 4, b % 4))

    stages = gather_stages(tree, sibling)
    C = 128
    chunks = width // C
    n_tiles = tokens // T
    n_query = tq // T
    stages[0]()

    @pl.loop(0, n_tiles)
    def _(i):
        pltpu.make_async_copy(xq.at[pl.ds(0, T)], X.at[pl.ds(pl.multiple_of(i * T, T), T)], xsem.at[i]).wait()
        per = lp // T
        seq = jnp.where(i < n_query, i // (lq // T), 4 + (i - n_query) // per)

        def step(n, sums):
            r = pl.ds(pl.multiple_of(i * T + n * 16, 16), 16)
            squares, later = [None] * 4, []
            for c in range(chunks):
                v = X[r, c * C:(c + 1) * C].astype(f32)
                w = v * v
                squares[c % 4] = w if squares[c % 4] is None else squares[c % 4] + w
                later.append(sums[c] + (v[0:8] + v[8:16]))
            scale_out[r, :] = (squares[0] + squares[1]) + (squares[2] + squares[3])
            return tuple(later)

        sums = lax.fori_loop(0, T // 16, step, tuple(
            macc[seq, :, c * C:(c + 1) * C] for c in range(chunks)))
        for c in range(chunks):
            macc[seq, :, c * C:(c + 1) * C] = sums[c]
        for at, stage in ((7, 1), (11, 2)):
            @pl.when(i == at)
            def _():
                stages[stage]()

    order = GATHERED

    @pl.loop(0, len(order))
    def _(i):
        a, b = pick(i, [o[0] % 4 for o in order]), pick(i, [o[1] % 4 for o in order])
        sib_copy(i, a, b, True).wait_recv()
        chip = chip_of(a, b)
        cols = pl.ds(pl.multiple_of(chip * 2 * depth, 2 * depth), 2 * depth)
        w = W[pl.ds(chip * 2, 2)].reshape(2 * depth, W.shape[2])
        total = jnp.dot(X[:, cols], w, preferred_element_type=f32)
        acc[...] = acc[...] + total
        for at, stage in ((0, 3), (4, 4), (6, 5), (8, 6), (11, 7)):
            @pl.when(i == at)
            def _():
                stages[stage]()

    assert sib_sent == [(a % 4, b % 4) for a, b in order]

    @pl.loop(0, n_tiles)
    def _(i):
        tile = pl.ds(pl.multiple_of(i * T, T), T)
        total = jnp.sum(scale_out[tile, :], axis=1, keepdims=True)
        scale = lax.rsqrt(total * (1.0 / width) + eps_norm)
        scale_out[tile, :] = jnp.broadcast_to(scale, (T, C))
        rows_out[tile, :] = (acc[tile, :] * scale).astype(bf16)

    for s in range(8):
        mean_out[s:s + 1, :] = jnp.sum(macc[s], axis=0, keepdims=True) * (1.0 / (lq if s < 4 else lp))
    tree.finish()
    for i, (a, b) in enumerate(sib_sent):
        sib_copy(i, a, b, False).wait_send()


def project(xq, xp, gain, wq, wk, wv):
    tokens, width = xq.shape[0] + xp.shape[0], xq.shape[1]
    cols = wq.shape[1] + wk.shape[1] + wv.shape[1]
    rows = wq.shape[0]
    ANY, VM = pl.BlockSpec(memory_space=pl.ANY), pl.BlockSpec(memory_space=pltpu.VMEM)
    dma = pltpu.SemaphoreType.DMA
    return pl.pallas_call(
        project_kernel,
        out_shape=(
            jax.ShapeDtypeStruct((tokens, cols), bf16),
            jax.ShapeDtypeStruct((tokens, 128), f32),
            jax.ShapeDtypeStruct((8, width), f32),
        ),
        in_specs=[ANY, ANY, VM, ANY, ANY, ANY],
        out_specs=(VM, VM, VM),
        scratch_shapes=[
            pltpu.VMEM((32, rows, cols), bf16),
            pltpu.VMEM((rows, cols), bf16),
            pltpu.VMEM((tokens, width), bf16),
            pltpu.VMEM((tokens, cols), f32),
            pltpu.VMEM((8, 8, width), f32),
            dma((3,)), dma((tokens // 128,)),
            dma((40,)), dma((40,)), dma((16,)), dma((16,)),
        ],
        compiler_params=pltpu.CompilerParams(
            collective_id=0, has_side_effects=True, vmem_limit_bytes=62 * 1024 * 1024),
        cost_estimate=pl.CostEstimate(flops=2 * tokens * width * cols, bytes_accessed=2 * tokens * width,
                                      transcendentals=0),
        name="gather_project",
    )(xq, xp, gain.reshape(1, -1), wq, wk, wv)


ORDER = ((2, 2), (2, 1), (2, -1), (1, 2), (-1, 2), (2, 0), (0, 2), (1, 1), (1, -1), (-1, 1), (-1, -1),
         (1, 0), (-1, 0), (0, 1), (0, -1), (0, 0))


def key_of(a, b):
    return a % 4, b % 4


class Fold:
    def __init__(self, part, landed, send_sem, recv_sem):
        self.part, self.landed, self.send_sem, self.recv_sem = part, landed, send_sem, recv_sem
        self.sends, self.pieces, self.used, self.waited = [], {}, 0, set()
        self.index = {key_of(a, b): i for i, (a, b) in enumerate(ORDER)}

    def copy(self, i):
        a, b, lo, n, dx, dz, off = self.sends[i]
        return pltpu.make_async_remote_copy(
            src_ref=self.part.at[self.index[key_of(a, b)], pl.ds(lo, n)], dst_ref=self.landed.at[pl.ds(off, n)],
            send_sem=self.send_sem.at[i], recv_sem=self.recv_sem.at[i],
            device_id=dev(dx, dz), device_id_type=MESH)

    def send(self, a, b, lo, n, dx, dz):
        i = len(self.sends)
        self.sends.append((a, b, lo, n, dx, dz, self.used))
        self.used += n
        self.pieces[(*key_of(a - dx, b - dz), lo, n, *key_of(-dx, -dz))] = i
        self.copy(i).start()

    def recv(self, a, b, lo, n, dx, dz):
        i = self.pieces[(*key_of(a, b), lo, n, *key_of(dx, dz))]
        self.copy(i).wait_recv()
        self.waited.add(i)
        off = self.sends[i][6]
        return self.landed.at[pl.ds(off, n)]

    def add(self, a, b, lo, n, *froms):
        at = self.index[key_of(a, b)]
        for m, (dx, dz) in froms:
            piece = self.recv(a, b, m[0], m[1], dx, dz)
            cut = piece.shape[1] // 2

            @pl.loop(0, 2 * m[1])
            def _(n):
                q, rows = n // 2, pl.ds(pl.multiple_of(n % 2 * cut, cut), cut)
                self.part[at, m[0] + q, rows, :] = self.part[at, m[0] + q, rows, :] + piece[q, rows, :]

    def finish(self):
        assert self.waited == set(range(len(self.sends))), (len(self.waited), len(self.sends))
        for i in range(len(self.sends)):
            self.copy(i).wait_send()


def ends(fold, a, b, half):
    if half == 0:
        fold.send(a, b, 0, 1, 0, -1)
        fold.send(a, b, 1, 1, 0, 1)
    else:
        fold.send(a, b, 2, 1, -1, 0)
        fold.send(a, b, 3, 1, 1, 0)


def fold_steps(fold):
    def first(i):
        a, b = ORDER[i]
        if (a, b) == (2, 2):
            ends(fold, a, b, 0)
            ends(fold, a, b, 1)
        elif a == 2:
            ends(fold, a, b, 1)
        elif b == 2:
            ends(fold, a, b, 0)
        elif a and b:
            q = up(-b)
            fold.add(a, b, 0, 2, ((q, 1), (0, -b)))
            fold.send(a, b, 0, 2, 0, b)
            q = 2 + up(-a)
            fold.add(a, b, 2, 2, ((q, 1), (-a, 0)))
            fold.send(a, b, 2, 2, a, 0)

    def second():
        for s in (1, -1):
            fold.add(2, s, 0, 2, ((up(-s), 1), (0, -s)))
            fold.send(2, s, 0, 2, 0, s)
            fold.add(s, 2, 2, 2, ((2 + up(-s), 1), (-s, 0)))
            fold.send(s, 2, 2, 2, s, 0)

    def third():
        fold.add(2, 0, 0, 2, ((0, 2), (0, 1)), ((0, 2), (0, -1)))
        fold.send(2, 0, 0, 1, -1, 0)
        fold.send(2, 0, 1, 1, 1, 0)
        fold.add(0, 2, 2, 2, ((2, 2), (1, 0)), ((2, 2), (-1, 0)))
        fold.send(0, 2, 2, 1, 0, -1)
        fold.send(0, 2, 3, 1, 0, 1)

    def fourth():
        for s in (1, -1):
            fold.add(s, 0, 2, 2, ((2 + up(-s), 1), (-s, 0)))
            fold.send(s, 0, 2, 2, s, 0)
            fold.add(0, s, 0, 2, ((up(-s), 1), (0, -s)))
            fold.send(0, s, 0, 2, 0, s)

    def fifth():
        for s in (1, -1):
            fold.add(s, 0, 0, 2, ((0, 2), (0, 1)), ((0, 2), (0, -1)), ((up(-s), 1), (-s, 0)))
            fold.send(s, 0, 0, 2, s, 0)
            fold.add(0, s, 2, 2, ((2, 2), (1, 0)), ((2, 2), (-1, 0)), ((2 + up(-s), 1), (0, -s)))
            fold.send(0, s, 2, 2, 0, s)

    steps = {i: [functools.partial(first, i)] for i in range(11)}
    steps[6].append(second)
    steps[11] = [third]
    steps[14] = [fourth]
    steps[15] = [fifth]
    return steps


def scatter_kernel(xq, xp, dgt, out, X, part, both, sib, landed, xsem, ssem, rsem, sibs, sibr):
    depth = 2 * out.shape[1]
    tq, tp = xq.shape[0], xp.shape[0]
    rows = dgt.shape[0]
    qr = part.shape[2]
    loads = []
    for i, (a, b) in enumerate(ORDER):
        cols = pl.ds(pl.multiple_of(chip_of(a, b) * depth, depth), depth)
        loads.append((
            pltpu.make_async_copy(xq.at[:, cols], X.at[i, pl.ds(0, tq)], xsem.at[i]),
            pltpu.make_async_copy(xp.at[:, cols], X.at[i, pl.ds(tq, tp)], xsem.at[16 + i])))
    for pair in loads:
        for load in pair:
            load.start()
    meet([dev(1, 0), dev(-1, 0), dev(0, 1), dev(0, -1), dev(0, 0, flip=True)])
    half = depth // 2
    core = place()[2]
    own = pl.ds(pl.multiple_of(core * half, half), half)
    other = pl.ds(pl.multiple_of((1 - core) * half, half), half)

    def sib_copy(i):
        return pltpu.make_async_remote_copy(
            src_ref=both.at[i, :, :, other], dst_ref=sib.at[i], send_sem=sibs.at[i], recv_sem=sibr.at[i],
            device_id=dev(0, 0, flip=True), device_id_type=MESH)

    fold = Fold(part, landed, ssem, rsem)
    steps = fold_steps(fold)

    @pl.loop(0, 17)
    def _(i):
        @pl.when(i < 16)
        def _():
            pltpu.make_async_copy(xq.at[:, pl.ds(0, depth)], X.at[i, pl.ds(0, tq)], xsem.at[i]).wait()
            pltpu.make_async_copy(xp.at[:, pl.ds(0, depth)], X.at[i, pl.ds(tq, tp)], xsem.at[16 + i]).wait()
            total = jnp.dot(dgt[...], X[i], preferred_element_type=f32).astype(bf16)
            both[i] = total.reshape(4, qr, depth)
            sib_copy(i).start()

        @pl.when(i > 0)
        def _():
            sib_copy(i - 1).wait_recv()

            @pl.loop(0, 4)
            def _(n):
                part[i - 1, n] = both[i - 1, n, :, own] + sib[i - 1, n]

        for at in sorted(steps):
            @pl.when(i == at + 1)
            def _():
                for step in steps[at]:
                    step()

    for side in (0, 1):
        total = part[15, pl.ds(2 * side, 2)].astype(f32)
        for dx, dz in ((1, 0), (-1, 0), (0, 1), (0, -1)):
            total = total + fold.recv(0, 0, 2 * side, 2, dx, dz)[...].astype(f32)
        out[pl.ds(side * 2 * qr, 2 * qr), :] = total.reshape(2 * qr, half)
    fold.finish()
    for i in range(16):
        sib_copy(i).wait_send()


def scatter(xq, xp, dgt, depth):
    tokens, width = xq.shape[0] + xp.shape[0], xq.shape[1]
    rows = dgt.shape[0]
    ANY, VM = pl.BlockSpec(memory_space=pl.ANY), pl.BlockSpec(memory_space=pltpu.VMEM)
    dma = pltpu.SemaphoreType.DMA
    return pl.pallas_call(
        scatter_kernel,
        out_shape=jax.ShapeDtypeStruct((rows, depth), f32),
        in_specs=[ANY, ANY, VM],
        out_specs=VM,
        scratch_shapes=[
            pltpu.VMEM((16, tokens, 2 * depth), bf16),
            pltpu.VMEM((16, 4, rows // 4, depth), bf16),
            pltpu.VMEM((16, 4, rows // 4, 2 * depth), bf16),
            pltpu.VMEM((16, 4, rows // 4, depth), bf16),
            pltpu.VMEM((60, rows // 4, depth), bf16),
            dma((32,)), dma((40,)), dma((40,)), dma((16,)), dma((16,)),
        ],
        compiler_params=pltpu.CompilerParams(
            collective_id=1, has_side_effects=True, vmem_limit_bytes=62 * 1024 * 1024),
        cost_estimate=pl.CostEstimate(flops=2 * tokens * width * rows, bytes_accessed=2 * tokens * width,
                                      transcendentals=0),
        name="grad_scatter",
    )(xq, xp, dgt)


def finish_kernel(sums, gain, gq, gk, gv):
    H = HEAD_DIM
    depth = sums.shape[1]
    own = gain[:, pl.ds(pl.multiple_of(slot_of(0, 0) * depth, depth), depth)]
    heads = gq.shape[1] // H
    for n in range(heads + 2):
        block = (sums[n * H:(n + 1) * H, :] * own).T
        if n < heads:
            gq[:, n * H:(n + 1) * H] = block
        elif n == heads:
            gk[...] = block
        else:
            gv[...] = block


def finish(sums, gain):
    rows, depth = sums.shape
    cols = (rows - 2 * HEAD_DIM, HEAD_DIM, HEAD_DIM)
    VM = pl.BlockSpec(memory_space=pltpu.VMEM)
    return pl.pallas_call(
        finish_kernel,
        out_shape=tuple(jax.ShapeDtypeStruct((depth, n), f32) for n in cols),
        in_specs=[VM, VM],
        out_specs=(VM, VM, VM),
        name="finish_rows",
    )(sums, gain.reshape(1, -1))


NT = (((1,), (1,)), ((), ()))
NN = (((1,), (0,)), ((), ()))
EXACT = lax.Precision.HIGHEST
AROUND = tuple((a, b) for a in (1, 3, 0, 2) for b in (1, 3, 0, 2) if (a, b) != (0, 0))


def units_of(s, is_passage, blocks):
    return (blocks * (blocks + 1) // 2) * s


def attend_forward(rows, att, wts, pooled, base, blocks, unit, seq, groups):
    H = HEAD_DIM
    key_at, value_at = groups * H, (groups + 1) * H
    L = blocks * H
    k = rows[pl.ds(base, L), key_at:key_at + H]
    v = rows[pl.ds(base, L), value_at:value_at + H].astype(f32)
    causal = iota((H, H), 0) <= iota((H, H), 1)
    n = 0
    for h in range(groups):
        w = [None] * blocks
        for ib in range(blocks):
            q = rows[pl.ds(pl.multiple_of(base + ib * H, H), H), h * H:(h + 1) * H]
            e = []
            for jb in range(ib + 1):
                st = lax.dot_general(k[jb * H:(jb + 1) * H], q, NT, preferred_element_type=f32)
                st = jnp.exp(st * (1.0 / math.sqrt(H)))
                e.append(jnp.where(causal, st, 0.0) if jb == ib else st)
            total = jnp.sum(e[0], axis=0, keepdims=True)
            for one in e[1:]:
                total = total + jnp.sum(one, axis=0, keepdims=True)
            r = 1.0 / total
            for jb in range(ib + 1):
                at = e[jb] * r
                att[unit + n] = at
                n += 1
                w[jb] = at if w[jb] is None else w[jb] + at
        out = None
        for jb in range(blocks):
            col = jnp.sum(w[jb], axis=1, keepdims=True) * (1.0 / L)
            wts[h, pl.ds(pl.multiple_of(base + jb * H, H), H), :] = jnp.broadcast_to(col, (H, H))
            part = jnp.sum(col * v[jb * H:(jb + 1) * H], axis=0, keepdims=True)
            out = part if out is None else out + part
        pooled[seq, :, h * H:(h + 1) * H] = jnp.broadcast_to(out, (8, H))


def attend_backward(rows, scale, att, wts, ups, dgt, base, blocks, unit, seq, groups):
    H = HEAD_DIM
    key_at, value_at = groups * H, (groups + 1) * H
    L = blocks * H
    k = rows[pl.ds(base, L), key_at:key_at + H]
    v = rows[pl.ds(base, L), value_at:value_at + H].astype(f32)
    kt = k.astype(f32).T.astype(bf16)
    dk, dv = [None] * blocks, [None] * blocks
    eye = iota((H, H), 0) == iota((H, H), 1)
    along = []
    for jb in range(blocks):
        column = scale[pl.ds(pl.multiple_of(base + jb * H, H), H), 0:1]
        along.append(jnp.sum(jnp.where(eye, column, 0.0), axis=0, keepdims=True))
    n = 0
    for h in range(groups):
        u = ups[seq, :, h * H:(h + 1) * H][0:1]
        c = [jnp.sum(v[jb * H:(jb + 1) * H] * u, axis=1, keepdims=True) * (1.0 / L) for jb in range(blocks)]
        for ib in range(blocks):
            span = pl.ds(pl.multiple_of(base + ib * H, H), H)
            q = rows[span, h * H:(h + 1) * H]
            at = [att[unit + n + jb] for jb in range(ib + 1)]
            n += ib + 1
            m = None
            for jb in range(ib + 1):
                part = jnp.sum(at[jb] * c[jb], axis=0, keepdims=True)
                m = part if m is None else m + part
            dq = None
            for jb in range(ib + 1):
                ds = (at[jb] * ((c[jb] - m) * (1.0 / math.sqrt(H)))).astype(bf16)
                part = jnp.dot(kt[:, jb * H:(jb + 1) * H], ds, preferred_element_type=f32)
                dq = part if dq is None else dq + part
                part = jnp.dot(ds, q, preferred_element_type=f32)
                dk[jb] = part if dk[jb] is None else dk[jb] + part
            dgt[h * H:(h + 1) * H, span] = (dq * along[ib]).astype(bf16)
        for jb in range(blocks):
            part = wts[h, pl.ds(pl.multiple_of(base + jb * H, H), H), :] * u
            dv[jb] = part if dv[jb] is None else dv[jb] + part
    for jb in range(blocks):
        span = pl.ds(pl.multiple_of(base + jb * H, H), H)
        dgt[key_at:key_at + H, span] = (dk[jb].T * along[jb]).astype(bf16)
        dgt[value_at:value_at + H, span] = (dv[jb].T * along[jb]).astype(bf16)


def middle_kernel(lq, lp, rows, scale, means, wout_hbm, owner, place_in, dgt, loss,
                  wout, att, wts, pooled, ups, terms, got, embeds, qs, ps, gram, dl, dlt, raws,
                  wsem, asem, arecv, bsem, brecv, sibs, sibr, csem, crecv, dsem, drecv):
    H = HEAD_DIM
    groups = rows.shape[1] // H - 2
    width = wout.shape[1]
    seqs = 4
    nt = 4
    part_w = width // nt
    load = pltpu.make_async_copy(wout_hbm, wout, wsem)
    load.start()
    x, z, core = place()
    t = lax.axis_index("tensor")
    meet([{"tensor": (t + d) % nt} for d in (1, 2, 3)] + [dev(a, b) for a, b in AROUND] + [dev(0, 0, flip=True)])
    base_p = seqs * lq
    bq, bp = lq // H, lp // H
    uq, up_ = groups * bq * (bq + 1) // 2, groups * bp * (bp + 1) // 2

    @pl.loop(0, seqs)
    def _(s):
        attend_forward(rows, att, wts, pooled, pl.multiple_of(s * lq, H), bq, s * uq, s, groups)

    @pl.loop(0, seqs)
    def _(s):
        attend_forward(rows, att, wts, pooled, pl.multiple_of(base_p + s * lp, H), bp,
                       seqs * uq + s * up_, seqs + s, groups)

    load.wait()
    row = iota((8, groups * H), 0)
    low = pooled[0]
    for s in range(1, 8):
        low = jnp.where(row == s, pooled[s], low)
    low = low.astype(bf16)

    def y_copy(src, dst, d, send_sem, recv_sem):
        return pltpu.make_async_remote_copy(
            src_ref=src, dst_ref=dst, send_sem=send_sem.at[d - 1], recv_sem=recv_sem.at[d - 1],
            device_id={"tensor": (t + d) % nt}, device_id_type=MESH)

    def term(o):
        cols = pl.ds(pl.multiple_of(o * part_w, part_w), part_w)
        return jnp.dot(low, wout[:, cols], preferred_element_type=f32)

    a_copies = []
    for d in (2, 1, 3):
        terms[d] = term((t + d) % nt)
        copy = y_copy(terms.at[d], got.at[d], d, asem, arecv)
        copy.start()
        a_copies.append(copy)
    mine = term(t) + means[:, pl.ds(pl.multiple_of(t * part_w, part_w), part_w)]
    n_rows = qs.shape[0]
    ids = owner[...] * seqs + place_in[...]
    col = iota((n_rows, n_rows), 1)
    counts = jnp.zeros((n_rows, n_rows), f32)
    for j in range(ids.shape[0]):
        counts = counts + jnp.where(ids[j:j + 1, :] == iota((n_rows, n_rows), 0), 1.0, 0.0)
    counts = counts.T
    for copy in a_copies:
        copy.wait_recv()
    mine = mine + got[1] + got[2] + got[3]
    here = slot_of(0, 0)
    embeds[here] = mine

    def b_copy(n, a, b):
        view = embeds.at[here]
        return pltpu.make_async_remote_copy(
            src_ref=view, dst_ref=view, send_sem=bsem.at[n], recv_sem=brecv.at[n],
            device_id=dev(a, b), device_id_type=MESH)

    def s_copy(n, a, b, flip):
        view = embeds.at[slot_of(a, b, flip=flip)]
        return pltpu.make_async_remote_copy(
            src_ref=view, dst_ref=view, send_sem=sibs.at[n], recv_sem=sibr.at[n],
            device_id=dev(0, 0, flip=True), device_id_type=MESH)

    for n, (a, b) in enumerate(AROUND):
        b_copy(n, a, b).start()
    s_copy(15, 0, 0, False).start()
    for n, (a, b) in enumerate(AROUND):
        view = embeds.at[slot_of(-a, -b)]
        pltpu.make_async_remote_copy(
            src_ref=view, dst_ref=view, send_sem=bsem.at[n], recv_sem=brecv.at[n],
            device_id=dev(a, b), device_id_type=MESH).wait_recv()
        s_copy(n, -a, -b, False).start()
    s_copy(15, 0, 0, True).wait_recv()
    for n, (a, b) in enumerate(AROUND):
        s_copy(n, -a, -b, True).wait_recv()

    first = iota((8, part_w), 0) < seqs

    @pl.loop(0, n_rows // 8)
    def _(k):
        one, two = embeds[2 * k], embeds[2 * k + 1]
        span = pl.ds(pl.multiple_of(k * 8, 8), 8)
        qs[span, :] = jnp.where(first, one, pltpu.roll(two, seqs, 0))
        ps[span, :] = jnp.where(first, pltpu.roll(one, seqs, 0), two)

    q, p = qs[...], ps[...]
    gram[0, pl.ds(0, n_rows), :] = lax.dot_general(q, p, NT, precision=EXACT, preferred_element_type=f32)
    ones = jnp.ones((8, part_w), f32)
    gram[0, pl.ds(n_rows, 8), :] = lax.dot_general(ones, q * q, NT, precision=EXACT, preferred_element_type=f32)
    gram[0, pl.ds(n_rows + 8, 8), :] = lax.dot_general(ones, p * p, NT, precision=EXACT, preferred_element_type=f32)
    c_copies = []
    for d in (2, 1, 3):
        copy = y_copy(gram.at[0], gram.at[d], d, csem, crecv)
        copy.start()
        c_copies.append(copy)
    for copy in c_copies:
        copy.wait_recv()
    whole = (gram[0] + gram[2]) + (gram[1] + gram[3])
    eye = iota((n_rows, n_rows), 0) == col
    inv = lax.rsqrt(whole[n_rows:] + eps_unit)
    inv_q_row, inv_p_row = inv[0:1], inv[8:9]
    inv_q = jnp.sum(jnp.where(eye, inv_q_row, 0.0), axis=1, keepdims=True)
    inv_p = jnp.sum(jnp.where(eye, inv_p_row, 0.0), axis=1, keepdims=True)
    cosine = whole[:n_rows] * inv_q * inv_p_row
    logits = cosine * (1.0 / sharpness_divisor)
    raised = jnp.exp(logits) * (1.0 + counts)
    sums = jnp.sum(raised, axis=1, keepdims=True)
    diagonal = jnp.sum(jnp.where(eye, logits, 0.0), axis=1, keepdims=True)
    loss[...] = jnp.sum(jnp.log(sums) - diagonal, axis=0, keepdims=True) * (1.0 / n_rows)
    slope = (raised / sums - jnp.where(eye, 1.0, 0.0)) * (1.0 / sharpness_divisor)
    dl[0] = slope
    dlt[0] = slope.T
    weighted = slope * cosine
    dl[1] = jnp.broadcast_to(jnp.sum(weighted, axis=1, keepdims=True), (n_rows, n_rows))
    dlt[1] = jnp.broadcast_to(jnp.sum(weighted, axis=0, keepdims=True), (n_rows, n_rows)).T
    dl[2] = jnp.broadcast_to(inv_q, (n_rows, n_rows))
    dlt[2] = jnp.broadcast_to(inv_p, (n_rows, n_rows))
    chip = pl.ds(pl.multiple_of(chip_of(0, 0) * 8, 8), 8)

    def back(table, own, others, scale):
        d = jnp.dot(table[0, chip, :], others * scale, precision=EXACT, preferred_element_type=f32)
        inverse = table[2, chip, :][:, 0:1]
        e = own[chip, :] * inverse
        return inverse * (d - e * table[1, chip, :][:, 0:1])

    rq = back(dl, qs, p, inv_p)
    rp = back(dlt, ps, q, inv_q)
    left = core == 0
    rq = jnp.where(left, rq, pltpu.roll(rq, seqs, 0))
    rp = jnp.where(left, pltpu.roll(rp, seqs, 0), rp)
    raws[t] = jnp.where(first, rq, rp)
    d_copies = []
    for d in (2, 1, 3):
        copy = y_copy(raws.at[t], raws.at[t], d, dsem, drecv)
        copy.start()
        d_copies.append(copy)
    total = None
    for d in (0, 1, 3, 2):
        o = (t - d) % nt
        if d:
            y_copy(raws.at[o], raws.at[o], d, dsem, drecv).wait_recv()
        cols = pl.ds(pl.multiple_of(o * part_w, part_w), part_w)
        part = lax.dot_general(raws[o].astype(bf16), wout[:, cols], NT, preferred_element_type=f32)
        total = part if total is None else total + part
    for s in range(8):
        ups[s] = jnp.broadcast_to(total[s:s + 1], (8, groups * H))

    @pl.loop(0, seqs)
    def _(s):
        attend_backward(rows, scale, att, wts, ups, dgt, pl.multiple_of(s * lq, H), bq, s * uq, s, groups)

    @pl.loop(0, seqs)
    def _(s):
        attend_backward(rows, scale, att, wts, ups, dgt, pl.multiple_of(base_p + s * lp, H), bp,
                        seqs * uq + s * up_, seqs + s, groups)

    for copy in a_copies + c_copies + d_copies:
        copy.wait_send()
    for n, (a, b) in enumerate(AROUND):
        b_copy(n, a, b).wait_send()
        s_copy(n, -a, -b, False).wait_send()
    s_copy(15, 0, 0, False).wait_send()


def middle(rows, scale, means, w_out, neg_owner, neg_slot, lq, lp):
    tokens, cols = rows.shape
    width = w_out.shape[1]
    groups = cols // HEAD_DIM - 2
    n = neg_owner.shape[1]
    bq, bp = lq // HEAD_DIM, lp // HEAD_DIM
    units = 4 * groups * (bq * (bq + 1) // 2 + bp * (bp + 1) // 2)
    ANY, VM = pl.BlockSpec(memory_space=pl.ANY), pl.BlockSpec(memory_space=pltpu.VMEM)
    dma = pltpu.SemaphoreType.DMA
    H = HEAD_DIM
    return pl.pallas_call(
        functools.partial(middle_kernel, lq, lp),
        out_shape=(jax.ShapeDtypeStruct((cols, tokens), bf16), jax.ShapeDtypeStruct((1, 1), f32)),
        in_specs=[VM, VM, VM, ANY, VM, VM],
        out_specs=(VM, VM),
        scratch_shapes=[
            pltpu.VMEM(w_out.shape, bf16),
            pltpu.VMEM((units, H, H), f32),
            pltpu.VMEM((groups, tokens, H), f32),
            pltpu.VMEM((8, 8, groups * H), f32),
            pltpu.VMEM((8, 8, groups * H), f32),
            pltpu.VMEM((4, 8, width // 4), f32),
            pltpu.VMEM((4, 8, width // 4), f32),
            pltpu.VMEM((32, 8, width // 4), f32),
            pltpu.VMEM((n, width // 4), f32),
            pltpu.VMEM((n, width // 4), f32),
            pltpu.VMEM((4, n + 16, n), f32),
            pltpu.VMEM((3, n, n), f32),
            pltpu.VMEM((3, n, n), f32),
            pltpu.VMEM((4, 8, width // 4), f32),
            dma, dma((3,)), dma((3,)), dma((15,)), dma((15,)), dma((16,)), dma((16,)),
            dma((3,)), dma((3,)), dma((3,)), dma((3,)),
        ],
        compiler_params=pltpu.CompilerParams(
            collective_id=2, has_side_effects=True, vmem_limit_bytes=62 * 1024 * 1024),
        cost_estimate=pl.CostEstimate(flops=2 * 10 ** 9, bytes_accessed=10 ** 7, transcendentals=10 ** 6),
        name="contrast_middle",
    )(rows, scale, means, w_out, neg_owner, neg_slot)


def body(
    query_states, passage_states, norm_gain, w_query, w_key, w_value, w_out, neg_owner, neg_slot
):
    owned, query_length, _ = query_states.shape
    passage_length = passage_states.shape[1]
    xq = query_states.reshape(owned * query_length, -1)
    xp = passage_states.reshape(owned * passage_length, -1)
    rows, scale, means = project(xq, xp, norm_gain, w_query, w_key, w_value)
    dgt, loss = middle(rows, scale, means, w_out, neg_owner.T, neg_slot.T, query_length, passage_length)
    return (loss[0, 0], *finish(scatter(xq, xp, dgt, w_query.shape[0]), norm_gain))


def solution(mesh):
    in_specs = (
        P("dp", None, None),
        P("dp", None, None),
        P(),
        P("dp", "tensor"),
        P("dp", "tensor"),
        P("dp", "tensor"),
        P("tensor", None),
        P(),
        P(),
    )
    out_specs = (P(), P("dp", "tensor"), P("dp", "tensor"), P("dp", "tensor"))
    return jax.shard_map(body, mesh=mesh, in_specs=in_specs, out_specs=out_specs, check_vma=False)
```

```python
import functools
import math
import types

import jax
import jax.numpy as jnp
from jax import lax
from jax.experimental import pallas as pl
from jax.experimental.pallas import tpu as pltpu
from jax.sharding import PartitionSpec as P

HEAD_DIM = 128
eps_norm = 1e-06
eps_unit = 1e-06
sharpness_divisor = 0.05
MESH = pl.DeviceIdType.MESH
f32, bf16 = jnp.float32, jnp.bfloat16
XS, ZS = 4, 4
VMEM_LIMIT = 63 * 1024 * 1024


def iota(shape, dim):
    return lax.broadcasted_iota(jnp.int32, shape, dim)


def place():
    p = lax.axis_index("dp")
    return p // (2 * ZS), (p // 2) % ZS, p % 2


def slot_of(a, b, core=None, flip=False):
    x, z, c = place()
    c = 1 - c if flip else c
    return ((x + a) % XS * ZS + (z + b) % ZS) * 2 + c


def chip_of(a, b):
    x, z, _ = place()
    return (x + a) % XS * ZS + (z + b) % ZS


def dev(a, b, flip=False):
    return {"dp": slot_of(a, b, flip=flip)}


GATHERED = ((0, 0), (1, 0), (0, 1), (-1, 0), (0, -1), (1, 1), (1, -1), (-1, 1), (-1, -1), (2, 0), (0, 2),
            (2, 1), (1, 2), (2, -1), (-1, 2), (2, 2))


def pick(i, values):
    out = values[0]
    for n, value in enumerate(values[1:], 1):
        out = jnp.where(i == n, value, out)
    return out


class Tree:
    def __init__(self, buf, rows, send_sem, recv_sem):
        self.buf, self.rows, self.send_sem, self.recv_sem = buf, rows, send_sem, recv_sem
        self.sends, self.pieces, self.waited = [], {}, set()

    def view(self, a, b, lo, n):
        return self.buf.at[slot_of(a, b), pl.ds(lo * self.rows, n * self.rows)]

    def copy(self, i):
        a, b, lo, n, dx, dz = self.sends[i]
        view = self.view(a, b, lo, n)
        return pltpu.make_async_remote_copy(
            src_ref=view, dst_ref=view, send_sem=self.send_sem.at[i], recv_sem=self.recv_sem.at[i],
            device_id=dev(dx, dz), device_id_type=MESH)

    def send(self, a, b, lo, n, dx, dz):
        i = len(self.sends)
        self.sends.append((a, b, lo, n, dx, dz))
        self.pieces[((a - dx) % 4, (b - dz) % 4, lo, n)] = i
        self.copy(i).start()

    def wait(self, a, b, lo, n):
        i = self.pieces[(a % 4, b % 4, lo, n)]
        view = self.view(a, b, lo, n)
        pltpu.make_async_remote_copy(
            src_ref=view, dst_ref=view, send_sem=self.send_sem.at[i], recv_sem=self.recv_sem.at[i],
            device_id=dev(1, 0), device_id_type=MESH).wait_recv()
        self.waited.add(i)

    def finish(self):
        assert self.waited == set(range(len(self.sends)))
        for i in range(len(self.sends)):
            self.copy(i).wait_send()


def up(d):
    return 0 if d > 0 else 1


def gather_stages(tree, sibling):
    def first():
        for d in (1, -1):
            tree.send(0, 0, 0, 2, d, 0)
            tree.send(0, 0, 2, 2, 0, d)
        for d in (1, -1):
            tree.send(0, 0, 2, 2, d, 0)
            tree.send(0, 0, 0, 2, 0, d)
        sibling(0, 0)

    def second():
        for s in (1, -1):
            tree.wait(s, 0, 0, 2)
            tree.send(s, 0, up(-s), 1, -s, 0)
            tree.wait(0, s, 2, 2)
            tree.send(0, s, 2 + up(-s), 1, 0, -s)
        for s in (1, -1):
            for d in (1, -1):
                tree.send(s, 0, 0, 2, 0, d)
                tree.send(0, s, 2, 2, d, 0)

    def third():
        for s in (1, -1):
            tree.wait(s, 0, 2, 2)
            tree.send(s, 0, 2 + up(-s), 1, -s, 0)
            tree.wait(0, s, 0, 2)
            tree.send(0, s, up(-s), 1, 0, -s)
        for s in (1, -1):
            sibling(s, 0)
            sibling(0, s)

    def fourth():
        for q in (0, 1):
            tree.wait(2, 0, q, 1)
            tree.wait(0, 2, 2 + q, 1)
        for d in (1, -1):
            tree.send(2, 0, 0, 2, 0, d)
            tree.send(0, 2, 2, 2, d, 0)

    def fifth():
        for sx in (1, -1):
            for sz in (1, -1):
                tree.wait(sx, sz, 0, 2)
                tree.send(sx, sz, up(-sz), 1, 0, -sz)
                tree.wait(sx, sz, 2, 2)
                tree.send(sx, sz, 2 + up(-sx), 1, -sx, 0)
                sibling(sx, sz)

    def sixth():
        for q in (0, 1):
            tree.wait(2, 0, 2 + q, 1)
            tree.wait(0, 2, q, 1)
        sibling(2, 0)
        sibling(0, 2)
        for s in (1, -1):
            tree.wait(2, s, 0, 2)
            tree.send(2, s, up(-s), 1, 0, -s)
            tree.wait(s, 2, 2, 2)
            tree.send(s, 2, 2 + up(-s), 1, -s, 0)

    def seventh():
        for s in (1, -1):
            for q in (0, 1):
                tree.wait(2, s, 2 + q, 1)
                tree.wait(s, 2, q, 1)
            sibling(2, s)
            sibling(s, 2)

    def eighth():
        for q in (0, 1, 2, 3):
            tree.wait(2, 2, q, 1)
        sibling(2, 2)

    return first, second, third, fourth, fifth, sixth, seventh, eighth


def gather_part(r):
    xq, xp, W, X, acc, macc, scale = r.xq, r.xp, r.W, r.X, r.acc, r.macc, r.scale
    wsem, xsem, ssem, rsem, sibs, sibr = r.wsem, r.xsem, r.gsend, r.grecv, r.gsibs, r.gsibr
    lq, lp = xq.shape[0] // 4, xp.shape[0] // 4
    tq, tokens = xq.shape[0], X.shape[0]
    width = X.shape[1]
    depth = W.shape[1]
    T = 128
    mine = slot_of(0, 0)
    loads = []
    lo = 0
    for n, w in enumerate((r.wq, r.wk, r.wv)):
        loads.append(pltpu.make_async_copy(w, r.held.at[:, pl.ds(lo, w.shape[1])], wsem.at[n]))
        lo += w.shape[1]
    for load in loads:
        load.start()
    for i in range(tq // T):
        pltpu.make_async_copy(xq.at[pl.ds(i * T, T)], X.at[pl.ds(i * T, T)], xsem.at[i]).start()
    macc[...] = jnp.zeros_like(macc)
    eye = iota((depth, depth), 0) == iota((depth, depth), 1)
    own = r.gain[:, pl.ds(pl.multiple_of(mine * depth, depth), depth)]
    column = jnp.sum(jnp.where(eye, own, 0.0), axis=1, keepdims=True)
    for load in loads:
        load.wait()
    W[mine] = (r.held[...].astype(f32) * column).astype(bf16)
    pl.semaphore_wait(pltpu.get_barrier_semaphore(), len(peers()))

    tree = Tree(W, depth // 4, ssem, rsem)
    sib_sent = []

    def sib_copy(i, a, b, flip):
        view = W.at[slot_of(a, b, flip=flip)]
        return pltpu.make_async_remote_copy(
            src_ref=view, dst_ref=view, send_sem=sibs.at[i], recv_sem=sibr.at[i],
            device_id=dev(0, 0, flip=True), device_id_type=MESH)

    def sibling(a, b):
        sib_copy(len(sib_sent), a, b, False).start()
        sib_sent.append((a % 4, b % 4))

    stages = gather_stages(tree, sibling)
    C = 128
    chunks = width // C
    n_tiles = tokens // T
    n_query = tq // T
    stages[0]()
    pltpu.make_async_copy(r.wout_hbm, r.wout, r.osem).start()

    @pl.loop(0, n_tiles)
    def _(i):
        pltpu.make_async_copy(xq.at[pl.ds(0, T)], X.at[pl.ds(pl.multiple_of(i * T, T), T)], xsem.at[i]).wait()
        acc[pl.ds(pl.multiple_of(i * T, T), T), :] = jnp.zeros((T, acc.shape[1]), f32)

        @pl.when(i < n_tiles - n_query)
        def _():
            pltpu.make_async_copy(xp.at[pl.ds(pl.multiple_of(i * T, T), T)],
                                  X.at[pl.ds(pl.multiple_of((i + n_query) * T, T), T)],
                                  xsem.at[i + n_query]).start()

        per = lp // T
        seq = jnp.where(i < n_query, i // (lq // T), 4 + (i - n_query) // per)

        def step(n, sums):
            span = pl.ds(pl.multiple_of(i * T + n * 16, 16), 16)
            squares, later = [None] * 4, []
            for c in range(chunks):
                v = X[span, c * C:(c + 1) * C].astype(f32)
                w = v * v
                squares[c % 4] = w if squares[c % 4] is None else squares[c % 4] + w
                later.append(sums[c] + (v[0:8] + v[8:16]))
            scale[span, :] = (squares[0] + squares[1]) + (squares[2] + squares[3])
            return tuple(later)

        sums = lax.fori_loop(0, T // 16, step, tuple(
            macc[seq, :, c * C:(c + 1) * C] for c in range(chunks)))
        for c in range(chunks):
            macc[seq, :, c * C:(c + 1) * C] = sums[c]
        for at, stage in ((7, 1), (11, 2)):
            @pl.when(i == at)
            def _():
                stages[stage]()

    order = GATHERED

    @pl.loop(0, len(order))
    def _(i):
        a, b = pick(i, [o[0] % 4 for o in order]), pick(i, [o[1] % 4 for o in order])
        sib_copy(i, a, b, True).wait_recv()
        chip = chip_of(a, b)
        cols = pl.ds(pl.multiple_of(chip * 2 * depth, 2 * depth), 2 * depth)
        w = W[pl.ds(chip * 2, 2)].reshape(2 * depth, W.shape[2])
        total = jnp.dot(X[:, cols], w, preferred_element_type=f32)
        acc[...] = acc[...] + total
        for at, stage in ((0, 3), (4, 4), (6, 5), (8, 6), (11, 7)):
            @pl.when(i == at)
            def _():
                stages[stage]()

    assert sib_sent == [(a % 4, b % 4) for a, b in order]

    @pl.loop(0, n_tiles)
    def _(i):
        tile = pl.ds(pl.multiple_of(i * T, T), T)
        total = jnp.sum(scale[tile, :], axis=1, keepdims=True)
        factor = lax.rsqrt(total * (1.0 / width) + eps_norm)
        scale[tile, :] = jnp.broadcast_to(factor, (T, C))
        r.rows[tile, :] = (acc[tile, :] * factor).astype(bf16)

    for s in range(8):
        r.means[s:s + 1, :] = jnp.sum(macc[s], axis=0, keepdims=True) * (1.0 / (lq if s < 4 else lp))
    tree.finish()
    for i, (a, b) in enumerate(sib_sent):
        sib_copy(i, a, b, False).wait_send()


ORDER = ((2, 2), (2, 1), (2, -1), (1, 2), (-1, 2), (2, 0), (0, 2), (1, 1), (1, -1), (-1, 1), (-1, -1),
         (1, 0), (-1, 0), (0, 1), (0, -1), (0, 0))


def key_of(a, b):
    return a % 4, b % 4


class Fold:
    def __init__(self, part, landed, send_sem, recv_sem):
        self.part, self.landed, self.send_sem, self.recv_sem = part, landed, send_sem, recv_sem
        self.sends, self.pieces, self.used, self.waited = [], {}, 0, set()
        self.index = {key_of(a, b): i for i, (a, b) in enumerate(ORDER)}

    def copy(self, i):
        a, b, lo, n, dx, dz, off = self.sends[i]
        return pltpu.make_async_remote_copy(
            src_ref=self.part.at[self.index[key_of(a, b)], pl.ds(lo, n)], dst_ref=self.landed.at[pl.ds(off, n)],
            send_sem=self.send_sem.at[i], recv_sem=self.recv_sem.at[i],
            device_id=dev(dx, dz), device_id_type=MESH)

    def send(self, a, b, lo, n, dx, dz):
        i = len(self.sends)
        self.sends.append((a, b, lo, n, dx, dz, self.used))
        self.used += n
        self.pieces[(*key_of(a - dx, b - dz), lo, n, *key_of(-dx, -dz))] = i
        self.copy(i).start()

    def recv(self, a, b, lo, n, dx, dz):
        i = self.pieces[(*key_of(a, b), lo, n, *key_of(dx, dz))]
        self.copy(i).wait_recv()
        self.waited.add(i)
        off = self.sends[i][6]
        return self.landed.at[pl.ds(off, n)]

    def add(self, a, b, lo, n, *froms):
        at = self.index[key_of(a, b)]
        for m, (dx, dz) in froms:
            piece = self.recv(a, b, m[0], m[1], dx, dz)
            cut = piece.shape[1] // 2

            @pl.loop(0, 2 * m[1])
            def _(n):
                q, rows = n // 2, pl.ds(pl.multiple_of(n % 2 * cut, cut), cut)
                self.part[at, m[0] + q, rows, :] = self.part[at, m[0] + q, rows, :] + piece[q, rows, :]

    def finish(self):
        assert self.waited == set(range(len(self.sends))), (len(self.waited), len(self.sends))
        for i in range(len(self.sends)):
            self.copy(i).wait_send()


def ends(fold, a, b, half):
    if half == 0:
        fold.send(a, b, 0, 1, 0, -1)
        fold.send(a, b, 1, 1, 0, 1)
    else:
        fold.send(a, b, 2, 1, -1, 0)
        fold.send(a, b, 3, 1, 1, 0)


def fold_steps(fold):
    def first(i):
        a, b = ORDER[i]
        if (a, b) == (2, 2):
            ends(fold, a, b, 0)
            ends(fold, a, b, 1)
        elif a == 2:
            ends(fold, a, b, 1)
        elif b == 2:
            ends(fold, a, b, 0)
        elif a and b:
            q = up(-b)
            fold.add(a, b, 0, 2, ((q, 1), (0, -b)))
            fold.send(a, b, 0, 2, 0, b)
            q = 2 + up(-a)
            fold.add(a, b, 2, 2, ((q, 1), (-a, 0)))
            fold.send(a, b, 2, 2, a, 0)

    def second():
        for s in (1, -1):
            fold.add(2, s, 0, 2, ((up(-s), 1), (0, -s)))
            fold.send(2, s, 0, 2, 0, s)
            fold.add(s, 2, 2, 2, ((2 + up(-s), 1), (-s, 0)))
            fold.send(s, 2, 2, 2, s, 0)

    def third():
        fold.add(2, 0, 0, 2, ((0, 2), (0, 1)), ((0, 2), (0, -1)))
        fold.send(2, 0, 0, 1, -1, 0)
        fold.send(2, 0, 1, 1, 1, 0)
        fold.add(0, 2, 2, 2, ((2, 2), (1, 0)), ((2, 2), (-1, 0)))
        fold.send(0, 2, 2, 1, 0, -1)
        fold.send(0, 2, 3, 1, 0, 1)

    def fourth():
        for s in (1, -1):
            fold.add(s, 0, 2, 2, ((2 + up(-s), 1), (-s, 0)))
            fold.send(s, 0, 2, 2, s, 0)
            fold.add(0, s, 0, 2, ((up(-s), 1), (0, -s)))
            fold.send(0, s, 0, 2, 0, s)

    def fifth():
        for s in (1, -1):
            fold.add(s, 0, 0, 2, ((0, 2), (0, 1)), ((0, 2), (0, -1)), ((up(-s), 1), (-s, 0)))
            fold.send(s, 0, 0, 2, s, 0)
            fold.add(0, s, 2, 2, ((2, 2), (1, 0)), ((2, 2), (-1, 0)), ((2 + up(-s), 1), (0, -s)))
            fold.send(0, s, 2, 2, 0, s)

    steps = {i: [functools.partial(first, i)] for i in range(11)}
    steps[6].append(second)
    steps[11] = [third]
    steps[14] = [fourth]
    steps[15] = [fifth]
    return steps


NT = (((1,), (1,)), ((), ()))
EXACT = lax.Precision.HIGHEST
AROUND = tuple((a, b) for a in (1, 3, 0, 2) for b in (1, 3, 0, 2) if (a, b) != (0, 0))


def block_of(row, n):
    H = HEAD_DIM
    return pl.ds(pl.multiple_of((row + n // 6) * H, H), H), slice(n % 6 * H, (n % 6 + 1) * H)


def attend_forward(rows, att, wts, pooled, base, blocks, row, seq, groups):
    H = HEAD_DIM
    key_at, value_at = groups * H, (groups + 1) * H
    L = blocks * H
    k = rows[pl.ds(base, L), key_at:key_at + H]
    v = rows[pl.ds(base, L), value_at:value_at + H].astype(f32)
    causal = iota((H, H), 0) <= iota((H, H), 1)
    n = 0
    for h in range(groups):
        w = [None] * blocks
        for ib in range(blocks):
            q = rows[pl.ds(pl.multiple_of(base + ib * H, H), H), h * H:(h + 1) * H]
            e = []
            for jb in range(ib + 1):
                st = lax.dot_general(k[jb * H:(jb + 1) * H], q, NT, preferred_element_type=f32)
                st = jnp.exp(st * (1.0 / math.sqrt(H)))
                e.append(jnp.where(causal, st, 0.0) if jb == ib else st)
            total = jnp.sum(e[0], axis=0, keepdims=True)
            for one in e[1:]:
                total = total + jnp.sum(one, axis=0, keepdims=True)
            r = 1.0 / total
            for jb in range(ib + 1):
                at = e[jb] * r
                att[block_of(row, n)] = at
                n += 1
                w[jb] = at if w[jb] is None else w[jb] + at
        out = None
        for jb in range(blocks):
            col = jnp.sum(w[jb], axis=1, keepdims=True) * (1.0 / L)
            wts[pl.ds(pl.multiple_of(base + jb * H, H), H), h:h + 1] = col
            part = jnp.sum(col * v[jb * H:(jb + 1) * H], axis=0, keepdims=True)
            out = part if out is None else out + part
        pooled[seq, :, h * H:(h + 1) * H] = jnp.broadcast_to(out, (8, H))


def attend_backward(rows, scale, att, wts, ups, dgt, base, blocks, row, seq, groups):
    H = HEAD_DIM
    key_at, value_at = groups * H, (groups + 1) * H
    L = blocks * H
    k = rows[pl.ds(base, L), key_at:key_at + H]
    v = rows[pl.ds(base, L), value_at:value_at + H].astype(f32)
    kt = k.astype(f32).T.astype(bf16)
    dk, dv = [None] * blocks, [None] * blocks
    eye = iota((H, H), 0) == iota((H, H), 1)
    along = []
    for jb in range(blocks):
        column = scale[pl.ds(pl.multiple_of(base + jb * H, H), H), 0:1]
        along.append(jnp.sum(jnp.where(eye, column, 0.0), axis=0, keepdims=True))
    n = 0
    for h in range(groups):
        u = ups[seq, :, h * H:(h + 1) * H][0:1]
        c = [jnp.sum(v[jb * H:(jb + 1) * H] * u, axis=1, keepdims=True) * (1.0 / L) for jb in range(blocks)]
        for ib in range(blocks):
            span = pl.ds(pl.multiple_of(base + ib * H, H), H)
            q = rows[span, h * H:(h + 1) * H]
            at = [att[block_of(row, n + jb)] for jb in range(ib + 1)]
            n += ib + 1
            m = None
            for jb in range(ib + 1):
                part = jnp.sum(at[jb] * c[jb], axis=0, keepdims=True)
                m = part if m is None else m + part
            dq = None
            for jb in range(ib + 1):
                ds = (at[jb] * ((c[jb] - m) * (1.0 / math.sqrt(H)))).astype(bf16)
                part = jnp.dot(kt[:, jb * H:(jb + 1) * H], ds, preferred_element_type=f32)
                dq = part if dq is None else dq + part
                part = jnp.dot(ds, q, preferred_element_type=f32)
                dk[jb] = part if dk[jb] is None else dk[jb] + part
            dgt[h * H:(h + 1) * H, span] = (dq * along[ib]).astype(bf16)
        for jb in range(blocks):
            part = wts[pl.ds(pl.multiple_of(base + jb * H, H), H), h:h + 1] * u
            dv[jb] = part if dv[jb] is None else dv[jb] + part
    for jb in range(blocks):
        span = pl.ds(pl.multiple_of(base + jb * H, H), H)
        dgt[key_at:key_at + H, span] = (dk[jb].T * along[jb]).astype(bf16)
        dgt[value_at:value_at + H, span] = (dv[jb].T * along[jb]).astype(bf16)


def middle_part(r):
    lq, lp = r.xq.shape[0] // 4, r.xp.shape[0] // 4
    rows, scale, means, wout, att, wts = r.rows, r.scale, r.means, r.wout, r.acc, r.wts
    pooled, ups, terms, got, embeds, qs, ps = r.pooled, r.ups, r.terms, r.got, r.embeds, r.qs, r.ps
    gram, dl, dlt, raws, dgt, loss, owner, place_in = (
        r.gram, r.dl, r.dlt, r.raws, r.dgt, r.loss, r.owner, r.place_in)
    asem, arecv, bsem, brecv, sibs, sibr = r.asend, r.arecv, r.bsend, r.brecv, r.msibs, r.msibr
    csem, crecv, dsem, drecv = r.csend, r.crecv, r.dsend, r.drecv
    H = HEAD_DIM
    groups = rows.shape[1] // H - 2
    width = wout.shape[1]
    seqs = 4
    nt = 4
    part_w = width // nt
    x, z, core = place()
    t = lax.axis_index("tensor")
    base_p = seqs * lq
    bq, bp = lq // H, lp // H

    @pl.loop(0, seqs)
    def _(s):
        attend_forward(rows, att, wts, pooled, pl.multiple_of(s * lq, H), bq, s, s, groups)

    @pl.loop(0, seqs)
    def _(s):
        attend_forward(rows, att, wts, pooled, pl.multiple_of(base_p + s * lp, H), bp, seqs + 2 * s, seqs + s, groups)

    pltpu.make_async_copy(r.wout_hbm, wout, r.osem).wait()
    row = iota((8, groups * H), 0)
    low = pooled[0]
    for s in range(1, 8):
        low = jnp.where(row == s, pooled[s], low)
    low = low.astype(bf16)

    def y_copy(src, dst, d, send_sem, recv_sem):
        return pltpu.make_async_remote_copy(
            src_ref=src, dst_ref=dst, send_sem=send_sem.at[d - 1], recv_sem=recv_sem.at[d - 1],
            device_id={"tensor": (t + d) % nt}, device_id_type=MESH)

    def term(o):
        cols = pl.ds(pl.multiple_of(o * part_w, part_w), part_w)
        return jnp.dot(low, wout[:, cols], preferred_element_type=f32)

    a_copies = []
    for d in (2, 1, 3):
        terms[d] = term((t + d) % nt)
        copy = y_copy(terms.at[d], got.at[d], d, asem, arecv)
        copy.start()
        a_copies.append(copy)
    mine = term(t) + means[:, pl.ds(pl.multiple_of(t * part_w, part_w), part_w)]
    n_rows = qs.shape[0]
    ids = owner[...] * seqs + place_in[...]
    col = iota((n_rows, n_rows), 1)
    counts = jnp.zeros((n_rows, n_rows), f32)
    for j in range(ids.shape[0]):
        counts = counts + jnp.where(ids[j:j + 1, :] == iota((n_rows, n_rows), 0), 1.0, 0.0)
    counts = counts.T
    for copy in a_copies:
        copy.wait_recv()
    mine = mine + got[1] + got[2] + got[3]
    here = slot_of(0, 0)
    embeds[here] = mine

    def b_copy(n, a, b):
        view = embeds.at[here]
        return pltpu.make_async_remote_copy(
            src_ref=view, dst_ref=view, send_sem=bsem.at[n], recv_sem=brecv.at[n],
            device_id=dev(a, b), device_id_type=MESH)

    def s_copy(n, a, b, flip):
        view = embeds.at[slot_of(a, b, flip=flip)]
        return pltpu.make_async_remote_copy(
            src_ref=view, dst_ref=view, send_sem=sibs.at[n], recv_sem=sibr.at[n],
            device_id=dev(0, 0, flip=True), device_id_type=MESH)

    for n, (a, b) in enumerate(AROUND):
        b_copy(n, a, b).start()
    s_copy(15, 0, 0, False).start()
    for n, (a, b) in enumerate(AROUND):
        view = embeds.at[slot_of(-a, -b)]
        pltpu.make_async_remote_copy(
            src_ref=view, dst_ref=view, send_sem=bsem.at[n], recv_sem=brecv.at[n],
            device_id=dev(a, b), device_id_type=MESH).wait_recv()
        s_copy(n, -a, -b, False).start()
    s_copy(15, 0, 0, True).wait_recv()
    for n, (a, b) in enumerate(AROUND):
        s_copy(n, -a, -b, True).wait_recv()

    first = iota((8, part_w), 0) < seqs

    @pl.loop(0, n_rows // 8)
    def _(k):
        one, two = embeds[2 * k], embeds[2 * k + 1]
        span = pl.ds(pl.multiple_of(k * 8, 8), 8)
        qs[span, :] = jnp.where(first, one, pltpu.roll(two, seqs, 0))
        ps[span, :] = jnp.where(first, pltpu.roll(one, seqs, 0), two)

    q, p = qs[...], ps[...]
    gram[0, pl.ds(0, n_rows), :] = lax.dot_general(q, p, NT, precision=EXACT, preferred_element_type=f32)
    ones = jnp.ones((8, part_w), f32)
    gram[0, pl.ds(n_rows, 8), :] = lax.dot_general(ones, q * q, NT, precision=EXACT, preferred_element_type=f32)
    gram[0, pl.ds(n_rows + 8, 8), :] = lax.dot_general(ones, p * p, NT, precision=EXACT, preferred_element_type=f32)
    c_copies = []
    for d in (2, 1, 3):
        copy = y_copy(gram.at[0], gram.at[d], d, csem, crecv)
        copy.start()
        c_copies.append(copy)
    for copy in c_copies:
        copy.wait_recv()
    whole = (gram[0] + gram[2]) + (gram[1] + gram[3])
    eye = iota((n_rows, n_rows), 0) == col
    inv = lax.rsqrt(whole[n_rows:] + eps_unit)
    inv_q_row, inv_p_row = inv[0:1], inv[8:9]
    inv_q = jnp.sum(jnp.where(eye, inv_q_row, 0.0), axis=1, keepdims=True)
    inv_p = jnp.sum(jnp.where(eye, inv_p_row, 0.0), axis=1, keepdims=True)
    cosine = whole[:n_rows] * inv_q * inv_p_row
    logits = cosine * (1.0 / sharpness_divisor)
    raised = jnp.exp(logits) * (1.0 + counts)
    sums = jnp.sum(raised, axis=1, keepdims=True)
    diagonal = jnp.sum(jnp.where(eye, logits, 0.0), axis=1, keepdims=True)
    loss[...] = jnp.sum(jnp.log(sums) - diagonal, axis=0, keepdims=True) * (1.0 / n_rows)
    slope = (raised / sums - jnp.where(eye, 1.0, 0.0)) * (1.0 / sharpness_divisor)
    dl[0] = slope
    dlt[0] = slope.T
    weighted = slope * cosine
    dl[1] = jnp.broadcast_to(jnp.sum(weighted, axis=1, keepdims=True), (n_rows, n_rows))
    dlt[1] = jnp.broadcast_to(jnp.sum(weighted, axis=0, keepdims=True), (n_rows, n_rows)).T
    dl[2] = jnp.broadcast_to(inv_q, (n_rows, n_rows))
    dlt[2] = jnp.broadcast_to(inv_p, (n_rows, n_rows))
    chip = pl.ds(pl.multiple_of(chip_of(0, 0) * 8, 8), 8)

    def back(table, own, others, scale):
        d = jnp.dot(table[0, chip, :], others * scale, precision=EXACT, preferred_element_type=f32)
        inverse = table[2, chip, :][:, 0:1]
        e = own[chip, :] * inverse
        return inverse * (d - e * table[1, chip, :][:, 0:1])

    rq = back(dl, qs, p, inv_p)
    rp = back(dlt, ps, q, inv_q)
    left = core == 0
    rq = jnp.where(left, rq, pltpu.roll(rq, seqs, 0))
    rp = jnp.where(left, pltpu.roll(rp, seqs, 0), rp)
    raws[t] = jnp.where(first, rq, rp)
    d_copies = []
    for d in (2, 1, 3):
        copy = y_copy(raws.at[t], raws.at[t], d, dsem, drecv)
        copy.start()
        d_copies.append(copy)
    total = None
    for d in (0, 1, 3, 2):
        o = (t - d) % nt
        if d:
            y_copy(raws.at[o], raws.at[o], d, dsem, drecv).wait_recv()
        cols = pl.ds(pl.multiple_of(o * part_w, part_w), part_w)
        part = lax.dot_general(raws[o].astype(bf16), wout[:, cols], NT, preferred_element_type=f32)
        total = part if total is None else total + part
    for s in range(8):
        ups[s] = jnp.broadcast_to(total[s:s + 1], (8, groups * H))

    @pl.loop(0, seqs)
    def _(s):
        attend_backward(rows, scale, att, wts, ups, dgt, pl.multiple_of(s * lq, H), bq, s, s, groups)

    @pl.loop(0, seqs)
    def _(s):
        attend_backward(rows, scale, att, wts, ups, dgt, pl.multiple_of(base_p + s * lp, H), bp,
                        seqs + 2 * s, seqs + s, groups)

    for copy in a_copies + c_copies + d_copies:
        copy.wait_send()
    for n, (a, b) in enumerate(AROUND):
        b_copy(n, a, b).wait_send()
        s_copy(n, -a, -b, False).wait_send()
    s_copy(15, 0, 0, False).wait_send()


def scatter_part(r):
    part, both, sib, landed = r.part, r.both, r.sib, r.landed
    ssem, rsem, sibs, sibr = r.fsend, r.frecv, r.fsibs, r.fsibr
    depth = 2 * r.out.shape[1]
    qr = part.shape[2]
    half = depth // 2
    core = place()[2]
    own = pl.ds(pl.multiple_of(core * half, half), half)
    other = pl.ds(pl.multiple_of((1 - core) * half, half), half)

    def sib_copy(i):
        return pltpu.make_async_remote_copy(
            src_ref=both.at[i, :, :, other], dst_ref=sib.at[i], send_sem=sibs.at[i], recv_sem=sibr.at[i],
            device_id=dev(0, 0, flip=True), device_id_type=MESH)

    fold = Fold(part, landed, ssem, rsem)
    steps = fold_steps(fold)

    @pl.loop(0, 17)
    def _(i):
        @pl.when(i < 16)
        def _():
            chip = chip_of(pick(i, [o[0] % 4 for o in ORDER]), pick(i, [o[1] % 4 for o in ORDER]))
            cols = pl.ds(pl.multiple_of(chip * depth, depth), depth)
            total = jnp.dot(r.dgt[...], r.X[:, cols], preferred_element_type=f32).astype(bf16)
            both[i] = total.reshape(4, qr, depth)
            sib_copy(i).start()

        @pl.when(i > 0)
        def _():
            sib_copy(i - 1).wait_recv()

            @pl.loop(0, 4)
            def _(n):
                part[i - 1, n] = both[i - 1, n, :, own] + sib[i - 1, n]

        for at in sorted(steps):
            @pl.when(i == at + 1)
            def _():
                for step in steps[at]:
                    step()

    for side in (0, 1):
        total = part[15, pl.ds(2 * side, 2)].astype(f32)
        for dx, dz in ((1, 0), (-1, 0), (0, 1), (0, -1)):
            total = total + fold.recv(0, 0, 2 * side, 2, dx, dz)[...].astype(f32)
        r.out[pl.ds(side * 2 * qr, 2 * qr), :] = total.reshape(2 * qr, half)
    fold.finish()
    for i in range(16):
        sib_copy(i).wait_send()


def finish_kernel(sums, gain, gq, gk, gv):
    H = HEAD_DIM
    depth = sums.shape[1]
    own = gain[:, pl.ds(pl.multiple_of(slot_of(0, 0) * depth, depth), depth)]
    heads = gq.shape[1] // H
    for n in range(heads + 2):
        block = (sums[n * H:(n + 1) * H, :] * own).T
        if n < heads:
            gq[:, n * H:(n + 1) * H] = block
        elif n == heads:
            gk[...] = block
        else:
            gv[...] = block


def finish(sums, gain):
    rows, depth = sums.shape
    cols = (rows - 2 * HEAD_DIM, HEAD_DIM, HEAD_DIM)
    VM = pl.BlockSpec(memory_space=pltpu.VMEM)
    return pl.pallas_call(
        finish_kernel,
        out_shape=tuple(jax.ShapeDtypeStruct((depth, n), f32) for n in cols),
        in_specs=[VM, VM],
        out_specs=(VM, VM, VM),
        name="finish_rows",
    )(sums, gain.reshape(1, -1))


def peers():
    t = lax.axis_index("tensor")
    return [{"tensor": (t + d) % 4} for d in (1, 2, 3)] + [dev(a, b) for a, b in AROUND] + [dev(0, 0, flip=True)]


def step_kernel(names, *refs):
    r = types.SimpleNamespace(**dict(zip(names, refs, strict=True)))
    barrier = pltpu.get_barrier_semaphore()
    for peer in peers():
        pl.semaphore_signal(barrier, inc=1, device_id=peer, device_id_type=MESH)
    gather_part(r)
    middle_part(r)
    scatter_part(r)


def step(xq, xp, gain, wq, wk, wv, w_out, owner, place_in):
    tokens, width = xq.shape[0] + xp.shape[0], xq.shape[1]
    depth, heads = wq.shape
    cols = heads + wk.shape[1] + wv.shape[1]
    n = owner.shape[1]
    H = HEAD_DIM
    ANY, VM = pl.BlockSpec(memory_space=pl.ANY), pl.BlockSpec(memory_space=pltpu.VMEM)

    def dma(*shape):
        return pltpu.SemaphoreType.DMA(shape)

    ins = dict(xq=ANY, xp=ANY, gain=VM, wq=ANY, wk=ANY, wv=ANY, wout_hbm=ANY, owner=VM, place_in=VM)
    outs = dict(out=jax.ShapeDtypeStruct((cols, depth), f32), loss=jax.ShapeDtypeStruct((1, 1), f32))
    scratch = dict(
        W=pltpu.VMEM((32, depth, cols), bf16), held=pltpu.VMEM((depth, cols), bf16),
        X=pltpu.VMEM((tokens, width), bf16), acc=pltpu.VMEM((tokens, cols), f32),
        macc=pltpu.VMEM((8, 8, width), f32), rows=pltpu.VMEM((tokens, cols), bf16),
        scale=pltpu.VMEM((tokens, H), f32), means=pltpu.VMEM((8, width), f32),
        wout=pltpu.VMEM(w_out.shape, bf16), wts=pltpu.VMEM((tokens, H), f32),
        pooled=pltpu.VMEM((8, 8, heads), f32), ups=pltpu.VMEM((8, 8, heads), f32),
        terms=pltpu.VMEM((4, 8, width // 4), f32), got=pltpu.VMEM((4, 8, width // 4), f32),
        embeds=pltpu.VMEM((32, 8, width // 4), f32),
        qs=pltpu.VMEM((n, width // 4), f32), ps=pltpu.VMEM((n, width // 4), f32),
        gram=pltpu.VMEM((4, n + 16, n), f32), dl=pltpu.VMEM((3, n, n), f32), dlt=pltpu.VMEM((3, n, n), f32),
        raws=pltpu.VMEM((4, 8, width // 4), f32), dgt=pltpu.VMEM((cols, tokens), bf16),
        part=pltpu.VMEM((16, 4, cols // 4, depth), bf16), both=pltpu.VMEM((16, 4, cols // 4, 2 * depth), bf16),
        sib=pltpu.VMEM((16, 4, cols // 4, depth), bf16), landed=pltpu.VMEM((60, cols // 4, depth), bf16),
        wsem=dma(3), xsem=dma(tokens // 128), osem=dma(),
        gsend=dma(40), grecv=dma(40), gsibs=dma(16), gsibr=dma(16),
        asend=dma(3), arecv=dma(3), bsend=dma(15), brecv=dma(15), msibs=dma(16), msibr=dma(16),
        csend=dma(3), crecv=dma(3), dsend=dma(3), drecv=dma(3),
        fsend=dma(40), frecv=dma(40), fsibs=dma(16), fsibr=dma(16))
    return pl.pallas_call(
        functools.partial(step_kernel, (*ins, *outs, *scratch)),
        out_shape=tuple(outs.values()),
        in_specs=list(ins.values()),
        out_specs=(VM, VM),
        scratch_shapes=list(scratch.values()),
        compiler_params=pltpu.CompilerParams(
            collective_id=0, has_side_effects=True, vmem_limit_bytes=VMEM_LIMIT),
        cost_estimate=pl.CostEstimate(flops=4 * tokens * width * cols, bytes_accessed=2 * tokens * width,
                                      transcendentals=0),
        name="contrast_step",
    )(xq, xp, gain.reshape(1, -1), wq, wk, wv, w_out, owner, place_in)


def body(
    query_states, passage_states, norm_gain, w_query, w_key, w_value, w_out, neg_owner, neg_slot
):
    owned, query_length, _ = query_states.shape
    passage_length = passage_states.shape[1]
    xq = query_states.reshape(owned * query_length, -1)
    xp = passage_states.reshape(owned * passage_length, -1)
    sums, loss = step(xq, xp, norm_gain, w_query, w_key, w_value, w_out, neg_owner.T, neg_slot.T)
    return (loss[0, 0], *finish(sums, norm_gain))


def solution(mesh):
    in_specs = (
        P("dp", None, None),
        P("dp", None, None),
        P(),
        P("dp", "tensor"),
        P("dp", "tensor"),
        P("dp", "tensor"),
        P("tensor", None),
        P(),
        P(),
    )
    out_specs = (P(), P("dp", "tensor"), P("dp", "tensor"), P("dp", "tensor"))
    return jax.shard_map(body, mesh=mesh, in_specs=in_specs, out_specs=out_specs, check_vma=False)
```

```python
import functools
import math
import types

import jax
import jax.numpy as jnp
from jax import lax
from jax.experimental import pallas as pl
from jax.experimental.pallas import tpu as pltpu
from jax.sharding import PartitionSpec as P

HEAD_DIM = 128
eps_norm = 1e-06
eps_unit = 1e-06
sharpness_divisor = 0.05
MESH = pl.DeviceIdType.MESH
f32, bf16 = jnp.float32, jnp.bfloat16
XS, ZS = 4, 4
STAT_STEPS = ((7, 1), (11, 2))
SUM_STEPS = ((0, 3), (4, 4), (6, 5), (8, 6), (13, 7))
VMEM_LIMIT = 63 * 1024 * 1024


def iota(shape, dim):
    return lax.broadcasted_iota(jnp.int32, shape, dim)


def place():
    p = lax.axis_index("dp")
    return p // (2 * ZS), (p // 2) % ZS, p % 2


def slot_of(a, b, core=None, flip=False):
    x, z, c = place()
    c = 1 - c if flip else c
    return ((x + a) % XS * ZS + (z + b) % ZS) * 2 + c


def chip_of(a, b):
    x, z, _ = place()
    return (x + a) % XS * ZS + (z + b) % ZS


def dev(a, b, flip=False):
    return {"dp": slot_of(a, b, flip=flip)}


GATHERED = ((0, 0), (1, 0), (0, 1), (-1, 0), (0, -1), (1, 1), (1, -1), (-1, 1), (-1, -1), (2, 0), (0, 2),
            (2, 1), (1, 2), (2, -1), (-1, 2), (2, 2))


def pick(i, values):
    out = values[0]
    for n, value in enumerate(values[1:], 1):
        out = jnp.where(i == n, value, out)
    return out


class Tree:
    def __init__(self, buf, rows, send_sem, recv_sem):
        self.buf, self.rows, self.send_sem, self.recv_sem = buf, rows, send_sem, recv_sem
        self.sends, self.pieces, self.waited = [], {}, set()

    def view(self, a, b, lo, n):
        return self.buf.at[slot_of(a, b), pl.ds(lo * self.rows, n * self.rows)]

    def copy(self, i):
        a, b, lo, n, dx, dz = self.sends[i]
        view = self.view(a, b, lo, n)
        return pltpu.make_async_remote_copy(
            src_ref=view, dst_ref=view, send_sem=self.send_sem.at[i], recv_sem=self.recv_sem.at[i],
            device_id=dev(dx, dz), device_id_type=MESH)

    def send(self, a, b, lo, n, dx, dz):
        i = len(self.sends)
        self.sends.append((a, b, lo, n, dx, dz))
        self.pieces[((a - dx) % 4, (b - dz) % 4, lo, n)] = i
        self.copy(i).start()

    def wait(self, a, b, lo, n):
        i = self.pieces[(a % 4, b % 4, lo, n)]
        view = self.view(a, b, lo, n)
        pltpu.make_async_remote_copy(
            src_ref=view, dst_ref=view, send_sem=self.send_sem.at[i], recv_sem=self.recv_sem.at[i],
            device_id=dev(1, 0), device_id_type=MESH).wait_recv()
        self.waited.add(i)

    def finish(self):
        assert self.waited == set(range(len(self.sends)))
        for i in range(len(self.sends)):
            self.copy(i).wait_send()


def up(d):
    return 0 if d > 0 else 1


def gather_stages(tree, sibling):
    def first():
        for d in (1, -1):
            tree.send(0, 0, 0, 2, d, 0)
            tree.send(0, 0, 2, 2, 0, d)
        for d in (1, -1):
            tree.send(0, 0, 2, 2, d, 0)
            tree.send(0, 0, 0, 2, 0, d)
        sibling(0, 0)

    def second():
        for s in (1, -1):
            tree.wait(s, 0, 0, 2)
            tree.send(s, 0, up(-s), 1, -s, 0)
            tree.wait(0, s, 2, 2)
            tree.send(0, s, 2 + up(-s), 1, 0, -s)
        for s in (1, -1):
            for d in (1, -1):
                tree.send(s, 0, 0, 2, 0, d)
                tree.send(0, s, 2, 2, d, 0)

    def third():
        for s in (1, -1):
            tree.wait(s, 0, 2, 2)
            tree.send(s, 0, 2 + up(-s), 1, -s, 0)
            tree.wait(0, s, 0, 2)
            tree.send(0, s, up(-s), 1, 0, -s)
        for s in (1, -1):
            sibling(s, 0)
            sibling(0, s)

    def fourth():
        for q in (0, 1):
            tree.wait(2, 0, q, 1)
            tree.wait(0, 2, 2 + q, 1)
        for d in (1, -1):
            tree.send(2, 0, 0, 2, 0, d)
            tree.send(0, 2, 2, 2, d, 0)

    def fifth():
        for sx in (1, -1):
            for sz in (1, -1):
                tree.wait(sx, sz, 0, 2)
                tree.send(sx, sz, up(-sz), 1, 0, -sz)
                tree.wait(sx, sz, 2, 2)
                tree.send(sx, sz, 2 + up(-sx), 1, -sx, 0)
                sibling(sx, sz)

    def sixth():
        for q in (0, 1):
            tree.wait(2, 0, 2 + q, 1)
            tree.wait(0, 2, q, 1)
        sibling(2, 0)
        sibling(0, 2)
        for s in (1, -1):
            tree.wait(2, s, 0, 2)
            tree.send(2, s, up(-s), 1, 0, -s)
            tree.wait(s, 2, 2, 2)
            tree.send(s, 2, 2 + up(-s), 1, -s, 0)

    def seventh():
        for s in (1, -1):
            for q in (0, 1):
                tree.wait(2, s, 2 + q, 1)
                tree.wait(s, 2, q, 1)
            sibling(2, s)
            sibling(s, 2)

    def eighth():
        for q in (0, 1, 2, 3):
            tree.wait(2, 2, q, 1)
        sibling(2, 2)

    return first, second, third, fourth, fifth, sixth, seventh, eighth


def gather_part(r):
    xq, xp, W, X, acc, macc, scale = r.xq, r.xp, r.W, r.X, r.acc, r.macc, r.scale
    wsem, xsem, ssem, rsem, sibs, sibr = r.wsem, r.xsem, r.gsend, r.grecv, r.gsibs, r.gsibr
    lq, lp = xq.shape[0] // 4, xp.shape[0] // 4
    tq, tokens = xq.shape[0], X.shape[0]
    width = X.shape[1]
    depth = W.shape[1]
    T = 128
    mine = slot_of(0, 0)
    loads = []
    lo = 0
    for n, w in enumerate((r.wq, r.wk, r.wv)):
        loads.append(pltpu.make_async_copy(w, r.held.at[:, pl.ds(lo, w.shape[1])], wsem.at[n]))
        lo += w.shape[1]
    for load in loads:
        load.start()
    for i in range(tq // T):
        pltpu.make_async_copy(xq.at[pl.ds(i * T, T)], X.at[pl.ds(i * T, T)], xsem.at[i]).start(priority=1)
    macc[...] = jnp.zeros_like(macc)
    eye = iota((depth, depth), 0) == iota((depth, depth), 1)
    own = r.gain[:, pl.ds(pl.multiple_of(mine * depth, depth), depth)]
    column = jnp.sum(jnp.where(eye, own, 0.0), axis=1, keepdims=True)
    for load in loads:
        load.wait()
    W[mine] = (r.held[...].astype(f32) * column).astype(bf16)
    pl.semaphore_wait(pltpu.get_barrier_semaphore(), len(peers()))

    tree = Tree(W, depth // 4, ssem, rsem)
    sib_sent = []

    def sib_copy(i, a, b, flip):
        view = W.at[slot_of(a, b, flip=flip)]
        return pltpu.make_async_remote_copy(
            src_ref=view, dst_ref=view, send_sem=sibs.at[i], recv_sem=sibr.at[i],
            device_id=dev(0, 0, flip=True), device_id_type=MESH)

    def sibling(a, b):
        sib_copy(len(sib_sent), a, b, False).start()
        sib_sent.append((a % 4, b % 4))

    stages = gather_stages(tree, sibling)
    C = 128
    chunks = width // C
    n_tiles = tokens // T
    n_query = tq // T
    stages[0]()
    pltpu.make_async_copy(r.wout_hbm, r.wout, r.osem).start(priority=1)

    @pl.loop(0, n_tiles)
    def _(i):
        pltpu.make_async_copy(xq.at[pl.ds(0, T)], X.at[pl.ds(pl.multiple_of(i * T, T), T)], xsem.at[i]).wait()
        acc[pl.ds(pl.multiple_of(i * T, T), T), :] = jnp.zeros((T, acc.shape[1]), f32)

        @pl.when(i < n_tiles - n_query)
        def _():
            pltpu.make_async_copy(xp.at[pl.ds(pl.multiple_of(i * T, T), T)],
                                  X.at[pl.ds(pl.multiple_of((i + n_query) * T, T), T)],
                                  xsem.at[i + n_query]).start(priority=1)

        per = lp // T
        seq = jnp.where(i < n_query, i // (lq // T), 4 + (i - n_query) // per)

        def step(n, sums):
            span = pl.ds(pl.multiple_of(i * T + n * 16, 16), 16)
            squares, later = [None] * 4, []
            for c in range(chunks):
                v = X[span, c * C:(c + 1) * C].astype(f32)
                w = v * v
                squares[c % 4] = w if squares[c % 4] is None else squares[c % 4] + w
                later.append(sums[c] + (v[0:8] + v[8:16]))
            scale[span, :] = (squares[0] + squares[1]) + (squares[2] + squares[3])
            return tuple(later)

        sums = lax.fori_loop(0, T // 16, step, tuple(
            macc[seq, :, c * C:(c + 1) * C] for c in range(chunks)))
        for c in range(chunks):
            macc[seq, :, c * C:(c + 1) * C] = sums[c]
        for at, stage in STAT_STEPS:
            @pl.when(i == at)
            def _():
                stages[stage]()

    @pl.loop(0, n_tiles)
    def _(i):
        tile = pl.ds(pl.multiple_of(i * T, T), T)
        total = jnp.sum(scale[tile, :], axis=1, keepdims=True)
        scale[tile, :] = jnp.broadcast_to(lax.rsqrt(total * (1.0 / width) + eps_norm), (T, C))

    for s in range(8):
        r.means[s:s + 1, :] = jnp.sum(macc[s], axis=0, keepdims=True) * (1.0 / (lq if s < 4 else lp))

    order = GATHERED

    @pl.loop(0, len(order))
    def _(i):
        a, b = pick(i, [o[0] % 4 for o in order]), pick(i, [o[1] % 4 for o in order])
        sib_copy(i, a, b, True).wait_recv()
        chip = chip_of(a, b)
        cols = pl.ds(pl.multiple_of(chip * 2 * depth, 2 * depth), 2 * depth)
        w = W[pl.ds(chip * 2, 2)].reshape(2 * depth, W.shape[2])
        total = jnp.dot(X[:, cols], w, preferred_element_type=f32)
        acc[...] = acc[...] + total
        for at, stage in SUM_STEPS:
            @pl.when(i == at)
            def _():
                stages[stage]()

    assert sib_sent == [(a % 4, b % 4) for a, b in order]

    @pl.loop(0, n_tiles)
    def _(i):
        tile = pl.ds(pl.multiple_of(i * T, T), T)
        r.rows[tile, :] = (acc[tile, :] * scale[tile, 0:1]).astype(bf16)

    tree.finish()
    for i, (a, b) in enumerate(sib_sent):
        sib_copy(i, a, b, False).wait_send()


ORDER = ((2, 2), (2, 1), (2, -1), (1, 2), (-1, 2), (2, 0), (0, 2), (1, 1), (1, -1), (-1, 1), (-1, -1),
         (1, 0), (-1, 0), (0, 1), (0, -1), (0, 0))


def key_of(a, b):
    return a % 4, b % 4


class Fold:
    def __init__(self, part, landed, send_sem, recv_sem):
        self.part, self.landed, self.send_sem, self.recv_sem = part, landed, send_sem, recv_sem
        self.sends, self.pieces, self.used, self.waited = [], {}, 0, set()
        self.index = {key_of(a, b): i for i, (a, b) in enumerate(ORDER)}

    def copy(self, i):
        a, b, lo, n, dx, dz, off = self.sends[i]
        return pltpu.make_async_remote_copy(
            src_ref=self.part.at[self.index[key_of(a, b)], pl.ds(lo, n)], dst_ref=self.landed.at[pl.ds(off, n)],
            send_sem=self.send_sem.at[i], recv_sem=self.recv_sem.at[i],
            device_id=dev(dx, dz), device_id_type=MESH)

    def send(self, a, b, lo, n, dx, dz):
        i = len(self.sends)
        self.sends.append((a, b, lo, n, dx, dz, self.used))
        self.used += n
        self.pieces[(*key_of(a - dx, b - dz), lo, n, *key_of(-dx, -dz))] = i
        self.copy(i).start()

    def recv(self, a, b, lo, n, dx, dz):
        i = self.pieces[(*key_of(a, b), lo, n, *key_of(dx, dz))]
        self.copy(i).wait_recv()
        self.waited.add(i)
        off = self.sends[i][6]
        return self.landed.at[pl.ds(off, n)]

    def add(self, a, b, lo, n, *froms):
        at = self.index[key_of(a, b)]
        for m, (dx, dz) in froms:
            piece = self.recv(a, b, m[0], m[1], dx, dz)
            cut = piece.shape[1] // 2

            @pl.loop(0, 2 * m[1])
            def _(n):
                q, rows = n // 2, pl.ds(pl.multiple_of(n % 2 * cut, cut), cut)
                self.part[at, m[0] + q, rows, :] = self.part[at, m[0] + q, rows, :] + piece[q, rows, :]

    def finish(self):
        assert self.waited == set(range(len(self.sends))), (len(self.waited), len(self.sends))
        for i in range(len(self.sends)):
            self.copy(i).wait_send()


def ends(fold, a, b, half):
    if half == 0:
        fold.send(a, b, 0, 1, 0, -1)
        fold.send(a, b, 1, 1, 0, 1)
    else:
        fold.send(a, b, 2, 1, -1, 0)
        fold.send(a, b, 3, 1, 1, 0)


def fold_steps(fold):
    def first(i):
        a, b = ORDER[i]
        if (a, b) == (2, 2):
            ends(fold, a, b, 0)
            ends(fold, a, b, 1)
        elif a == 2:
            ends(fold, a, b, 1)
        elif b == 2:
            ends(fold, a, b, 0)
        elif a and b:
            q = up(-b)
            fold.add(a, b, 0, 2, ((q, 1), (0, -b)))
            fold.send(a, b, 0, 2, 0, b)
            q = 2 + up(-a)
            fold.add(a, b, 2, 2, ((q, 1), (-a, 0)))
            fold.send(a, b, 2, 2, a, 0)

    def second():
        for s in (1, -1):
            fold.add(2, s, 0, 2, ((up(-s), 1), (0, -s)))
            fold.send(2, s, 0, 2, 0, s)
            fold.add(s, 2, 2, 2, ((2 + up(-s), 1), (-s, 0)))
            fold.send(s, 2, 2, 2, s, 0)

    def third():
        fold.add(2, 0, 0, 2, ((0, 2), (0, 1)), ((0, 2), (0, -1)))
        fold.send(2, 0, 0, 1, -1, 0)
        fold.send(2, 0, 1, 1, 1, 0)
        fold.add(0, 2, 2, 2, ((2, 2), (1, 0)), ((2, 2), (-1, 0)))
        fold.send(0, 2, 2, 1, 0, -1)
        fold.send(0, 2, 3, 1, 0, 1)

    def fourth():
        for s in (1, -1):
            fold.add(s, 0, 2, 2, ((2 + up(-s), 1), (-s, 0)))
            fold.send(s, 0, 2, 2, s, 0)
            fold.add(0, s, 0, 2, ((up(-s), 1), (0, -s)))
            fold.send(0, s, 0, 2, 0, s)

    def fifth():
        for s in (1, -1):
            fold.add(s, 0, 0, 2, ((0, 2), (0, 1)), ((0, 2), (0, -1)), ((up(-s), 1), (-s, 0)))
            fold.send(s, 0, 0, 2, s, 0)
            fold.add(0, s, 2, 2, ((2, 2), (1, 0)), ((2, 2), (-1, 0)), ((2 + up(-s), 1), (0, -s)))
            fold.send(0, s, 2, 2, 0, s)

    steps = {i: [functools.partial(first, i)] for i in range(11)}
    steps[6].append(second)
    steps[11] = [third]
    steps[14] = [fourth, fifth]
    return steps


NT = (((1,), (1,)), ((), ()))
EXACT = lax.Precision.HIGHEST
AROUND = tuple((a, b) for a in (1, 3, 0, 2) for b in (1, 3, 0, 2) if (a, b) != (0, 0))


def block_of(row, n):
    H = HEAD_DIM
    return pl.ds(pl.multiple_of((row + n // 6) * H, H), H), slice(n % 6 * H, (n % 6 + 1) * H)


def attend_forward(rows, att, wts, pooled, base, blocks, row, seq, groups):
    H = HEAD_DIM
    key_at, value_at = groups * H, (groups + 1) * H
    L = blocks * H
    k = rows[pl.ds(base, L), key_at:key_at + H]
    v = rows[pl.ds(base, L), value_at:value_at + H].astype(f32)
    causal = iota((H, H), 0) <= iota((H, H), 1)
    n = 0
    for h in range(groups):
        w = [None] * blocks
        for ib in range(blocks):
            q = rows[pl.ds(pl.multiple_of(base + ib * H, H), H), h * H:(h + 1) * H]
            e = []
            for jb in range(ib + 1):
                st = lax.dot_general(k[jb * H:(jb + 1) * H], q, NT, preferred_element_type=f32)
                st = jnp.exp(st * (1.0 / math.sqrt(H)))
                e.append(jnp.where(causal, st, 0.0) if jb == ib else st)
            total = jnp.sum(e[0], axis=0, keepdims=True)
            for one in e[1:]:
                total = total + jnp.sum(one, axis=0, keepdims=True)
            r = 1.0 / total
            for jb in range(ib + 1):
                at = e[jb] * r
                att[block_of(row, n)] = at
                n += 1
                w[jb] = at if w[jb] is None else w[jb] + at
        out = None
        for jb in range(blocks):
            col = jnp.sum(w[jb], axis=1, keepdims=True) * (1.0 / L)
            wts[pl.ds(pl.multiple_of(base + jb * H, H), H), h:h + 1] = col
            part = jnp.sum(col * v[jb * H:(jb + 1) * H], axis=0, keepdims=True)
            out = part if out is None else out + part
        pooled[seq, :, h * H:(h + 1) * H] = jnp.broadcast_to(out, (8, H))


def attend_backward(rows, scale, att, wts, ups, dgt, base, blocks, row, seq, groups):
    H = HEAD_DIM
    key_at, value_at = groups * H, (groups + 1) * H
    L = blocks * H
    k = rows[pl.ds(base, L), key_at:key_at + H]
    v = rows[pl.ds(base, L), value_at:value_at + H].astype(f32)
    kt = k.astype(f32).T.astype(bf16)
    dk, dv = [None] * blocks, [None] * blocks
    eye = iota((H, H), 0) == iota((H, H), 1)
    along = []
    for jb in range(blocks):
        column = scale[pl.ds(pl.multiple_of(base + jb * H, H), H), 0:1]
        along.append(jnp.sum(jnp.where(eye, column, 0.0), axis=0, keepdims=True))
    n = 0
    for h in range(groups):
        u = ups[seq, :, h * H:(h + 1) * H][0:1]
        c = [jnp.sum(v[jb * H:(jb + 1) * H] * u, axis=1, keepdims=True) * (1.0 / L) for jb in range(blocks)]
        for ib in range(blocks):
            span = pl.ds(pl.multiple_of(base + ib * H, H), H)
            q = rows[span, h * H:(h + 1) * H]
            at = [att[block_of(row, n + jb)] for jb in range(ib + 1)]
            n += ib + 1
            m = None
            for jb in range(ib + 1):
                part = jnp.sum(at[jb] * c[jb], axis=0, keepdims=True)
                m = part if m is None else m + part
            dq = None
            for jb in range(ib + 1):
                ds = (at[jb] * ((c[jb] - m) * (1.0 / math.sqrt(H)))).astype(bf16)
                part = jnp.dot(kt[:, jb * H:(jb + 1) * H], ds, preferred_element_type=f32)
                dq = part if dq is None else dq + part
                part = jnp.dot(ds, q, preferred_element_type=f32)
                dk[jb] = part if dk[jb] is None else dk[jb] + part
            dgt[h * H:(h + 1) * H, span] = (dq * along[ib]).astype(bf16)
        for jb in range(blocks):
            part = wts[pl.ds(pl.multiple_of(base + jb * H, H), H), h:h + 1] * u
            dv[jb] = part if dv[jb] is None else dv[jb] + part
    for jb in range(blocks):
        span = pl.ds(pl.multiple_of(base + jb * H, H), H)
        dgt[key_at:key_at + H, span] = (dk[jb].T * along[jb]).astype(bf16)
        dgt[value_at:value_at + H, span] = (dv[jb].T * along[jb]).astype(bf16)


def middle_part(r):
    lq, lp = r.xq.shape[0] // 4, r.xp.shape[0] // 4
    rows, scale, means, wout, att, wts = r.rows, r.scale, r.means, r.wout, r.acc, r.wts
    pooled, ups, terms, got, embeds, qs, ps = r.pooled, r.ups, r.terms, r.got, r.embeds, r.qs, r.ps
    gram, dl, dlt, raws, dgt, loss, owner, place_in = (
        r.gram, r.dl, r.dlt, r.raws, r.dgt, r.loss, r.owner, r.place_in)
    asem, arecv, bsem, brecv, sibs, sibr = r.asend, r.arecv, r.bsend, r.brecv, r.msibs, r.msibr
    csem, crecv, dsem, drecv = r.csend, r.crecv, r.dsend, r.drecv
    H = HEAD_DIM
    groups = rows.shape[1] // H - 2
    width = wout.shape[1]
    seqs = 4
    nt = 4
    part_w = width // nt
    x, z, core = place()
    t = lax.axis_index("tensor")
    base_p = seqs * lq
    bq, bp = lq // H, lp // H

    @pl.loop(0, seqs, unroll=seqs)
    def _(s):
        attend_forward(rows, att, wts, pooled, pl.multiple_of(s * lq, H), bq, s, s, groups)

    @pl.loop(0, seqs, unroll=seqs)
    def _(s):
        attend_forward(rows, att, wts, pooled, pl.multiple_of(base_p + s * lp, H), bp, seqs + 2 * s, seqs + s, groups)

    pltpu.make_async_copy(r.wout_hbm, wout, r.osem).wait()
    row = iota((8, groups * H), 0)
    low = pooled[0]
    for s in range(1, 8):
        low = jnp.where(row == s, pooled[s], low)
    low = low.astype(bf16)

    def y_copy(src, dst, d, send_sem, recv_sem):
        return pltpu.make_async_remote_copy(
            src_ref=src, dst_ref=dst, send_sem=send_sem.at[d - 1], recv_sem=recv_sem.at[d - 1],
            device_id={"tensor": (t + d) % nt}, device_id_type=MESH)

    def term(o):
        cols = pl.ds(pl.multiple_of(o * part_w, part_w), part_w)
        return jnp.dot(low, wout[:, cols], preferred_element_type=f32)

    def folded(value):
        return jnp.concatenate([value[:, :part_w // 2], value[:, part_w // 2:]], axis=0).astype(bf16)

    def unfolded(value):
        value = value.astype(f32)
        return jnp.concatenate([value[:8], value[8:]], axis=1)

    a_copies = []
    for d in (2, 1, 3):
        terms[d] = folded(term((t + d) % nt))
        copy = y_copy(terms.at[d], got.at[d], d, asem, arecv)
        copy.start()
        a_copies.append(copy)
    mine = term(t) + means[:, pl.ds(pl.multiple_of(t * part_w, part_w), part_w)]
    n_rows = qs.shape[0]
    ids = owner[...] * seqs + place_in[...]
    col = iota((n_rows, n_rows), 1)
    counts = jnp.zeros((n_rows, n_rows), f32)
    for j in range(ids.shape[0]):
        counts = counts + jnp.where(ids[j:j + 1, :] == iota((n_rows, n_rows), 0), 1.0, 0.0)
    counts = counts.T
    for copy in a_copies:
        copy.wait_recv()
    mine = mine + unfolded(got[1]) + unfolded(got[2]) + unfolded(got[3])
    here = slot_of(0, 0)
    embeds[here] = mine

    def b_copy(n, a, b):
        view = embeds.at[here]
        return pltpu.make_async_remote_copy(
            src_ref=view, dst_ref=view, send_sem=bsem.at[n], recv_sem=brecv.at[n],
            device_id=dev(a, b), device_id_type=MESH)

    def s_copy(n, a, b, flip):
        view = embeds.at[slot_of(a, b, flip=flip)]
        return pltpu.make_async_remote_copy(
            src_ref=view, dst_ref=view, send_sem=sibs.at[n], recv_sem=sibr.at[n],
            device_id=dev(0, 0, flip=True), device_id_type=MESH)

    for n, (a, b) in enumerate(AROUND):
        b_copy(n, a, b).start()
    s_copy(15, 0, 0, False).start()
    for n, (a, b) in enumerate(AROUND):
        view = embeds.at[slot_of(-a, -b)]
        pltpu.make_async_remote_copy(
            src_ref=view, dst_ref=view, send_sem=bsem.at[n], recv_sem=brecv.at[n],
            device_id=dev(a, b), device_id_type=MESH).wait_recv()
        s_copy(n, -a, -b, False).start()
    s_copy(15, 0, 0, True).wait_recv()
    for n, (a, b) in enumerate(AROUND):
        s_copy(n, -a, -b, True).wait_recv()

    first = iota((8, part_w), 0) < seqs

    @pl.loop(0, n_rows // 8)
    def _(k):
        one, two = embeds[2 * k], embeds[2 * k + 1]
        span = pl.ds(pl.multiple_of(k * 8, 8), 8)
        qs[span, :] = jnp.where(first, one, pltpu.roll(two, seqs, 0))
        ps[span, :] = jnp.where(first, pltpu.roll(one, seqs, 0), two)

    q, p = qs[...], ps[...]
    gram[0, pl.ds(0, n_rows), :] = lax.dot_general(q, p, NT, precision=EXACT, preferred_element_type=f32)
    eye = iota((n_rows, n_rows), 0) == col

    def squares(value):
        column = jnp.sum(value * value, axis=1, keepdims=True)
        return jnp.broadcast_to(jnp.sum(jnp.where(eye, column, 0.0), axis=0, keepdims=True), (8, n_rows))

    gram[0, pl.ds(n_rows, 8), :] = squares(q)
    gram[0, pl.ds(n_rows + 8, 8), :] = squares(p)
    c_copies = []
    for d in (2, 1, 3):
        copy = y_copy(gram.at[0], gram.at[d], d, csem, crecv)
        copy.start()
        c_copies.append(copy)
    for copy in c_copies:
        copy.wait_recv()
    whole = (gram[0] + gram[2]) + (gram[1] + gram[3])
    inv = lax.rsqrt(whole[n_rows:] + eps_unit)
    inv_q_row, inv_p_row = inv[0:1], inv[8:9]
    inv_q = jnp.sum(jnp.where(eye, inv_q_row, 0.0), axis=1, keepdims=True)
    inv_p = jnp.sum(jnp.where(eye, inv_p_row, 0.0), axis=1, keepdims=True)
    cosine = whole[:n_rows] * inv_q * inv_p_row
    logits = cosine * (1.0 / sharpness_divisor)
    raised = jnp.exp(logits) * (1.0 + counts)
    sums = jnp.sum(raised, axis=1, keepdims=True)
    diagonal = jnp.sum(jnp.where(eye, logits, 0.0), axis=1, keepdims=True)
    loss[...] = jnp.sum(jnp.log(sums) - diagonal, axis=0, keepdims=True) * (1.0 / n_rows)
    slope = (raised / sums - jnp.where(eye, 1.0, 0.0)) * (1.0 / sharpness_divisor)
    dl[0] = slope
    dlt[0] = slope.T
    weighted = slope * cosine
    dl[1] = jnp.broadcast_to(jnp.sum(weighted, axis=1, keepdims=True), (n_rows, n_rows))
    dlt[1] = jnp.broadcast_to(jnp.sum(weighted, axis=0, keepdims=True), (n_rows, n_rows)).T
    dl[2] = jnp.broadcast_to(inv_q, (n_rows, n_rows))
    dlt[2] = jnp.broadcast_to(inv_p, (n_rows, n_rows))
    chip = pl.ds(pl.multiple_of(chip_of(0, 0) * 8, 8), 8)

    def back(table, own, others, scale):
        d = jnp.dot(table[0, chip, :], others * scale, precision=EXACT, preferred_element_type=f32)
        inverse = table[2, chip, :][:, 0:1]
        e = own[chip, :] * inverse
        return inverse * (d - e * table[1, chip, :][:, 0:1])

    rq = back(dl, qs, p, inv_p)
    rp = back(dlt, ps, q, inv_q)
    left = core == 0
    rq = jnp.where(left, rq, pltpu.roll(rq, seqs, 0))
    rp = jnp.where(left, pltpu.roll(rp, seqs, 0), rp)
    raws[t] = folded(jnp.where(first, rq, rp))
    d_copies = []
    for d in (2, 1, 3):
        copy = y_copy(raws.at[t], raws.at[t], d, dsem, drecv)
        copy.start()
        d_copies.append(copy)
    total = None
    for d in (0, 1, 3, 2):
        o = (t - d) % nt
        if d:
            y_copy(raws.at[o], raws.at[o], d, dsem, drecv).wait_recv()
        cols = pl.ds(pl.multiple_of(o * part_w, part_w), part_w)
        part = lax.dot_general(unfolded(raws[o]).astype(bf16), wout[:, cols], NT, preferred_element_type=f32)
        total = part if total is None else total + part
    for s in range(8):
        ups[s] = jnp.broadcast_to(total[s:s + 1], (8, groups * H))

    @pl.loop(0, seqs, unroll=seqs)
    def _(s):
        attend_backward(rows, scale, att, wts, ups, dgt, pl.multiple_of(s * lq, H), bq, s, s, groups)

    @pl.loop(0, seqs, unroll=seqs)
    def _(s):
        attend_backward(rows, scale, att, wts, ups, dgt, pl.multiple_of(base_p + s * lp, H), bp,
                        seqs + 2 * s, seqs + s, groups)

    for copy in a_copies + c_copies + d_copies:
        copy.wait_send()
    for n, (a, b) in enumerate(AROUND):
        b_copy(n, a, b).wait_send()
        s_copy(n, -a, -b, False).wait_send()
    s_copy(15, 0, 0, False).wait_send()


def scatter_part(r):
    part, both, sib, landed = r.part, r.both, r.sib, r.landed
    ssem, rsem, sibs, sibr = r.fsend, r.frecv, r.fsibs, r.fsibr
    depth = 2 * r.out.shape[1]
    qr = part.shape[2]
    half = depth // 2
    core = place()[2]
    own = pl.ds(pl.multiple_of(core * half, half), half)
    other = pl.ds(pl.multiple_of((1 - core) * half, half), half)

    def sib_copy(i):
        return pltpu.make_async_remote_copy(
            src_ref=both.at[i, :, :, other], dst_ref=sib.at[i], send_sem=sibs.at[i], recv_sem=sibr.at[i],
            device_id=dev(0, 0, flip=True), device_id_type=MESH)

    fold = Fold(part, landed, ssem, rsem)
    steps = fold_steps(fold)

    n = len(ORDER) // 2

    @pl.loop(0, n + 1)
    def _(i):
        @pl.when(i < n)
        def _():
            for k in (2 * i, 2 * i + 1):
                chip = chip_of(pick(k, [o[0] % 4 for o in ORDER]), pick(k, [o[1] % 4 for o in ORDER]))
                cols = pl.ds(pl.multiple_of(chip * depth, depth), depth)
                total = jnp.dot(r.dgt[...], r.X[:, cols], preferred_element_type=f32).astype(bf16)
                both[k] = total.reshape(4, qr, depth)
            for k in (2 * i, 2 * i + 1):
                sib_copy(k).start()

        @pl.when(i > 0)
        def _():
            for k in (2 * i - 2, 2 * i - 1):
                sib_copy(k).wait_recv()
            for k in (2 * i - 2, 2 * i - 1):
                part[k] = both[k, :, :, own] + sib[k]

        for m in range(n):
            @pl.when(i == m + 1)
            def _():
                for at in (2 * m, 2 * m + 1):
                    for step in steps.get(at, ()):
                        step()

    for side in (0, 1):
        total = part[15, pl.ds(2 * side, 2)].astype(f32)
        for dx, dz in ((1, 0), (-1, 0), (0, 1), (0, -1)):
            total = total + fold.recv(0, 0, 2 * side, 2, dx, dz)[...].astype(f32)
        r.out[pl.ds(side * 2 * qr, 2 * qr), :] = total.reshape(2 * qr, half)
    fold.finish()
    for i in range(16):
        sib_copy(i).wait_send()


def finish_kernel(sums, gain, gq, gk, gv):
    H = HEAD_DIM
    depth = sums.shape[1]
    own = gain[:, pl.ds(pl.multiple_of(slot_of(0, 0) * depth, depth), depth)]
    heads = gq.shape[1] // H
    for n in range(heads + 2):
        block = (sums[n * H:(n + 1) * H, :] * own).T
        if n < heads:
            gq[:, n * H:(n + 1) * H] = block
        elif n == heads:
            gk[...] = block
        else:
            gv[...] = block


def finish(sums, gain):
    rows, depth = sums.shape
    cols = (rows - 2 * HEAD_DIM, HEAD_DIM, HEAD_DIM)
    VM = pl.BlockSpec(memory_space=pltpu.VMEM)
    return pl.pallas_call(
        finish_kernel,
        out_shape=tuple(jax.ShapeDtypeStruct((depth, n), f32) for n in cols),
        in_specs=[VM, VM],
        out_specs=(VM, VM, VM),
        name="finish_rows",
    )(sums, gain.reshape(1, -1))


def peers():
    t = lax.axis_index("tensor")
    return [{"tensor": (t + d) % 4} for d in (1, 2, 3)] + [dev(a, b) for a, b in AROUND] + [dev(0, 0, flip=True)]


def step_kernel(names, *refs):
    r = types.SimpleNamespace(**dict(zip(names, refs, strict=True)))
    barrier = pltpu.get_barrier_semaphore()
    for peer in peers():
        pl.semaphore_signal(barrier, inc=1, device_id=peer, device_id_type=MESH)
    gather_part(r)
    middle_part(r)
    scatter_part(r)


def step(xq, xp, gain, wq, wk, wv, w_out, owner, place_in):
    tokens, width = xq.shape[0] + xp.shape[0], xq.shape[1]
    depth, heads = wq.shape
    cols = heads + wk.shape[1] + wv.shape[1]
    n = owner.shape[1]
    H = HEAD_DIM
    ANY, VM = pl.BlockSpec(memory_space=pl.ANY), pl.BlockSpec(memory_space=pltpu.VMEM)

    def dma(*shape):
        return pltpu.SemaphoreType.DMA(shape)

    ins = dict(xq=ANY, xp=ANY, gain=VM, wq=ANY, wk=ANY, wv=ANY, wout_hbm=ANY, owner=VM, place_in=VM)
    outs = dict(out=jax.ShapeDtypeStruct((cols, depth), f32), loss=jax.ShapeDtypeStruct((1, 1), f32))
    scratch = dict(
        W=pltpu.VMEM((32, depth, cols), bf16), held=pltpu.VMEM((depth, cols), bf16),
        X=pltpu.VMEM((tokens, width), bf16), acc=pltpu.VMEM((tokens, cols), f32),
        macc=pltpu.VMEM((8, 8, width), f32), rows=pltpu.VMEM((tokens, cols), bf16),
        scale=pltpu.VMEM((tokens, H), f32), means=pltpu.VMEM((8, width), f32),
        wout=pltpu.VMEM(w_out.shape, bf16), wts=pltpu.VMEM((tokens, H), f32),
        pooled=pltpu.VMEM((8, 8, heads), f32), ups=pltpu.VMEM((8, 8, heads), f32),
        terms=pltpu.VMEM((4, 16, width // 8), bf16), got=pltpu.VMEM((4, 16, width // 8), bf16),
        embeds=pltpu.VMEM((32, 8, width // 4), f32),
        qs=pltpu.VMEM((n, width // 4), f32), ps=pltpu.VMEM((n, width // 4), f32),
        gram=pltpu.VMEM((4, n + 16, n), f32), dl=pltpu.VMEM((3, n, n), f32), dlt=pltpu.VMEM((3, n, n), f32),
        raws=pltpu.VMEM((4, 16, width // 8), bf16), dgt=pltpu.VMEM((cols, tokens), bf16),
        part=pltpu.VMEM((16, 4, cols // 4, depth), bf16), both=pltpu.VMEM((16, 4, cols // 4, 2 * depth), bf16),
        sib=pltpu.VMEM((16, 4, cols // 4, depth), bf16), landed=pltpu.VMEM((60, cols // 4, depth), bf16),
        wsem=dma(3), xsem=dma(tokens // 128), osem=dma(),
        gsend=dma(40), grecv=dma(40), gsibs=dma(16), gsibr=dma(16),
        asend=dma(3), arecv=dma(3), bsend=dma(15), brecv=dma(15), msibs=dma(16), msibr=dma(16),
        csend=dma(3), crecv=dma(3), dsend=dma(3), drecv=dma(3),
        fsend=dma(40), frecv=dma(40), fsibs=dma(16), fsibr=dma(16))
    return pl.pallas_call(
        functools.partial(step_kernel, (*ins, *outs, *scratch)),
        out_shape=tuple(outs.values()),
        in_specs=list(ins.values()),
        out_specs=(VM, VM),
        scratch_shapes=list(scratch.values()),
        compiler_params=pltpu.CompilerParams(
            collective_id=0, has_side_effects=True, vmem_limit_bytes=VMEM_LIMIT),
        cost_estimate=pl.CostEstimate(flops=4 * tokens * width * cols, bytes_accessed=2 * tokens * width,
                                      transcendentals=0),
        name="contrast_step",
    )(xq, xp, gain.reshape(1, -1), wq, wk, wv, w_out, owner, place_in)


def body(
    query_states, passage_states, norm_gain, w_query, w_key, w_value, w_out, neg_owner, neg_slot
):
    owned, query_length, _ = query_states.shape
    passage_length = passage_states.shape[1]
    xq = query_states.reshape(owned * query_length, -1)
    xp = passage_states.reshape(owned * passage_length, -1)
    sums, loss = step(xq, xp, norm_gain, w_query, w_key, w_value, w_out, neg_owner.T, neg_slot.T)
    return (loss[0, 0], *finish(sums, norm_gain))


def solution(mesh):
    in_specs = (
        P("dp", None, None),
        P("dp", None, None),
        P(),
        P("dp", "tensor"),
        P("dp", "tensor"),
        P("dp", "tensor"),
        P("tensor", None),
        P(),
        P(),
    )
    out_specs = (P(), P("dp", "tensor"), P("dp", "tensor"), P("dp", "tensor"))
    return jax.shard_map(body, mesh=mesh, in_specs=in_specs, out_specs=out_specs, check_vma=False)
```

```python
import functools
import math
import types

import jax
import jax.numpy as jnp
from jax import lax
from jax.experimental import pallas as pl
from jax.experimental.pallas import tpu as pltpu
from jax.sharding import PartitionSpec as P

HEAD_DIM = 128
eps_norm = 1e-06
eps_unit = 1e-06
sharpness_divisor = 0.05
MESH = pl.DeviceIdType.MESH
f32, bf16 = jnp.float32, jnp.bfloat16
XS, ZS = 4, 4
STAT_STEPS = ((7, 1), (11, 2))
SUM_STEPS = ((0, 3), (4, 4), (6, 5), (8, 6), (13, 7))
VMEM_LIMIT = 63 * 1024 * 1024


def iota(shape, dim):
    return lax.broadcasted_iota(jnp.int32, shape, dim)


HERE = {}


def place():
    if "at" in HERE:
        return HERE["at"]
    p = lax.axis_index("dp")
    return p // (2 * ZS), (p // 2) % ZS, p % 2


def settle():
    HERE.clear()
    x, z, c = place()
    HERE.update(at=(x, z, c), xs=[(x + a) % XS for a in range(XS)], zs=[(z + b) % ZS for b in range(ZS)], other=1 - c)


def chip_of(a, b):
    if "at" in HERE and isinstance(a, int) and isinstance(b, int):
        return HERE["xs"][a % XS] * ZS + HERE["zs"][b % ZS]
    x, z, _ = place()
    return (x + a) % XS * ZS + (z + b) % ZS


def slot_of(a, b, flip=False):
    c = place()[2]
    if flip:
        c = HERE.get("other", 1 - c)
    return chip_of(a, b) * 2 + c


def dev(a, b, flip=False):
    return {"dp": slot_of(a, b, flip=flip)}


GATHERED = ((0, 0), (1, 0), (0, 1), (-1, 0), (0, -1), (1, 1), (1, -1), (-1, 1), (-1, -1), (2, 0), (0, 2),
            (2, 1), (1, 2), (2, -1), (-1, 2), (2, 2))


def pick(i, values):
    out = values[0]
    for n, value in enumerate(values[1:], 1):
        out = jnp.where(i == n, value, out)
    return out


class Tree:
    def __init__(self, buf, rows, send_sem, recv_sem):
        self.buf, self.rows, self.send_sem, self.recv_sem = buf, rows, send_sem, recv_sem
        self.sends, self.pieces, self.waited = [], {}, set()

    def view(self, a, b, lo, n):
        return self.buf.at[slot_of(a, b), pl.ds(lo * self.rows, n * self.rows)]

    def copy(self, i):
        a, b, lo, n, dx, dz = self.sends[i]
        view = self.view(a, b, lo, n)
        return pltpu.make_async_remote_copy(
            src_ref=view, dst_ref=view, send_sem=self.send_sem.at[i], recv_sem=self.recv_sem.at[i],
            device_id=dev(dx, dz), device_id_type=MESH)

    def send(self, a, b, lo, n, dx, dz):
        i = len(self.sends)
        self.sends.append((a, b, lo, n, dx, dz))
        self.pieces[((a - dx) % 4, (b - dz) % 4, lo, n)] = i
        self.copy(i).start()

    def wait(self, a, b, lo, n):
        i = self.pieces[(a % 4, b % 4, lo, n)]
        view = self.view(a, b, lo, n)
        pltpu.make_async_remote_copy(
            src_ref=view, dst_ref=view, send_sem=self.send_sem.at[i], recv_sem=self.recv_sem.at[i],
            device_id=dev(1, 0), device_id_type=MESH).wait_recv()
        self.waited.add(i)

    def finish(self):
        assert self.waited == set(range(len(self.sends)))
        for i in range(len(self.sends)):
            self.copy(i).wait_send()


def up(d):
    return 0 if d > 0 else 1


def gather_stages(tree, sibling):
    def first():
        for d in (1, -1):
            tree.send(0, 0, 0, 2, d, 0)
            tree.send(0, 0, 2, 2, 0, d)
        for d in (1, -1):
            tree.send(0, 0, 2, 2, d, 0)
            tree.send(0, 0, 0, 2, 0, d)
        sibling(0, 0)

    def second():
        for s in (1, -1):
            tree.wait(s, 0, 0, 2)
            tree.send(s, 0, up(-s), 1, -s, 0)
            tree.wait(0, s, 2, 2)
            tree.send(0, s, 2 + up(-s), 1, 0, -s)
        for s in (1, -1):
            for d in (1, -1):
                tree.send(s, 0, 0, 2, 0, d)
                tree.send(0, s, 2, 2, d, 0)

    def third():
        for s in (1, -1):
            tree.wait(s, 0, 2, 2)
            tree.send(s, 0, 2 + up(-s), 1, -s, 0)
            tree.wait(0, s, 0, 2)
            tree.send(0, s, up(-s), 1, 0, -s)
        for s in (1, -1):
            sibling(s, 0)
            sibling(0, s)

    def fourth():
        for q in (0, 1):
            tree.wait(2, 0, q, 1)
            tree.wait(0, 2, 2 + q, 1)
        for d in (1, -1):
            tree.send(2, 0, 0, 2, 0, d)
            tree.send(0, 2, 2, 2, d, 0)

    def fifth():
        for sx in (1, -1):
            for sz in (1, -1):
                tree.wait(sx, sz, 0, 2)
                tree.send(sx, sz, up(-sz), 1, 0, -sz)
                tree.wait(sx, sz, 2, 2)
                tree.send(sx, sz, 2 + up(-sx), 1, -sx, 0)
                sibling(sx, sz)

    def sixth():
        for q in (0, 1):
            tree.wait(2, 0, 2 + q, 1)
            tree.wait(0, 2, q, 1)
        sibling(2, 0)
        sibling(0, 2)
        for s in (1, -1):
            tree.wait(2, s, 0, 2)
            tree.send(2, s, up(-s), 1, 0, -s)
            tree.wait(s, 2, 2, 2)
            tree.send(s, 2, 2 + up(-s), 1, -s, 0)

    def seventh():
        for s in (1, -1):
            for q in (0, 1):
                tree.wait(2, s, 2 + q, 1)
                tree.wait(s, 2, q, 1)
            sibling(2, s)
            sibling(s, 2)

    def eighth():
        for q in (0, 1, 2, 3):
            tree.wait(2, 2, q, 1)
        sibling(2, 2)

    return first, second, third, fourth, fifth, sixth, seventh, eighth


def gather_part(r):
    xq, xp, W, X, acc, macc, scale = r.xq, r.xp, r.W, r.X, r.acc, r.macc, r.scale
    wsem, xsem, ssem, rsem, sibs, sibr = r.wsem, r.xsem, r.gsend, r.grecv, r.gsibs, r.gsibr
    lq, lp = xq.shape[0] // 4, xp.shape[0] // 4
    tq, tokens = xq.shape[0], X.shape[0]
    width = X.shape[1]
    depth = W.shape[1]
    T = 128
    mine = slot_of(0, 0)
    loads = []
    lo = 0
    for n, w in enumerate((r.wq, r.wk, r.wv)):
        loads.append(pltpu.make_async_copy(w, r.held.at[:, pl.ds(lo, w.shape[1])], wsem.at[n]))
        lo += w.shape[1]
    for load in loads:
        load.start()
    for i in range(tq // T):
        pltpu.make_async_copy(xq.at[pl.ds(i * T, T)], X.at[pl.ds(i * T, T)], xsem.at[i]).start(priority=1)
    macc[...] = jnp.zeros_like(macc)
    eye = iota((depth, depth), 0) == iota((depth, depth), 1)
    own = r.gain[:, pl.ds(pl.multiple_of(mine * depth, depth), depth)]
    column = jnp.sum(jnp.where(eye, own, 0.0), axis=1, keepdims=True)
    for load in loads:
        load.wait()
    W[mine] = (r.held[...].astype(f32) * column).astype(bf16)
    pl.semaphore_wait(pltpu.get_barrier_semaphore(), len(peers()))

    tree = Tree(W, depth // 4, ssem, rsem)
    sib_sent = []

    def sib_copy(i, a, b, flip):
        view = W.at[slot_of(a, b, flip=flip)]
        return pltpu.make_async_remote_copy(
            src_ref=view, dst_ref=view, send_sem=sibs.at[i], recv_sem=sibr.at[i],
            device_id=dev(0, 0, flip=True), device_id_type=MESH)

    def sibling(a, b):
        sib_copy(len(sib_sent), a, b, False).start()
        sib_sent.append((a % 4, b % 4))

    stages = gather_stages(tree, sibling)
    C = 128
    chunks = width // C
    n_tiles = tokens // T
    n_query = tq // T
    stages[0]()

    @pl.loop(0, n_tiles)
    def _(i):
        pltpu.make_async_copy(xq.at[pl.ds(0, T)], X.at[pl.ds(pl.multiple_of(i * T, T), T)], xsem.at[i]).wait()
        acc[pl.ds(pl.multiple_of(i * T, T), T), :] = jnp.zeros((T, acc.shape[1]), f32)

        @pl.when(i < n_tiles - n_query)
        def _():
            pltpu.make_async_copy(xp.at[pl.ds(pl.multiple_of(i * T, T), T)],
                                  X.at[pl.ds(pl.multiple_of((i + n_query) * T, T), T)],
                                  xsem.at[i + n_query]).start(priority=1)

        per = lp // T
        seq = jnp.where(i < n_query, i // (lq // T), 4 + (i - n_query) // per)

        def step(n, sums):
            span = pl.ds(pl.multiple_of(i * T + n * 16, 16), 16)
            squares, later = [None] * 4, []
            for c in range(chunks):
                v = X[span, c * C:(c + 1) * C].astype(f32)
                w = v * v
                squares[c % 4] = w if squares[c % 4] is None else squares[c % 4] + w
                later.append(sums[c] + (v[0:8] + v[8:16]))
            scale[span, :] = (squares[0] + squares[1]) + (squares[2] + squares[3])
            return tuple(later)

        sums = lax.fori_loop(0, T // 16, step, tuple(
            macc[seq, :, c * C:(c + 1) * C] for c in range(chunks)))
        for c in range(chunks):
            macc[seq, :, c * C:(c + 1) * C] = sums[c]
        for at, stage in STAT_STEPS:
            @pl.when(i == at)
            def _():
                stages[stage]()

    @pl.loop(0, n_tiles)
    def _(i):
        tile = pl.ds(pl.multiple_of(i * T, T), T)
        total = jnp.sum(scale[tile, :], axis=1, keepdims=True)
        scale[tile, :] = jnp.broadcast_to(lax.rsqrt(total * (1.0 / width) + eps_norm), (T, C))

    for s in range(8):
        r.means[s:s + 1, :] = jnp.sum(macc[s], axis=0, keepdims=True) * (1.0 / (lq if s < 4 else lp))

    order = GATHERED

    @pl.loop(0, len(order))
    def _(i):
        a, b = pick(i, [o[0] % 4 for o in order]), pick(i, [o[1] % 4 for o in order])
        sib_copy(i, a, b, True).wait_recv()
        chip = chip_of(a, b)
        cols = pl.ds(pl.multiple_of(chip * 2 * depth, 2 * depth), 2 * depth)
        w = W[pl.ds(chip * 2, 2)].reshape(2 * depth, W.shape[2])
        total = jnp.dot(X[:, cols], w, preferred_element_type=f32)
        acc[...] = acc[...] + total
        for at, stage in SUM_STEPS:
            @pl.when(i == at)
            def _():
                stages[stage]()

    assert sib_sent == [(a % 4, b % 4) for a, b in order]

    @pl.loop(0, n_tiles)
    def _(i):
        tile = pl.ds(pl.multiple_of(i * T, T), T)
        r.rows[tile, :] = (acc[tile, :] * scale[tile, 0:1]).astype(bf16)

    pltpu.make_async_copy(r.wout_hbm, r.wout, r.osem).start(priority=1)

    def sent():
        tree.finish()
        for i, (a, b) in enumerate(sib_sent):
            sib_copy(i, a, b, False).wait_send()

    return sent


ORDER = ((2, 2), (2, 1), (2, -1), (1, 2), (-1, 2), (2, 0), (0, 2), (1, 1), (1, -1), (-1, 1), (-1, -1),
         (1, 0), (-1, 0), (0, 1), (0, -1), (0, 0))


def key_of(a, b):
    return a % 4, b % 4


class Fold:
    def __init__(self, part, landed, send_sem, recv_sem):
        self.part, self.landed, self.send_sem, self.recv_sem = part, landed, send_sem, recv_sem
        self.sends, self.pieces, self.used, self.waited = [], {}, 0, set()
        self.index = {key_of(a, b): i for i, (a, b) in enumerate(ORDER)}

    def copy(self, i):
        a, b, lo, n, dx, dz, off = self.sends[i]
        return pltpu.make_async_remote_copy(
            src_ref=self.part.at[self.index[key_of(a, b)], pl.ds(lo, n)], dst_ref=self.landed.at[pl.ds(off, n)],
            send_sem=self.send_sem.at[i], recv_sem=self.recv_sem.at[i],
            device_id=dev(dx, dz), device_id_type=MESH)

    def send(self, a, b, lo, n, dx, dz):
        i = len(self.sends)
        self.sends.append((a, b, lo, n, dx, dz, self.used))
        self.used += n
        self.pieces[(*key_of(a - dx, b - dz), lo, n, *key_of(-dx, -dz))] = i
        self.copy(i).start()

    def recv(self, a, b, lo, n, dx, dz):
        i = self.pieces[(*key_of(a, b), lo, n, *key_of(dx, dz))]
        self.copy(i).wait_recv()
        self.waited.add(i)
        off = self.sends[i][6]
        return self.landed.at[pl.ds(off, n)]

    def add(self, a, b, lo, n, *froms):
        at = self.index[key_of(a, b)]
        for m, (dx, dz) in froms:
            piece = self.recv(a, b, m[0], m[1], dx, dz)
            cut = piece.shape[1] // 2

            @pl.loop(0, 2 * m[1])
            def _(n):
                q, rows = n // 2, pl.ds(pl.multiple_of(n % 2 * cut, cut), cut)
                self.part[at, m[0] + q, rows, :] = self.part[at, m[0] + q, rows, :] + piece[q, rows, :]

    def finish(self):
        for i in range(len(self.sends)):
            self.copy(i).wait_send()


def ends(fold, a, b, half):
    if half == 0:
        fold.send(a, b, 0, 1, 0, -1)
        fold.send(a, b, 1, 1, 0, 1)
    else:
        fold.send(a, b, 2, 1, -1, 0)
        fold.send(a, b, 3, 1, 1, 0)


def fold_steps(fold):
    def first(i):
        a, b = ORDER[i]
        if (a, b) == (2, 2):
            ends(fold, a, b, 0)
            ends(fold, a, b, 1)
        elif a == 2:
            ends(fold, a, b, 1)
        elif b == 2:
            ends(fold, a, b, 0)
        elif a and b:
            q = up(-b)
            fold.add(a, b, 0, 2, ((q, 1), (0, -b)))
            fold.send(a, b, 0, 2, 0, b)
            q = 2 + up(-a)
            fold.add(a, b, 2, 2, ((q, 1), (-a, 0)))
            fold.send(a, b, 2, 2, a, 0)

    def second():
        for s in (1, -1):
            fold.add(2, s, 0, 2, ((up(-s), 1), (0, -s)))
            fold.send(2, s, 0, 2, 0, s)
            fold.add(s, 2, 2, 2, ((2 + up(-s), 1), (-s, 0)))
            fold.send(s, 2, 2, 2, s, 0)

    def third():
        fold.add(2, 0, 0, 2, ((0, 2), (0, 1)), ((0, 2), (0, -1)))
        fold.send(2, 0, 0, 1, -1, 0)
        fold.send(2, 0, 1, 1, 1, 0)
        fold.add(0, 2, 2, 2, ((2, 2), (1, 0)), ((2, 2), (-1, 0)))
        fold.send(0, 2, 2, 1, 0, -1)
        fold.send(0, 2, 3, 1, 0, 1)

    def fourth():
        for s in (1, -1):
            fold.add(s, 0, 2, 2, ((2 + up(-s), 1), (-s, 0)))
            fold.send(s, 0, 2, 2, s, 0)
            fold.add(0, s, 0, 2, ((up(-s), 1), (0, -s)))
            fold.send(0, s, 0, 2, 0, s)

    def fifth():
        for s in (1, -1):
            fold.add(s, 0, 0, 2, ((0, 2), (0, 1)), ((0, 2), (0, -1)), ((up(-s), 1), (-s, 0)))
            fold.send(s, 0, 0, 2, s, 0)
            fold.add(0, s, 2, 2, ((2, 2), (1, 0)), ((2, 2), (-1, 0)), ((2 + up(-s), 1), (0, -s)))
            fold.send(0, s, 2, 2, 0, s)

    steps = {i: [functools.partial(first, i)] for i in range(11)}
    steps[6].append(second)
    steps[11] = [third]
    steps[14] = [fourth, fifth]
    return steps


NT = (((1,), (1,)), ((), ()))
AROUND = tuple((a, b) for a in (1, 3, 0, 2) for b in (1, 3, 0, 2) if (a, b) != (0, 0))


def fine_dot(a, b, dims):
    def split(value):
        high = value.astype(bf16)
        return high, (value - high.astype(f32)).astype(bf16)

    def dot(one, two):
        return lax.dot_general(one, two, dims, preferred_element_type=f32)

    (ah, al), (bh, bl) = split(a), split(b)
    return dot(ah, bh) + (dot(ah, bl) + dot(al, bh))


def block_of(row, n):
    H = HEAD_DIM
    return pl.ds(pl.multiple_of((row + n // 6) * H, H), H), slice(n % 6 * H, (n % 6 + 1) * H)


def attend_forward(rows, att, wts, pooled, base, blocks, row, seq, groups):
    H = HEAD_DIM
    key_at, value_at = groups * H, (groups + 1) * H
    L = blocks * H
    k = rows[pl.ds(base, L), key_at:key_at + H]
    v = rows[pl.ds(base, L), value_at:value_at + H].astype(f32)
    causal = iota((H, H), 0) <= iota((H, H), 1)
    n = 0
    for h in range(groups):
        w = [None] * blocks
        for ib in range(blocks):
            q = rows[pl.ds(pl.multiple_of(base + ib * H, H), H), h * H:(h + 1) * H]
            e = []
            for jb in range(ib + 1):
                st = lax.dot_general(k[jb * H:(jb + 1) * H], q, NT, preferred_element_type=f32)
                st = jnp.exp(st * (1.0 / math.sqrt(H)))
                e.append(jnp.where(causal, st, 0.0) if jb == ib else st)
            total = jnp.sum(e[0], axis=0, keepdims=True)
            for one in e[1:]:
                total = total + jnp.sum(one, axis=0, keepdims=True)
            r = 1.0 / total
            for jb in range(ib + 1):
                at = e[jb] * r
                att[block_of(row, n)] = at
                n += 1
                w[jb] = at if w[jb] is None else w[jb] + at
        out = None
        for jb in range(blocks):
            col = jnp.sum(w[jb], axis=1, keepdims=True) * (1.0 / L)
            wts[pl.ds(pl.multiple_of(base + jb * H, H), H), h:h + 1] = col
            part = jnp.sum(col * v[jb * H:(jb + 1) * H], axis=0, keepdims=True)
            out = part if out is None else out + part
        pooled[seq, :, h * H:(h + 1) * H] = jnp.broadcast_to(out, (8, H))


def attend_backward(rows, scale, att, wts, ups, dgt, base, blocks, row, seq, groups):
    H = HEAD_DIM
    key_at, value_at = groups * H, (groups + 1) * H
    L = blocks * H
    k = rows[pl.ds(base, L), key_at:key_at + H]
    v = rows[pl.ds(base, L), value_at:value_at + H].astype(f32)
    kt = k.astype(f32).T.astype(bf16)
    dk, dv = [None] * blocks, [None] * blocks
    eye = iota((H, H), 0) == iota((H, H), 1)
    along = []
    for jb in range(blocks):
        column = scale[pl.ds(pl.multiple_of(base + jb * H, H), H), 0:1]
        along.append(jnp.sum(jnp.where(eye, column, 0.0), axis=0, keepdims=True))
    n = 0
    for h in range(groups):
        u = ups[seq, :, h * H:(h + 1) * H][0:1]
        c = [jnp.sum(v[jb * H:(jb + 1) * H] * u, axis=1, keepdims=True) * (1.0 / L) for jb in range(blocks)]
        for ib in range(blocks):
            span = pl.ds(pl.multiple_of(base + ib * H, H), H)
            q = rows[span, h * H:(h + 1) * H]
            at = [att[block_of(row, n + jb)] for jb in range(ib + 1)]
            n += ib + 1
            m = None
            for jb in range(ib + 1):
                part = jnp.sum(at[jb] * c[jb], axis=0, keepdims=True)
                m = part if m is None else m + part
            dq = None
            for jb in range(ib + 1):
                ds = (at[jb] * ((c[jb] - m) * (1.0 / math.sqrt(H)))).astype(bf16)
                part = jnp.dot(kt[:, jb * H:(jb + 1) * H], ds, preferred_element_type=f32)
                dq = part if dq is None else dq + part
                part = jnp.dot(ds, q, preferred_element_type=f32)
                dk[jb] = part if dk[jb] is None else dk[jb] + part
            dgt[h * H:(h + 1) * H, span] = (dq * along[ib]).astype(bf16)
        for jb in range(blocks):
            part = wts[pl.ds(pl.multiple_of(base + jb * H, H), H), h:h + 1] * u
            dv[jb] = part if dv[jb] is None else dv[jb] + part
    for jb in range(blocks):
        span = pl.ds(pl.multiple_of(base + jb * H, H), H)
        dgt[key_at:key_at + H, span] = (dk[jb].T * along[jb]).astype(bf16)
        dgt[value_at:value_at + H, span] = (dv[jb].T * along[jb]).astype(bf16)


def middle_part(r, sent):
    lq, lp = r.xq.shape[0] // 4, r.xp.shape[0] // 4
    rows, scale, means, wout, att, wts = r.rows, r.scale, r.means, r.wout, r.acc, r.wts
    pooled, ups, terms, got, embeds, qs, ps = r.pooled, r.ups, r.terms, r.got, r.embeds, r.qs, r.ps
    gram, dl, dlt, raws, dgt, loss, owner, place_in = (
        r.gram, r.dl, r.dlt, r.raws, r.dgt, r.loss, r.owner, r.place_in)
    asem, arecv, bsem, brecv, sibs, sibr = r.asend, r.arecv, r.bsend, r.brecv, r.msibs, r.msibr
    csem, crecv, dsem, drecv = r.csend, r.crecv, r.dsend, r.drecv
    H = HEAD_DIM
    groups = rows.shape[1] // H - 2
    width = wout.shape[1]
    seqs = 4
    nt = 4
    part_w = width // nt
    x, z, core = place()
    t = lax.axis_index("tensor")
    base_p = seqs * lq
    bq, bp = lq // H, lp // H

    @pl.loop(0, seqs, unroll=seqs)
    def _(s):
        attend_forward(rows, att, wts, pooled, pl.multiple_of(s * lq, H), bq, s, s, groups)

    @pl.loop(0, seqs, unroll=seqs)
    def _(s):
        attend_forward(rows, att, wts, pooled, pl.multiple_of(base_p + s * lp, H), bp, seqs + 2 * s, seqs + s, groups)

    pltpu.make_async_copy(r.wout_hbm, wout, r.osem).wait()
    row = iota((8, groups * H), 0)
    low = pooled[0]
    for s in range(1, 8):
        low = jnp.where(row == s, pooled[s], low)
    low = low.astype(bf16)

    def y_copy(src, dst, d, send_sem, recv_sem):
        return pltpu.make_async_remote_copy(
            src_ref=src, dst_ref=dst, send_sem=send_sem.at[d - 1], recv_sem=recv_sem.at[d - 1],
            device_id={"tensor": (t + d) % nt}, device_id_type=MESH)

    def term(o):
        cols = pl.ds(pl.multiple_of(o * part_w, part_w), part_w)
        return jnp.dot(low, wout[:, cols], preferred_element_type=f32)

    def folded(value):
        return jnp.concatenate([value[:, :part_w // 2], value[:, part_w // 2:]], axis=0).astype(bf16)

    def unfolded(value):
        value = value.astype(f32)
        return jnp.concatenate([value[:8], value[8:]], axis=1)

    a_copies = []
    for d in (2, 1, 3):
        terms[d] = folded(term((t + d) % nt))
        copy = y_copy(terms.at[d], got.at[d], d, asem, arecv)
        copy.start()
        a_copies.append(copy)
    mine = term(t) + means[:, pl.ds(pl.multiple_of(t * part_w, part_w), part_w)]
    n_rows = qs.shape[0]
    ids = owner[...] * seqs + place_in[...]
    col = iota((n_rows, n_rows), 1)
    counts = jnp.zeros((n_rows, n_rows), f32)
    for j in range(ids.shape[0]):
        counts = counts + jnp.where(ids[j:j + 1, :] == iota((n_rows, n_rows), 0), 1.0, 0.0)
    counts = counts.T
    sent()
    for copy in a_copies:
        copy.wait_recv()
    mine = mine + unfolded(got[1]) + unfolded(got[2]) + unfolded(got[3])
    here = slot_of(0, 0)
    embeds[here] = mine

    def b_copy(n, a, b):
        view = embeds.at[here]
        return pltpu.make_async_remote_copy(
            src_ref=view, dst_ref=view, send_sem=bsem.at[n], recv_sem=brecv.at[n],
            device_id=dev(a, b), device_id_type=MESH)

    def s_copy(n, a, b, flip):
        view = embeds.at[slot_of(a, b, flip=flip)]
        return pltpu.make_async_remote_copy(
            src_ref=view, dst_ref=view, send_sem=sibs.at[n], recv_sem=sibr.at[n],
            device_id=dev(0, 0, flip=True), device_id_type=MESH)

    for n, (a, b) in enumerate(AROUND):
        b_copy(n, a, b).start()
    s_copy(15, 0, 0, False).start()
    for n, (a, b) in enumerate(AROUND):
        view = embeds.at[slot_of(-a, -b)]
        pltpu.make_async_remote_copy(
            src_ref=view, dst_ref=view, send_sem=bsem.at[n], recv_sem=brecv.at[n],
            device_id=dev(a, b), device_id_type=MESH).wait_recv()
        s_copy(n, -a, -b, False).start()
    s_copy(15, 0, 0, True).wait_recv()
    for n, (a, b) in enumerate(AROUND):
        s_copy(n, -a, -b, True).wait_recv()

    first = iota((8, part_w), 0) < seqs

    @pl.loop(0, n_rows // 8)
    def _(k):
        one, two = embeds[2 * k], embeds[2 * k + 1]
        span = pl.ds(pl.multiple_of(k * 8, 8), 8)
        qs[span, :] = jnp.where(first, one, pltpu.roll(two, seqs, 0))
        ps[span, :] = jnp.where(first, pltpu.roll(one, seqs, 0), two)

    q, p = qs[...], ps[...]
    gram[0, pl.ds(0, n_rows), :] = fine_dot(q, p, NT)
    eye = iota((n_rows, n_rows), 0) == col

    def squares(value):
        column = jnp.sum(value * value, axis=1, keepdims=True)
        return jnp.sum(jnp.where(eye, column, 0.0), axis=0, keepdims=True)

    gram[0, pl.ds(n_rows, 8), :] = jnp.where(iota((8, n_rows), 0) == 0, squares(q), squares(p))
    c_copies = []
    for d in (2, 1, 3):
        copy = y_copy(gram.at[0], gram.at[d], d, csem, crecv)
        copy.start()
        c_copies.append(copy)
    for copy in a_copies:
        copy.wait_send()
    for n, (a, b) in enumerate(AROUND):
        b_copy(n, a, b).wait_send()
        s_copy(n, -a, -b, False).wait_send()
    s_copy(15, 0, 0, False).wait_send()
    for copy in c_copies:
        copy.wait_recv()
    whole = (gram[0] + gram[2]) + (gram[1] + gram[3])
    inv = lax.rsqrt(whole[n_rows:] + eps_unit)
    inv_q_row, inv_p_row = inv[0:1], inv[1:2]
    inv_q = jnp.sum(jnp.where(eye, inv_q_row, 0.0), axis=1, keepdims=True)
    inv_p = jnp.sum(jnp.where(eye, inv_p_row, 0.0), axis=1, keepdims=True)
    cosine = whole[:n_rows] * inv_q * inv_p_row
    logits = cosine * (1.0 / sharpness_divisor)
    raised = jnp.exp(logits) * (1.0 + counts)
    sums = jnp.sum(raised, axis=1, keepdims=True)
    diagonal = jnp.sum(jnp.where(eye, logits, 0.0), axis=1, keepdims=True)
    loss[...] = jnp.sum(jnp.log(sums) - diagonal, axis=0, keepdims=True) * (1.0 / n_rows)
    slope = (raised / sums - jnp.where(eye, 1.0, 0.0)) * (1.0 / sharpness_divisor)
    dl[0] = slope
    dlt[0] = slope.T
    weighted = slope * cosine
    dl[1] = jnp.broadcast_to(jnp.sum(weighted, axis=1, keepdims=True), (n_rows, n_rows))
    dlt[1] = jnp.broadcast_to(jnp.sum(weighted, axis=0, keepdims=True), (n_rows, n_rows)).T
    dl[2] = jnp.broadcast_to(inv_q, (n_rows, n_rows))
    dlt[2] = jnp.broadcast_to(inv_p, (n_rows, n_rows))
    chip = pl.ds(pl.multiple_of(chip_of(0, 0) * 8, 8), 8)

    def back(table, own, others, scale):
        d = fine_dot(table[0, chip, :], others * scale, (((1,), (0,)), ((), ())))
        inverse = table[2, chip, :][:, 0:1]
        e = own[chip, :] * inverse
        return inverse * (d - e * table[1, chip, :][:, 0:1])

    rq = back(dl, qs, p, inv_p)
    rp = back(dlt, ps, q, inv_q)
    left = core == 0
    rq = jnp.where(left, rq, pltpu.roll(rq, seqs, 0))
    rp = jnp.where(left, pltpu.roll(rp, seqs, 0), rp)
    raws[t] = folded(jnp.where(first, rq, rp))
    d_copies = []
    for d in (2, 1, 3):
        copy = y_copy(raws.at[t], raws.at[t], d, dsem, drecv)
        copy.start()
        d_copies.append(copy)
    total = None
    for d in (0, 1, 3, 2):
        o = (t - d) % nt
        if d:
            y_copy(raws.at[o], raws.at[o], d, dsem, drecv).wait_recv()
        cols = pl.ds(pl.multiple_of(o * part_w, part_w), part_w)
        part = lax.dot_general(unfolded(raws[o]).astype(bf16), wout[:, cols], NT, preferred_element_type=f32)
        total = part if total is None else total + part
    for s in range(8):
        ups[s] = jnp.broadcast_to(total[s:s + 1], (8, groups * H))

    @pl.loop(0, seqs, unroll=seqs)
    def _(s):
        attend_backward(rows, scale, att, wts, ups, dgt, pl.multiple_of(s * lq, H), bq, s, s, groups)

    @pl.loop(0, seqs, unroll=seqs)
    def _(s):
        attend_backward(rows, scale, att, wts, ups, dgt, pl.multiple_of(base_p + s * lp, H), bp,
                        seqs + 2 * s, seqs + s, groups)

    def last_sent():
        for copy in c_copies + d_copies:
            copy.wait_send()

    return last_sent


def scatter_part(r, sent):
    part, both, sib, landed = r.part, r.both, r.sib, r.landed
    ssem, rsem, sibs, sibr = r.fsend, r.frecv, r.fsibs, r.fsibr
    depth = 2 * r.out.shape[1]
    qr = part.shape[2]
    half = depth // 2
    core = place()[2]
    own = pl.ds(pl.multiple_of(core * half, half), half)
    other = pl.ds(pl.multiple_of((1 - core) * half, half), half)

    def sib_copy(i):
        return pltpu.make_async_remote_copy(
            src_ref=both.at[i, :, :, other], dst_ref=sib.at[i], send_sem=sibs.at[i], recv_sem=sibr.at[i],
            device_id=dev(0, 0, flip=True), device_id_type=MESH)

    fold = Fold(part, landed, ssem, rsem)
    steps = fold_steps(fold)

    n = len(ORDER) // 2

    @pl.loop(0, n + 1)
    def _(i):
        @pl.when(i < n)
        def _():
            for k in (2 * i, 2 * i + 1):
                chip = chip_of(pick(k, [o[0] % 4 for o in ORDER]), pick(k, [o[1] % 4 for o in ORDER]))
                cols = pl.ds(pl.multiple_of(chip * depth, depth), depth)
                total = jnp.dot(r.dgt[...], r.X[:, cols], preferred_element_type=f32).astype(bf16)
                both[k] = total.reshape(4, qr, depth)
            for k in (2 * i, 2 * i + 1):
                sib_copy(k).start()

        @pl.when(i > 0)
        def _():
            for k in (2 * i - 2, 2 * i - 1):
                sib_copy(k).wait_recv()
            for k in (2 * i - 2, 2 * i - 1):
                part[k] = both[k, :, :, own] + sib[k]

        for m in range(n):
            @pl.when(i == m + 1)
            def _():
                for at in (2 * m, 2 * m + 1):
                    for step in steps.get(at, ()):
                        step()

    sent()
    for i in range(16):
        sib_copy(i).wait_send()
    fold.finish()
    for side in (0, 1):
        total = part[15, pl.ds(2 * side, 2)].astype(f32)
        for dx, dz in ((1, 0), (-1, 0), (0, 1), (0, -1)):
            total = total + fold.recv(0, 0, 2 * side, 2, dx, dz)[...].astype(f32)
        r.out[pl.ds(side * 2 * qr, 2 * qr), :] = total.reshape(2 * qr, half)
    assert fold.waited == set(range(len(fold.sends)))


def finish_kernel(sums, gain, gq, gk, gv):
    H = HEAD_DIM
    depth = sums.shape[1]
    own = gain[:, pl.ds(pl.multiple_of(slot_of(0, 0) * depth, depth), depth)]
    heads = gq.shape[1] // H
    for n in range(heads + 2):
        block = (sums[n * H:(n + 1) * H, :] * own).T
        if n < heads:
            gq[:, n * H:(n + 1) * H] = block
        elif n == heads:
            gk[...] = block
        else:
            gv[...] = block


def finish(sums, gain):
    rows, depth = sums.shape
    cols = (rows - 2 * HEAD_DIM, HEAD_DIM, HEAD_DIM)
    VM = pl.BlockSpec(memory_space=pltpu.VMEM)
    return pl.pallas_call(
        finish_kernel,
        out_shape=tuple(jax.ShapeDtypeStruct((depth, n), f32) for n in cols),
        in_specs=[VM, VM],
        out_specs=(VM, VM, VM),
        name="finish_rows",
    )(sums, gain.reshape(1, -1))


def peers():
    t = lax.axis_index("tensor")
    return [{"tensor": (t + d) % 4} for d in (1, 2, 3)] + [dev(a, b) for a, b in AROUND] + [dev(0, 0, flip=True)]


def step_kernel(names, *refs):
    r = types.SimpleNamespace(**dict(zip(names, refs, strict=True)))
    settle()
    barrier = pltpu.get_barrier_semaphore()
    for peer in peers():
        pl.semaphore_signal(barrier, inc=1, device_id=peer, device_id_type=MESH)
    sent = gather_part(r)
    sent = middle_part(r, sent)
    scatter_part(r, sent)
    HERE.clear()


def step(xq, xp, gain, wq, wk, wv, w_out, owner, place_in):
    tokens, width = xq.shape[0] + xp.shape[0], xq.shape[1]
    depth, heads = wq.shape
    cols = heads + wk.shape[1] + wv.shape[1]
    n = owner.shape[1]
    H = HEAD_DIM
    ANY, VM = pl.BlockSpec(memory_space=pl.ANY), pl.BlockSpec(memory_space=pltpu.VMEM)

    def dma(*shape):
        return pltpu.SemaphoreType.DMA(shape)

    ins = dict(xq=ANY, xp=ANY, gain=VM, wq=ANY, wk=ANY, wv=ANY, wout_hbm=ANY, owner=VM, place_in=VM)
    outs = dict(out=jax.ShapeDtypeStruct((cols, depth), f32), loss=jax.ShapeDtypeStruct((1, 1), f32))
    scratch = dict(
        W=pltpu.VMEM((32, depth, cols), bf16), held=pltpu.VMEM((depth, cols), bf16),
        X=pltpu.VMEM((tokens, width), bf16), acc=pltpu.VMEM((tokens, cols), f32),
        macc=pltpu.VMEM((8, 8, width), f32), rows=pltpu.VMEM((tokens, cols), bf16),
        scale=pltpu.VMEM((tokens, H), f32), means=pltpu.VMEM((8, width), f32),
        wout=pltpu.VMEM(w_out.shape, bf16), wts=pltpu.VMEM((tokens, H), f32),
        pooled=pltpu.VMEM((8, 8, heads), f32), ups=pltpu.VMEM((8, 8, heads), f32),
        terms=pltpu.VMEM((4, 16, width // 8), bf16), got=pltpu.VMEM((4, 16, width // 8), bf16),
        embeds=pltpu.VMEM((32, 8, width // 4), f32),
        qs=pltpu.VMEM((n, width // 4), f32), ps=pltpu.VMEM((n, width // 4), f32),
        gram=pltpu.VMEM((4, n + 8, n), f32), dl=pltpu.VMEM((3, n, n), f32), dlt=pltpu.VMEM((3, n, n), f32),
        raws=pltpu.VMEM((4, 16, width // 8), bf16), dgt=pltpu.VMEM((cols, tokens), bf16),
        part=pltpu.VMEM((16, 4, cols // 4, depth), bf16), both=pltpu.VMEM((16, 4, cols // 4, 2 * depth), bf16),
        sib=pltpu.VMEM((16, 4, cols // 4, depth), bf16), landed=pltpu.VMEM((60, cols // 4, depth), bf16),
        wsem=dma(3), xsem=dma(tokens // 128), osem=dma(),
        gsend=dma(40), grecv=dma(40), gsibs=dma(16), gsibr=dma(16),
        asend=dma(3), arecv=dma(3), bsend=dma(15), brecv=dma(15), msibs=dma(16), msibr=dma(16),
        csend=dma(3), crecv=dma(3), dsend=dma(3), drecv=dma(3),
        fsend=dma(40), frecv=dma(40), fsibs=dma(16), fsibr=dma(16))
    return pl.pallas_call(
        functools.partial(step_kernel, (*ins, *outs, *scratch)),
        out_shape=tuple(outs.values()),
        in_specs=list(ins.values()),
        out_specs=(VM, VM),
        scratch_shapes=list(scratch.values()),
        compiler_params=pltpu.CompilerParams(
            collective_id=0, has_side_effects=True, vmem_limit_bytes=VMEM_LIMIT),
        cost_estimate=pl.CostEstimate(flops=4 * tokens * width * cols, bytes_accessed=2 * tokens * width,
                                      transcendentals=0),
        name="contrast_step",
    )(xq, xp, gain.reshape(1, -1), wq, wk, wv, w_out, owner, place_in)


def body(
    query_states, passage_states, norm_gain, w_query, w_key, w_value, w_out, neg_owner, neg_slot
):
    owned, query_length, _ = query_states.shape
    passage_length = passage_states.shape[1]
    xq = query_states.reshape(owned * query_length, -1)
    xp = passage_states.reshape(owned * passage_length, -1)
    sums, loss = step(xq, xp, norm_gain, w_query, w_key, w_value, w_out, neg_owner.T, neg_slot.T)
    return (loss[0, 0], *finish(sums, norm_gain))


def solution(mesh):
    in_specs = (
        P("dp", None, None),
        P("dp", None, None),
        P(),
        P("dp", "tensor"),
        P("dp", "tensor"),
        P("dp", "tensor"),
        P("tensor", None),
        P(),
        P(),
    )
    out_specs = (P(), P("dp", "tensor"), P("dp", "tensor"), P("dp", "tensor"))
    return jax.shard_map(body, mesh=mesh, in_specs=in_specs, out_specs=out_specs, check_vma=False)
```

```python
import functools
import math
import types

import jax
import jax.numpy as jnp
from jax import lax
from jax.experimental import pallas as pl
from jax.experimental.pallas import tpu as pltpu
from jax.sharding import PartitionSpec as P

HEAD_DIM = 128
eps_norm = 1e-06
eps_unit = 1e-06
sharpness_divisor = 0.05
MESH = pl.DeviceIdType.MESH
f32, bf16 = jnp.float32, jnp.bfloat16
XS, ZS = 4, 4
STAT_STEPS = ((7, 1), (11, 2))
SUM_STEPS = ((0, 3), (4, 4), (6, 5), (8, 6), (13, 7))
VMEM_LIMIT = 63 * 1024 * 1024


def iota(shape, dim):
    return lax.broadcasted_iota(jnp.int32, shape, dim)


HERE = {}


def place():
    if "at" in HERE:
        return HERE["at"]
    p = lax.axis_index("dp")
    return p // (2 * ZS), (p // 2) % ZS, p % 2


def settle():
    HERE.clear()
    x, z, c = place()
    HERE.update(at=(x, z, c), xs=[(x + a) % XS for a in range(XS)], zs=[(z + b) % ZS for b in range(ZS)], other=1 - c)


def chip_of(a, b):
    if "at" in HERE and isinstance(a, int) and isinstance(b, int):
        return HERE["xs"][a % XS] * ZS + HERE["zs"][b % ZS]
    x, z, _ = place()
    return (x + a) % XS * ZS + (z + b) % ZS


def slot_of(a, b, flip=False):
    c = place()[2]
    if flip:
        c = HERE.get("other", 1 - c)
    return chip_of(a, b) * 2 + c


def dev(a, b, flip=False):
    return {"dp": slot_of(a, b, flip=flip)}


GATHERED = ((0, 0), (1, 0), (0, 1), (-1, 0), (0, -1), (1, 1), (1, -1), (-1, 1), (-1, -1), (2, 0), (0, 2),
            (2, 1), (1, 2), (2, -1), (-1, 2), (2, 2))


def pick(i, values):
    out = values[0]
    for n, value in enumerate(values[1:], 1):
        out = jnp.where(i == n, value, out)
    return out


class Tree:
    def __init__(self, buf, rows, send_sem, recv_sem):
        self.buf, self.rows, self.send_sem, self.recv_sem = buf, rows, send_sem, recv_sem
        self.sends, self.pieces, self.waited = [], {}, set()

    def view(self, a, b, lo, n):
        return self.buf.at[slot_of(a, b), pl.ds(lo * self.rows, n * self.rows)]

    def copy(self, i):
        a, b, lo, n, dx, dz = self.sends[i]
        view = self.view(a, b, lo, n)
        return pltpu.make_async_remote_copy(
            src_ref=view, dst_ref=view, send_sem=self.send_sem.at[i], recv_sem=self.recv_sem.at[i],
            device_id=dev(dx, dz), device_id_type=MESH)

    def send(self, a, b, lo, n, dx, dz):
        i = len(self.sends)
        self.sends.append((a, b, lo, n, dx, dz))
        self.pieces[((a - dx) % 4, (b - dz) % 4, lo, n)] = i
        self.copy(i).start()

    def wait(self, a, b, lo, n):
        i = self.pieces[(a % 4, b % 4, lo, n)]
        view = self.view(a, b, lo, n)
        pltpu.make_async_remote_copy(
            src_ref=view, dst_ref=view, send_sem=self.send_sem.at[i], recv_sem=self.recv_sem.at[i],
            device_id=dev(1, 0), device_id_type=MESH).wait_recv()
        self.waited.add(i)

    def finish(self):
        assert self.waited == set(range(len(self.sends)))
        for i in range(len(self.sends)):
            self.copy(i).wait_send()


def up(d):
    return 0 if d > 0 else 1


def gather_stages(tree, sibling):
    def first():
        for d in (1, -1):
            tree.send(0, 0, 0, 2, d, 0)
            tree.send(0, 0, 2, 2, 0, d)
        for d in (1, -1):
            tree.send(0, 0, 2, 2, d, 0)
            tree.send(0, 0, 0, 2, 0, d)
        sibling(0, 0)

    def second():
        for s in (1, -1):
            tree.wait(s, 0, 0, 2)
            tree.send(s, 0, up(-s), 1, -s, 0)
            tree.wait(0, s, 2, 2)
            tree.send(0, s, 2 + up(-s), 1, 0, -s)
        for s in (1, -1):
            for d in (1, -1):
                tree.send(s, 0, 0, 2, 0, d)
                tree.send(0, s, 2, 2, d, 0)

    def third():
        for s in (1, -1):
            tree.wait(s, 0, 2, 2)
            tree.send(s, 0, 2 + up(-s), 1, -s, 0)
            tree.wait(0, s, 0, 2)
            tree.send(0, s, up(-s), 1, 0, -s)
        for s in (1, -1):
            sibling(s, 0)
            sibling(0, s)

    def fourth():
        for q in (0, 1):
            tree.wait(2, 0, q, 1)
            tree.wait(0, 2, 2 + q, 1)
        for d in (1, -1):
            tree.send(2, 0, 0, 2, 0, d)
            tree.send(0, 2, 2, 2, d, 0)

    def fifth():
        for sx in (1, -1):
            for sz in (1, -1):
                tree.wait(sx, sz, 0, 2)
                tree.send(sx, sz, up(-sz), 1, 0, -sz)
                tree.wait(sx, sz, 2, 2)
                tree.send(sx, sz, 2 + up(-sx), 1, -sx, 0)
                sibling(sx, sz)

    def sixth():
        for q in (0, 1):
            tree.wait(2, 0, 2 + q, 1)
            tree.wait(0, 2, q, 1)
        sibling(2, 0)
        sibling(0, 2)
        for s in (1, -1):
            tree.wait(2, s, 0, 2)
            tree.send(2, s, up(-s), 1, 0, -s)
            tree.wait(s, 2, 2, 2)
            tree.send(s, 2, 2 + up(-s), 1, -s, 0)

    def seventh():
        for s in (1, -1):
            for q in (0, 1):
                tree.wait(2, s, 2 + q, 1)
                tree.wait(s, 2, q, 1)
            sibling(2, s)
            sibling(s, 2)

    def eighth():
        for q in (0, 1, 2, 3):
            tree.wait(2, 2, q, 1)
        sibling(2, 2)

    return first, second, third, fourth, fifth, sixth, seventh, eighth


def gather_part(r):
    xq, xp, W, X, acc, macc, scale = r.xq, r.xp, r.W, r.X, r.acc, r.macc, r.scale
    wsem, xsem, ssem, rsem, sibs, sibr = r.wsem, r.xsem, r.gsend, r.grecv, r.gsibs, r.gsibr
    lq, lp = xq.shape[0] // 4, xp.shape[0] // 4
    tq, tokens = xq.shape[0], X.shape[0]
    width = X.shape[1]
    depth = W.shape[1]
    T = 128
    mine = slot_of(0, 0)
    loads = []
    lo = 0
    for n, w in enumerate((r.wq, r.wk, r.wv)):
        loads.append(pltpu.make_async_copy(w, r.held.at[:, pl.ds(lo, w.shape[1])], wsem.at[n]))
        lo += w.shape[1]
    for load in loads:
        load.start()
    for i in range(tq // T):
        pltpu.make_async_copy(xq.at[pl.ds(i * T, T)], X.at[pl.ds(i * T, T)], xsem.at[i]).start(priority=1)
    macc[...] = jnp.zeros_like(macc)
    eye = iota((depth, depth), 0) == iota((depth, depth), 1)
    own = r.gain[:, pl.ds(pl.multiple_of(mine * depth, depth), depth)]
    column = jnp.sum(jnp.where(eye, own, 0.0), axis=1, keepdims=True)
    for load in loads:
        load.wait()
    W[mine] = (r.held[...].astype(f32) * column).astype(bf16)
    pl.semaphore_wait(pltpu.get_barrier_semaphore(), len(peers()))

    tree = Tree(W, depth // 4, ssem, rsem)
    sib_sent = []

    def sib_copy(i, a, b, flip):
        view = W.at[slot_of(a, b, flip=flip)]
        return pltpu.make_async_remote_copy(
            src_ref=view, dst_ref=view, send_sem=sibs.at[i], recv_sem=sibr.at[i],
            device_id=dev(0, 0, flip=True), device_id_type=MESH)

    def sibling(a, b):
        sib_copy(len(sib_sent), a, b, False).start()
        sib_sent.append((a % 4, b % 4))

    stages = gather_stages(tree, sibling)
    C = 128
    chunks = width // C
    n_tiles = tokens // T
    n_query = tq // T
    stages[0]()

    @pl.loop(0, n_tiles)
    def _(i):
        pltpu.make_async_copy(xq.at[pl.ds(0, T)], X.at[pl.ds(pl.multiple_of(i * T, T), T)], xsem.at[i]).wait()
        acc[pl.ds(pl.multiple_of(i * T, T), T), :] = jnp.zeros((T, acc.shape[1]), f32)

        @pl.when(i < n_tiles - n_query)
        def _():
            pltpu.make_async_copy(xp.at[pl.ds(pl.multiple_of(i * T, T), T)],
                                  X.at[pl.ds(pl.multiple_of((i + n_query) * T, T), T)],
                                  xsem.at[i + n_query]).start(priority=1)

        per = lp // T
        seq = jnp.where(i < n_query, i // (lq // T), 4 + (i - n_query) // per)

        def step(n, sums):
            span = pl.ds(pl.multiple_of(i * T + n * 16, 16), 16)
            squares, later = [None] * 4, []
            for c in range(chunks):
                v = X[span, c * C:(c + 1) * C].astype(f32)
                w = v * v
                squares[c % 4] = w if squares[c % 4] is None else squares[c % 4] + w
                later.append(sums[c] + (v[0:8] + v[8:16]))
            scale[span, :] = (squares[0] + squares[1]) + (squares[2] + squares[3])
            return tuple(later)

        sums = lax.fori_loop(0, T // 16, step, tuple(
            macc[seq, :, c * C:(c + 1) * C] for c in range(chunks)))
        for c in range(chunks):
            macc[seq, :, c * C:(c + 1) * C] = sums[c]
        for at, stage in STAT_STEPS:
            @pl.when(i == at)
            def _():
                stages[stage]()

    @pl.loop(0, n_tiles)
    def _(i):
        tile = pl.ds(pl.multiple_of(i * T, T), T)
        total = jnp.sum(scale[tile, :], axis=1, keepdims=True)
        scale[tile, :] = jnp.broadcast_to(lax.rsqrt(total * (1.0 / width) + eps_norm), (T, C))

    for s in range(8):
        r.means[s:s + 1, :] = jnp.sum(macc[s], axis=0, keepdims=True) * (1.0 / (lq if s < 4 else lp))

    order = GATHERED

    @pl.loop(0, len(order))
    def _(i):
        a, b = pick(i, [o[0] % 4 for o in order]), pick(i, [o[1] % 4 for o in order])
        sib_copy(i, a, b, True).wait_recv()
        chip = chip_of(a, b)
        cols = pl.ds(pl.multiple_of(chip * 2 * depth, 2 * depth), 2 * depth)
        w = W[pl.ds(chip * 2, 2)].reshape(2 * depth, W.shape[2])
        total = jnp.dot(X[:, cols], w, preferred_element_type=f32)
        acc[...] = acc[...] + total
        for at, stage in SUM_STEPS:
            @pl.when(i == at)
            def _():
                stages[stage]()

    assert sib_sent == [(a % 4, b % 4) for a, b in order]

    @pl.loop(0, n_tiles)
    def _(i):
        tile = pl.ds(pl.multiple_of(i * T, T), T)
        r.rows[tile, :] = (acc[tile, :] * scale[tile, 0:1]).astype(bf16)

    pltpu.make_async_copy(r.wout_hbm, r.wout, r.osem).start(priority=1)

    def sent():
        tree.finish()
        for i, (a, b) in enumerate(sib_sent):
            sib_copy(i, a, b, False).wait_send()

    return sent


ORDER = ((2, 2), (2, 1), (2, -1), (1, 2), (-1, 2), (2, 0), (0, 2), (1, 1), (1, -1), (-1, 1), (-1, -1),
         (1, 0), (-1, 0), (0, 1), (0, -1), (0, 0))


def key_of(a, b):
    return a % 4, b % 4


class Fold:
    def __init__(self, part, landed, send_sem, recv_sem):
        self.part, self.landed, self.send_sem, self.recv_sem = part, landed, send_sem, recv_sem
        self.sends, self.pieces, self.used, self.waited = [], {}, 0, set()
        self.index = {key_of(a, b): i for i, (a, b) in enumerate(ORDER)}

    def copy(self, i):
        a, b, lo, n, dx, dz, off = self.sends[i]
        return pltpu.make_async_remote_copy(
            src_ref=self.part.at[self.index[key_of(a, b)], pl.ds(lo, n)], dst_ref=self.landed.at[pl.ds(off, n)],
            send_sem=self.send_sem.at[i], recv_sem=self.recv_sem.at[i],
            device_id=dev(dx, dz), device_id_type=MESH)

    def send(self, a, b, lo, n, dx, dz):
        i = len(self.sends)
        self.sends.append((a, b, lo, n, dx, dz, self.used))
        self.used += n
        self.pieces[(*key_of(a - dx, b - dz), lo, n, *key_of(-dx, -dz))] = i
        self.copy(i).start()

    def recv(self, a, b, lo, n, dx, dz):
        i = self.pieces[(*key_of(a, b), lo, n, *key_of(dx, dz))]
        self.copy(i).wait_recv()
        self.waited.add(i)
        off = self.sends[i][6]
        return self.landed.at[pl.ds(off, n)]

    def add(self, a, b, lo, n, *froms):
        at = self.index[key_of(a, b)]
        for m, (dx, dz) in froms:
            piece = self.recv(a, b, m[0], m[1], dx, dz)
            cut = piece.shape[1] // 2

            @pl.loop(0, 2 * m[1])
            def _(n):
                q, rows = n // 2, pl.ds(pl.multiple_of(n % 2 * cut, cut), cut)
                self.part[at, m[0] + q, rows, :] = self.part[at, m[0] + q, rows, :] + piece[q, rows, :]

    def finish(self):
        for i in range(len(self.sends)):
            self.copy(i).wait_send()


def ends(fold, a, b, half):
    if half == 0:
        fold.send(a, b, 0, 1, 0, -1)
        fold.send(a, b, 1, 1, 0, 1)
    else:
        fold.send(a, b, 2, 1, -1, 0)
        fold.send(a, b, 3, 1, 1, 0)


def fold_steps(fold):
    def first(i):
        a, b = ORDER[i]
        if (a, b) == (2, 2):
            ends(fold, a, b, 0)
            ends(fold, a, b, 1)
        elif a == 2:
            ends(fold, a, b, 1)
        elif b == 2:
            ends(fold, a, b, 0)
        elif a and b:
            q = up(-b)
            fold.add(a, b, 0, 2, ((q, 1), (0, -b)))
            fold.send(a, b, 0, 2, 0, b)
            q = 2 + up(-a)
            fold.add(a, b, 2, 2, ((q, 1), (-a, 0)))
            fold.send(a, b, 2, 2, a, 0)

    def second():
        for s in (1, -1):
            fold.add(2, s, 0, 2, ((up(-s), 1), (0, -s)))
            fold.send(2, s, 0, 2, 0, s)
            fold.add(s, 2, 2, 2, ((2 + up(-s), 1), (-s, 0)))
            fold.send(s, 2, 2, 2, s, 0)

    def third():
        fold.add(2, 0, 0, 2, ((0, 2), (0, 1)), ((0, 2), (0, -1)))
        fold.send(2, 0, 0, 1, -1, 0)
        fold.send(2, 0, 1, 1, 1, 0)
        fold.add(0, 2, 2, 2, ((2, 2), (1, 0)), ((2, 2), (-1, 0)))
        fold.send(0, 2, 2, 1, 0, -1)
        fold.send(0, 2, 3, 1, 0, 1)

    def fourth():
        for s in (1, -1):
            fold.add(s, 0, 2, 2, ((2 + up(-s), 1), (-s, 0)))
            fold.send(s, 0, 2, 2, s, 0)
            fold.add(0, s, 0, 2, ((up(-s), 1), (0, -s)))
            fold.send(0, s, 0, 2, 0, s)

    def fifth():
        for s in (1, -1):
            fold.add(s, 0, 0, 2, ((0, 2), (0, 1)), ((0, 2), (0, -1)), ((up(-s), 1), (-s, 0)))
            fold.send(s, 0, 0, 2, s, 0)
            fold.add(0, s, 2, 2, ((2, 2), (1, 0)), ((2, 2), (-1, 0)), ((2 + up(-s), 1), (0, -s)))
            fold.send(0, s, 2, 2, 0, s)

    steps = {i: [functools.partial(first, i)] for i in range(11)}
    steps[6].append(second)
    steps[11] = [third]
    steps[14] = [fourth, fifth]
    return steps


NT = (((1,), (1,)), ((), ()))
AROUND = ((2, 2), (2, 1), (2, 3), (1, 2), (3, 2), (2, 0), (0, 2), (1, 1), (1, 3), (3, 1), (3, 3),
          (1, 0), (3, 0), (0, 1), (0, 3))


def fine_dot(a, b, dims):
    def split(value):
        high = value.astype(bf16)
        return high, (value - high.astype(f32)).astype(bf16)

    def dot(one, two):
        return lax.dot_general(one, two, dims, preferred_element_type=f32)

    (ah, al), (bh, bl) = split(a), split(b)
    return dot(ah, bh) + (dot(ah, bl) + dot(al, bh))


def block_of(row, n):
    H = HEAD_DIM
    return pl.ds(pl.multiple_of((row + n // 6) * H, H), H), slice(n % 6 * H, (n % 6 + 1) * H)


def attend_forward(rows, att, wts, pooled, base, blocks, row, seq, groups):
    H = HEAD_DIM
    key_at, value_at = groups * H, (groups + 1) * H
    L = blocks * H
    k = rows[pl.ds(base, L), key_at:key_at + H]
    v = rows[pl.ds(base, L), value_at:value_at + H].astype(f32)
    causal = iota((H, H), 0) <= iota((H, H), 1)
    n = 0
    for h in range(groups):
        w = [None] * blocks
        for ib in range(blocks):
            q = rows[pl.ds(pl.multiple_of(base + ib * H, H), H), h * H:(h + 1) * H]
            e = []
            for jb in range(ib + 1):
                st = lax.dot_general(k[jb * H:(jb + 1) * H], q, NT, preferred_element_type=f32)
                st = jnp.exp(st * (1.0 / math.sqrt(H)))
                e.append(jnp.where(causal, st, 0.0) if jb == ib else st)
            total = jnp.sum(e[0], axis=0, keepdims=True)
            for one in e[1:]:
                total = total + jnp.sum(one, axis=0, keepdims=True)
            r = 1.0 / total
            for jb in range(ib + 1):
                at = e[jb] * r
                att[block_of(row, n)] = at
                n += 1
                w[jb] = at if w[jb] is None else w[jb] + at
        out = None
        for jb in range(blocks):
            col = jnp.sum(w[jb], axis=1, keepdims=True) * (1.0 / L)
            wts[pl.ds(pl.multiple_of(base + jb * H, H), H), h:h + 1] = col
            part = jnp.sum(col * v[jb * H:(jb + 1) * H], axis=0, keepdims=True)
            out = part if out is None else out + part
        pooled[seq, :, h * H:(h + 1) * H] = jnp.broadcast_to(out, (8, H))


def attend_backward(rows, scale, att, wts, ups, dgt, base, blocks, row, seq, groups):
    H = HEAD_DIM
    key_at, value_at = groups * H, (groups + 1) * H
    L = blocks * H
    k = rows[pl.ds(base, L), key_at:key_at + H]
    v = rows[pl.ds(base, L), value_at:value_at + H].astype(f32)
    kt = k.astype(f32).T.astype(bf16)
    dk, dv = [None] * blocks, [None] * blocks
    eye = iota((H, H), 0) == iota((H, H), 1)
    along = []
    for jb in range(blocks):
        column = scale[pl.ds(pl.multiple_of(base + jb * H, H), H), 0:1]
        along.append(jnp.sum(jnp.where(eye, column, 0.0), axis=0, keepdims=True))
    n = 0
    for h in range(groups):
        u = ups[seq, :, h * H:(h + 1) * H][0:1]
        c = [jnp.sum(v[jb * H:(jb + 1) * H] * u, axis=1, keepdims=True) * (1.0 / L) for jb in range(blocks)]
        for ib in range(blocks):
            span = pl.ds(pl.multiple_of(base + ib * H, H), H)
            q = rows[span, h * H:(h + 1) * H]
            at = [att[block_of(row, n + jb)] for jb in range(ib + 1)]
            n += ib + 1
            m = None
            for jb in range(ib + 1):
                part = jnp.sum(at[jb] * c[jb], axis=0, keepdims=True)
                m = part if m is None else m + part
            dq = None
            for jb in range(ib + 1):
                ds = (at[jb] * ((c[jb] - m) * (1.0 / math.sqrt(H)))).astype(bf16)
                part = jnp.dot(kt[:, jb * H:(jb + 1) * H], ds, preferred_element_type=f32)
                dq = part if dq is None else dq + part
                part = jnp.dot(ds, q, preferred_element_type=f32)
                dk[jb] = part if dk[jb] is None else dk[jb] + part
            dgt[h * H:(h + 1) * H, span] = (dq * along[ib]).astype(bf16)
        for jb in range(blocks):
            part = wts[pl.ds(pl.multiple_of(base + jb * H, H), H), h:h + 1] * u
            dv[jb] = part if dv[jb] is None else dv[jb] + part
    for jb in range(blocks):
        span = pl.ds(pl.multiple_of(base + jb * H, H), H)
        dgt[key_at:key_at + H, span] = (dk[jb].T * along[jb]).astype(bf16)
        dgt[value_at:value_at + H, span] = (dv[jb].T * along[jb]).astype(bf16)


def middle_part(r, sent):
    lq, lp = r.xq.shape[0] // 4, r.xp.shape[0] // 4
    rows, scale, means, wout, att, wts = r.rows, r.scale, r.means, r.wout, r.acc, r.wts
    pooled, ups, terms, got, embeds, qs, ps = r.pooled, r.ups, r.terms, r.got, r.embeds, r.qs, r.ps
    gram, dl, dlt, raws, dgt, loss, owner, place_in = (
        r.gram, r.dl, r.dlt, r.raws, r.dgt, r.loss, r.owner, r.place_in)
    asem, arecv, bsem, brecv, sibs, sibr = r.asend, r.arecv, r.bsend, r.brecv, r.msibs, r.msibr
    csem, crecv, dsem, drecv = r.csend, r.crecv, r.dsend, r.drecv
    H = HEAD_DIM
    groups = rows.shape[1] // H - 2
    width = wout.shape[1]
    seqs = 4
    nt = 4
    part_w = width // nt
    x, z, core = place()
    t = lax.axis_index("tensor")
    base_p = seqs * lq
    bq, bp = lq // H, lp // H

    @pl.loop(0, seqs, unroll=seqs)
    def _(s):
        attend_forward(rows, att, wts, pooled, pl.multiple_of(s * lq, H), bq, s, s, groups)

    @pl.loop(0, seqs, unroll=seqs)
    def _(s):
        attend_forward(rows, att, wts, pooled, pl.multiple_of(base_p + s * lp, H), bp, seqs + 2 * s, seqs + s, groups)

    pltpu.make_async_copy(r.wout_hbm, wout, r.osem).wait()
    row = iota((8, groups * H), 0)
    low = pooled[0]
    for s in range(1, 8):
        low = jnp.where(row == s, pooled[s], low)
    low = low.astype(bf16)

    def y_copy(src, dst, d, send_sem, recv_sem):
        return pltpu.make_async_remote_copy(
            src_ref=src, dst_ref=dst, send_sem=send_sem.at[d - 1], recv_sem=recv_sem.at[d - 1],
            device_id={"tensor": (t + d) % nt}, device_id_type=MESH)

    def term(o):
        cols = pl.ds(pl.multiple_of(o * part_w, part_w), part_w)
        return jnp.dot(low, wout[:, cols], preferred_element_type=f32)

    def folded(value):
        return jnp.concatenate([value[:, :part_w // 2], value[:, part_w // 2:]], axis=0).astype(bf16)

    def unfolded(value):
        value = value.astype(f32)
        return jnp.concatenate([value[:8], value[8:]], axis=1)

    a_copies = []
    for d in (2, 1, 3):
        terms[d] = folded(term((t + d) % nt))
        copy = y_copy(terms.at[d], got.at[d], d, asem, arecv)
        copy.start()
        a_copies.append(copy)
    mine = term(t) + means[:, pl.ds(pl.multiple_of(t * part_w, part_w), part_w)]
    n_rows = qs.shape[0]
    ids = owner[...] * seqs + place_in[...]
    col = iota((n_rows, n_rows), 1)
    counts = jnp.zeros((n_rows, n_rows), f32)
    for j in range(ids.shape[0]):
        counts = counts + jnp.where(ids[j:j + 1, :] == iota((n_rows, n_rows), 0), 1.0, 0.0)
    counts = counts.T
    sent()
    for copy in a_copies:
        copy.wait_recv()
    mine = mine + unfolded(got[1]) + unfolded(got[2]) + unfolded(got[3])
    here = slot_of(0, 0)
    embeds[here] = mine

    def b_copy(n, a, b):
        view = embeds.at[here]
        return pltpu.make_async_remote_copy(
            src_ref=view, dst_ref=view, send_sem=bsem.at[n], recv_sem=brecv.at[n],
            device_id=dev(a, b), device_id_type=MESH)

    def s_copy(n, a, b, flip):
        view = embeds.at[slot_of(a, b, flip=flip)]
        return pltpu.make_async_remote_copy(
            src_ref=view, dst_ref=view, send_sem=sibs.at[n], recv_sem=sibr.at[n],
            device_id=dev(0, 0, flip=True), device_id_type=MESH)

    s_copy(15, 0, 0, False).start()
    for n, (a, b) in enumerate(AROUND):
        b_copy(n, a, b).start()
    for n, (a, b) in enumerate(AROUND):
        view = embeds.at[slot_of(-a, -b)]
        pltpu.make_async_remote_copy(
            src_ref=view, dst_ref=view, send_sem=bsem.at[n], recv_sem=brecv.at[n],
            device_id=dev(a, b), device_id_type=MESH).wait_recv()
        s_copy(n, -a, -b, False).start()
    s_copy(15, 0, 0, True).wait_recv()
    for n, (a, b) in enumerate(AROUND):
        s_copy(n, -a, -b, True).wait_recv()

    first = iota((8, part_w), 0) < seqs

    @pl.loop(0, n_rows // 8)
    def _(k):
        one, two = embeds[2 * k], embeds[2 * k + 1]
        span = pl.ds(pl.multiple_of(k * 8, 8), 8)
        qs[span, :] = jnp.where(first, one, pltpu.roll(two, seqs, 0))
        ps[span, :] = jnp.where(first, pltpu.roll(one, seqs, 0), two)

    q, p = qs[...], ps[...]
    gram[0, pl.ds(0, n_rows), :] = fine_dot(q, p, NT)
    eye = iota((n_rows, n_rows), 0) == col

    def squares(value):
        column = jnp.sum(value * value, axis=1, keepdims=True)
        return jnp.sum(jnp.where(eye, column, 0.0), axis=0, keepdims=True)

    gram[0, pl.ds(n_rows, 8), :] = jnp.where(iota((8, n_rows), 0) == 0, squares(q), squares(p))
    c_copies = []
    for d in (2, 1, 3):
        copy = y_copy(gram.at[0], gram.at[d], d, csem, crecv)
        copy.start()
        c_copies.append(copy)
    for copy in a_copies:
        copy.wait_send()
    for n, (a, b) in enumerate(AROUND):
        b_copy(n, a, b).wait_send()
        s_copy(n, -a, -b, False).wait_send()
    s_copy(15, 0, 0, False).wait_send()
    for copy in c_copies:
        copy.wait_recv()
    whole = (gram[0] + gram[2]) + (gram[1] + gram[3])
    inv = lax.rsqrt(whole[n_rows:] + eps_unit)
    inv_q_row, inv_p_row = inv[0:1], inv[1:2]
    inv_q = jnp.sum(jnp.where(eye, inv_q_row, 0.0), axis=1, keepdims=True)
    inv_p = jnp.sum(jnp.where(eye, inv_p_row, 0.0), axis=1, keepdims=True)
    cosine = whole[:n_rows] * inv_q * inv_p_row
    logits = cosine * (1.0 / sharpness_divisor)
    raised = jnp.exp(logits) * (1.0 + counts)
    sums = jnp.sum(raised, axis=1, keepdims=True)
    diagonal = jnp.sum(jnp.where(eye, logits, 0.0), axis=1, keepdims=True)
    loss[...] = jnp.sum(jnp.log(sums) - diagonal, axis=0, keepdims=True) * (1.0 / n_rows)
    slope = (raised / sums - jnp.where(eye, 1.0, 0.0)) * (1.0 / sharpness_divisor)
    dl[0] = slope
    dlt[0] = slope.T
    weighted = slope * cosine
    dl[1] = jnp.broadcast_to(jnp.sum(weighted, axis=1, keepdims=True), (n_rows, n_rows))
    dlt[1] = jnp.broadcast_to(jnp.sum(weighted, axis=0, keepdims=True), (n_rows, n_rows)).T
    dl[2] = jnp.broadcast_to(inv_q, (n_rows, n_rows))
    dlt[2] = jnp.broadcast_to(inv_p, (n_rows, n_rows))
    chip = pl.ds(pl.multiple_of(chip_of(0, 0) * 8, 8), 8)

    def back(table, own, others, scale):
        d = fine_dot(table[0, chip, :], others * scale, (((1,), (0,)), ((), ())))
        inverse = table[2, chip, :][:, 0:1]
        e = own[chip, :] * inverse
        return inverse * (d - e * table[1, chip, :][:, 0:1])

    rq = back(dl, qs, p, inv_p)
    rp = back(dlt, ps, q, inv_q)
    left = core == 0
    rq = jnp.where(left, rq, pltpu.roll(rq, seqs, 0))
    rp = jnp.where(left, pltpu.roll(rp, seqs, 0), rp)
    raws[t] = folded(jnp.where(first, rq, rp))
    d_copies = []
    for d in (2, 1, 3):
        copy = y_copy(raws.at[t], raws.at[t], d, dsem, drecv)
        copy.start()
        d_copies.append(copy)
    total = None
    for d in (0, 1, 3, 2):
        o = (t - d) % nt
        if d:
            y_copy(raws.at[o], raws.at[o], d, dsem, drecv).wait_recv()
        cols = pl.ds(pl.multiple_of(o * part_w, part_w), part_w)
        part = lax.dot_general(unfolded(raws[o]).astype(bf16), wout[:, cols], NT, preferred_element_type=f32)
        total = part if total is None else total + part
    for s in range(8):
        ups[s] = jnp.broadcast_to(total[s:s + 1], (8, groups * H))

    @pl.loop(0, seqs, unroll=seqs)
    def _(s):
        attend_backward(rows, scale, att, wts, ups, dgt, pl.multiple_of(s * lq, H), bq, s, s, groups)

    @pl.loop(0, seqs, unroll=seqs)
    def _(s):
        attend_backward(rows, scale, att, wts, ups, dgt, pl.multiple_of(base_p + s * lp, H), bp,
                        seqs + 2 * s, seqs + s, groups)

    def last_sent():
        for copy in c_copies + d_copies:
            copy.wait_send()

    return last_sent


def scatter_part(r, sent):
    part, both, sib, landed = r.part, r.both, r.sib, r.landed
    ssem, rsem, sibs, sibr = r.fsend, r.frecv, r.fsibs, r.fsibr
    depth = 2 * r.out.shape[1]
    qr = part.shape[2]
    half = depth // 2
    core = place()[2]
    own = pl.ds(pl.multiple_of(core * half, half), half)
    other = pl.ds(pl.multiple_of((1 - core) * half, half), half)

    def sib_copy(i):
        return pltpu.make_async_remote_copy(
            src_ref=both.at[i, :, :, other], dst_ref=sib.at[i], send_sem=sibs.at[i], recv_sem=sibr.at[i],
            device_id=dev(0, 0, flip=True), device_id_type=MESH)

    fold = Fold(part, landed, ssem, rsem)
    steps = fold_steps(fold)

    n = len(ORDER) // 2

    @pl.loop(0, n + 1)
    def _(i):
        @pl.when(i < n)
        def _():
            for k in (2 * i, 2 * i + 1):
                chip = chip_of(pick(k, [o[0] % 4 for o in ORDER]), pick(k, [o[1] % 4 for o in ORDER]))
                cols = pl.ds(pl.multiple_of(chip * depth, depth), depth)
                total = jnp.dot(r.dgt[...], r.X[:, cols], preferred_element_type=f32).astype(bf16)
                both[k] = total.reshape(4, qr, depth)
            for k in (2 * i, 2 * i + 1):
                sib_copy(k).start()

        @pl.when(i > 0)
        def _():
            for k in (2 * i - 2, 2 * i - 1):
                sib_copy(k).wait_recv()
            for k in (2 * i - 2, 2 * i - 1):
                part[k] = both[k, :, :, own] + sib[k]

        for m in range(n):
            @pl.when(i == m + 1)
            def _():
                for at in (2 * m, 2 * m + 1):
                    for step in steps.get(at, ()):
                        step()

    sent()
    for i in range(16):
        sib_copy(i).wait_send()
    fold.finish()
    for side in (0, 1):
        total = part[15, pl.ds(2 * side, 2)].astype(f32)
        for dx, dz in ((1, 0), (-1, 0), (0, 1), (0, -1)):
            total = total + fold.recv(0, 0, 2 * side, 2, dx, dz)[...].astype(f32)
        r.out[pl.ds(side * 2 * qr, 2 * qr), :] = total.reshape(2 * qr, half)
    assert fold.waited == set(range(len(fold.sends)))


def finish_kernel(sums, gain, gq, gk, gv):
    H = HEAD_DIM
    depth = sums.shape[1]
    own = gain[:, pl.ds(pl.multiple_of(slot_of(0, 0) * depth, depth), depth)]
    heads = gq.shape[1] // H
    for n in range(heads + 2):
        block = (sums[n * H:(n + 1) * H, :] * own).T
        if n < heads:
            gq[:, n * H:(n + 1) * H] = block
        elif n == heads:
            gk[...] = block
        else:
            gv[...] = block


def finish(sums, gain):
    rows, depth = sums.shape
    cols = (rows - 2 * HEAD_DIM, HEAD_DIM, HEAD_DIM)
    VM = pl.BlockSpec(memory_space=pltpu.VMEM)
    return pl.pallas_call(
        finish_kernel,
        out_shape=tuple(jax.ShapeDtypeStruct((depth, n), f32) for n in cols),
        in_specs=[VM, VM],
        out_specs=(VM, VM, VM),
        name="finish_rows",
    )(sums, gain.reshape(1, -1))


def peers():
    t = lax.axis_index("tensor")
    return [{"tensor": (t + d) % 4} for d in (1, 2, 3)] + [dev(a, b) for a, b in AROUND] + [dev(0, 0, flip=True)]


def step_kernel(names, *refs):
    r = types.SimpleNamespace(**dict(zip(names, refs, strict=True)))
    settle()
    barrier = pltpu.get_barrier_semaphore()
    for peer in peers():
        pl.semaphore_signal(barrier, inc=1, device_id=peer, device_id_type=MESH)
    sent = gather_part(r)
    sent = middle_part(r, sent)
    scatter_part(r, sent)
    HERE.clear()


def step(xq, xp, gain, wq, wk, wv, w_out, owner, place_in):
    tokens, width = xq.shape[0] + xp.shape[0], xq.shape[1]
    depth, heads = wq.shape
    cols = heads + wk.shape[1] + wv.shape[1]
    n = owner.shape[1]
    H = HEAD_DIM
    ANY, VM = pl.BlockSpec(memory_space=pl.ANY), pl.BlockSpec(memory_space=pltpu.VMEM)

    def dma(*shape):
        return pltpu.SemaphoreType.DMA(shape)

    ins = dict(xq=ANY, xp=ANY, gain=VM, wq=ANY, wk=ANY, wv=ANY, wout_hbm=ANY, owner=VM, place_in=VM)
    outs = dict(out=jax.ShapeDtypeStruct((cols, depth), f32), loss=jax.ShapeDtypeStruct((1, 1), f32))
    scratch = dict(
        W=pltpu.VMEM((32, depth, cols), bf16), held=pltpu.VMEM((depth, cols), bf16),
        X=pltpu.VMEM((tokens, width), bf16), acc=pltpu.VMEM((tokens, cols), f32),
        macc=pltpu.VMEM((8, 8, width), f32), rows=pltpu.VMEM((tokens, cols), bf16),
        scale=pltpu.VMEM((tokens, H), f32), means=pltpu.VMEM((8, width), f32),
        wout=pltpu.VMEM(w_out.shape, bf16), wts=pltpu.VMEM((tokens, H), f32),
        pooled=pltpu.VMEM((8, 8, heads), f32), ups=pltpu.VMEM((8, 8, heads), f32),
        terms=pltpu.VMEM((4, 16, width // 8), bf16), got=pltpu.VMEM((4, 16, width // 8), bf16),
        embeds=pltpu.VMEM((32, 8, width // 4), f32),
        qs=pltpu.VMEM((n, width // 4), f32), ps=pltpu.VMEM((n, width // 4), f32),
        gram=pltpu.VMEM((4, n + 8, n), f32), dl=pltpu.VMEM((3, n, n), f32), dlt=pltpu.VMEM((3, n, n), f32),
        raws=pltpu.VMEM((4, 16, width // 8), bf16), dgt=pltpu.VMEM((cols, tokens), bf16),
        part=pltpu.VMEM((16, 4, cols // 4, depth), bf16), both=pltpu.VMEM((16, 4, cols // 4, 2 * depth), bf16),
        sib=pltpu.VMEM((16, 4, cols // 4, depth), bf16), landed=pltpu.VMEM((60, cols // 4, depth), bf16),
        wsem=dma(3), xsem=dma(tokens // 128), osem=dma(),
        gsend=dma(40), grecv=dma(40), gsibs=dma(16), gsibr=dma(16),
        asend=dma(3), arecv=dma(3), bsend=dma(15), brecv=dma(15), msibs=dma(16), msibr=dma(16),
        csend=dma(3), crecv=dma(3), dsend=dma(3), drecv=dma(3),
        fsend=dma(40), frecv=dma(40), fsibs=dma(16), fsibr=dma(16))
    return pl.pallas_call(
        functools.partial(step_kernel, (*ins, *outs, *scratch)),
        out_shape=tuple(outs.values()),
        in_specs=list(ins.values()),
        out_specs=(VM, VM),
        scratch_shapes=list(scratch.values()),
        compiler_params=pltpu.CompilerParams(
            collective_id=0, has_side_effects=True, vmem_limit_bytes=VMEM_LIMIT),
        cost_estimate=pl.CostEstimate(flops=4 * tokens * width * cols, bytes_accessed=2 * tokens * width,
                                      transcendentals=0),
        name="contrast_step",
    )(xq, xp, gain.reshape(1, -1), wq, wk, wv, w_out, owner, place_in)


def body(
    query_states, passage_states, norm_gain, w_query, w_key, w_value, w_out, neg_owner, neg_slot
):
    owned, query_length, _ = query_states.shape
    passage_length = passage_states.shape[1]
    xq = query_states.reshape(owned * query_length, -1)
    xp = passage_states.reshape(owned * passage_length, -1)
    sums, loss = step(xq, xp, norm_gain, w_query, w_key, w_value, w_out, neg_owner.T, neg_slot.T)
    return (loss[0, 0], *finish(sums, norm_gain))


def solution(mesh):
    in_specs = (
        P("dp", None, None),
        P("dp", None, None),
        P(),
        P("dp", "tensor"),
        P("dp", "tensor"),
        P("dp", "tensor"),
        P("tensor", None),
        P(),
        P(),
    )
    out_specs = (P(), P("dp", "tensor"), P("dp", "tensor"), P("dp", "tensor"))
    return jax.shard_map(body, mesh=mesh, in_specs=in_specs, out_specs=out_specs, check_vma=False)
```
